256 devices in a mesh: gx: 8 (over z), gy: 16 (over y, x), gz: 2 (over core).
Axes of the slice: x: 4, y: 4, z: 8, core: 2. Of those that a mesh axis runs over, the one named last changes fastest.
Arguments:
- initial_state: float32 [4, 12, 256, 1024], P(None, 'gz', 'gy', 'gx'), may hold values from -6 to 6
- state_cotangent: float32 [4, 12, 256, 1024], P(None, 'gz', 'gy', 'gx'), may hold values from -6 to 6
- diffusion: float32 [12, 256, 1024], P('gz', 'gy', 'gx'), may hold values from 0.02 to 0.15
- weight_in: bfloat16 [40, 128], replicated, may hold values from -1 to 1
- weight_second: bfloat16 [128, 128], replicated, may hold values from -0.5 to 0.5
- weight_third: bfloat16 [128, 128], replicated, may hold values from -0.5 to 0.5
- weight_out: bfloat16 [128, 4], replicated, may hold values from -3 to 3
- biases_hidden: float32 [3, 128], replicated, may hold values from -3 to 3
- bias_out: float32 [4], replicated, may hold values from -4 to 4
Outputs:
- final_state: float32 [4, 12, 256, 1024], P(None, 'gz', 'gy', 'gx')
- initial_adjoint: float32 [4, 12, 256, 1024], P(None, 'gz', 'gy', 'gx')
- grad_weight_in: float32 [40, 128], replicated
- grad_weight_second: float32 [128, 128], replicated
- grad_weight_third: float32 [128, 128], replicated
- grad_weight_out: float32 [128, 4], replicated
- grad_biases: float32 [3, 128], replicated
- grad_bias_out: float32 [4], replicated
The draws below stay inside these ranges and needn't reach their ends.
All inputs are finite; a program needn't handle non-finite values.
Results may differ from the reference program's by a relative error of at most 0.009.
Values sent between devices are 32-bit elements; how exact they have to be, the bound alone decides.
A program may use at most 64 MiB of HBM per device.

```python
import math
import jax
import jax.numpy as jnp
from jax import lax

FIELDS = 4
FEAT = 40
HID = 128
NX = 1024
NY = 256
NZ = 12


def shard_levels(stream_key, extent, pieces, least, high):
    factor_of, own = 1.0, jax.random.fold_in(stream_key, 6)
    for dim, parts in pieces:
        draws = jnp.exp(jax.random.uniform(jax.random.fold_in(own, dim), (parts,), jnp.float32, least / len(pieces), high / len(pieces)))
        factor_of = factor_of * jnp.repeat(draws, extent[dim] // parts).reshape([-1 if axis == dim else 1 for axis in range(len(extent))])
    return factor_of


def scatter_about(stream_key, shape, deviation, reach, pieces=(), held_as=jnp.bfloat16):
    result = deviation * jax.random.normal(stream_key, shape, jnp.float32)
    if pieces:
        result = result * shard_levels(stream_key, shape, pieces, -0.22, 0.18)
    return jnp.clip(result, -reach, reach).astype(held_as)


def setup_inputs(seed: int = 0) -> dict:
    key_list = jax.random.split(jax.random.key(seed), 10)
    return {
        "initial_state": scatter_about(key_list[0], (FIELDS, NZ, NY, NX), 1.0, 6.0, ((1, 2), (2, 16), (3, 8)), jnp.float32),
        "state_cotangent": scatter_about(key_list[1], (FIELDS, NZ, NY, NX), 1.0, 6.0, ((1, 2), (2, 16), (3, 8)), jnp.float32),
        "diffusion": jnp.clip(jnp.exp(math.log(0.15) - 2.014903 * jax.random.uniform(key_list[2], (NZ, NY, NX), jnp.float32) ** shard_levels(key_list[2], (NZ, NY, NX), ((0, 2), (1, 16), (2, 8)), -0.2, 0.2)), 0.02, 0.15),
        "weight_in": scatter_about(key_list[3], (FEAT, HID), FEAT ** -0.5, 1.0),
        "weight_second": scatter_about(key_list[4], (HID, HID), HID ** -0.5, 0.5),
        "weight_third": scatter_about(key_list[5], (HID, HID), HID ** -0.5, 0.5),
        "weight_out": scatter_about(key_list[6], (HID, FIELDS), FIELDS ** -0.5, 3.0),
        "biases_hidden": scatter_about(key_list[7], (3, HID), 0.5, 3.0, (), jnp.float32),
        "bias_out": scatter_about(key_list[8], (FIELDS,), 1.0, 4.0, (), jnp.float32),
    }


time_step = 0.1
offsets = ((0, 0, 0), (0, 0, 1), (0, 0, -1), (0, 1, 0), (0, -1, 0), (1, 0, 0), (-1, 0, 0), (0, 1, 1), (1, 1, 0), (1, 0, 1))

def contract(former, latter):
    return lax.dot_general(former, latter, (((0,), (0,)), ((), ())), preferred_element_type=jnp.float32)

def outer_sum(former, latter):
    return lax.dot_general(former, latter, (((1,), (1,)), ((), ())), preferred_element_type=jnp.float32)

def apply_back(weight, latter):
    return lax.dot_general(weight, latter, (((1,), (0,)), ((), ())), preferred_element_type=jnp.float32)

def silu_slope(values):
    sigmoid_value = jax.nn.sigmoid(values)
    return sigmoid_value * (1.0 + values * (1.0 - sigmoid_value))

def hidden_layers(features, weights, biases_hidden):
    pre_one = contract(weights[0], features) + biases_hidden[0][:, None]
    act_one = jax.nn.silu(pre_one).astype(jnp.bfloat16)
    pre_two = contract(weights[1], act_one) + biases_hidden[1][:, None]
    act_two = jax.nn.silu(pre_two).astype(jnp.bfloat16)
    pre_three = contract(weights[2], act_two) + biases_hidden[2][:, None]
    act_three = jax.nn.silu(pre_three).astype(jnp.bfloat16)
    return ((pre_one, pre_two, pre_three), (act_one, act_two, act_three))

def closure(features, weights, biases_hidden, bias_out):
    layered = hidden_layers(features, weights, biases_hidden)
    return contract(weights[3], layered[1][2]) + bias_out[:, None]

def backward(features, adjoint, weights, biases_hidden, own_mask):
    preacts, activations = hidden_layers(features, weights, biases_hidden)
    grad_out = (time_step * adjoint).astype(jnp.bfloat16)
    back_three = (apply_back(weights[3], grad_out) * silu_slope(preacts[2])).astype(jnp.bfloat16)
    back_two = (apply_back(weights[2], back_three) * silu_slope(preacts[1])).astype(jnp.bfloat16)
    back_one = (apply_back(weights[1], back_two) * silu_slope(preacts[0])).astype(jnp.bfloat16)
    feature_grad = apply_back(weights[0], back_one)
    if own_mask is not None:
        grad_out = grad_out * own_mask[None, :]
        back_three = back_three * own_mask[None, :]
        back_two = back_two * own_mask[None, :]
        back_one = back_one * own_mask[None, :]
    bias_terms = jnp.stack([lax.optimization_barrier(jnp.sum(back_one.astype(jnp.float32), axis=1)), lax.optimization_barrier(jnp.sum(back_two.astype(jnp.float32), axis=1)), lax.optimization_barrier(jnp.sum(back_three.astype(jnp.float32), axis=1))])
    gradients = (outer_sum(features, back_one), outer_sum(activations[0], back_two), outer_sum(activations[1], back_three), outer_sum(activations[2], grad_out), bias_terms, lax.optimization_barrier(jnp.sum(grad_out.astype(jnp.float32), axis=1)))
    return (feature_grad, gradients)

def roll_to(grid_field, offset, direction):
    return jnp.roll(grid_field, (direction * offset[0], direction * offset[1], direction * offset[2]), axis=(1, 2, 3))

def laplace(grid_field):
    summed = -6.0 * grid_field
    for offset in offsets[1:7]:
        summed = summed + roll_to(grid_field, offset, -1)
    return summed

def features_of(state):
    stacked = jnp.stack([roll_to(state, offset, -1) for offset in offsets])
    flat = stacked.reshape(FEAT, NZ, NY * NX).astype(jnp.bfloat16)
    return jnp.moveaxis(flat, 1, 0)

def advance(state, diffusion, weights, biases_hidden, bias_out):
    features = features_of(state)
    closed = lax.map(lambda plane_cells: closure(plane_cells, weights, biases_hidden, bias_out), features)
    closed = jnp.moveaxis(closed, 0, 1).reshape((FIELDS, NZ, NY, NX))
    return state + diffusion * laplace(state) + time_step * closed

def retreat(state, adjoint, diffusion, weights, biases_hidden):
    features = features_of(state)
    adjoint_planes = jnp.moveaxis(adjoint.reshape(FIELDS, NZ, NY * NX), 1, 0)

    def one_plane(running, inputs):
        feature_grad, gradients = backward(inputs[0], inputs[1], weights, biases_hidden, None)
        return (jax.tree.map(jnp.add, running, gradients), feature_grad)
    start_grads = (jnp.zeros((FEAT, HID), jnp.float32), jnp.zeros((HID, HID), jnp.float32), jnp.zeros((HID, HID), jnp.float32), jnp.zeros((HID, FIELDS), jnp.float32), jnp.zeros((3, HID), jnp.float32), jnp.zeros((FIELDS,), jnp.float32))
    gradients, feature_grads = lax.scan(one_plane, start_grads, (features, adjoint_planes))
    feature_grads = jnp.moveaxis(feature_grads, 0, 1).reshape((len(offsets), FIELDS, NZ, NY, NX))
    updated = adjoint + laplace(diffusion * adjoint)
    for number in range(len(offsets)):
        updated = updated + roll_to(feature_grads[number], offsets[number], 1)
    return (updated, gradients)

def reference(initial_state, state_cotangent, diffusion, weight_in, weight_second, weight_third, weight_out, biases_hidden, bias_out):
    weights = (weight_in, weight_second, weight_third, weight_out)
    middle = advance(initial_state, diffusion, weights, biases_hidden, bias_out)
    final_state = advance(middle, diffusion, weights, biases_hidden, bias_out)
    adjoint_middle, later_grads = retreat(middle, state_cotangent, diffusion, weights, biases_hidden)
    initial_adjoint, earlier_grads = retreat(initial_state, adjoint_middle, diffusion, weights, biases_hidden)
    grad_scale = 1.0 / (time_step * math.sqrt(float(NX * NY * NZ)))
    totals = jax.tree.map(lambda former, latter: (former + latter) * grad_scale, later_grads, earlier_grads)
    return (final_state, initial_adjoint, totals[0], totals[1], totals[2], totals[3], totals[4], totals[5])
```

```python
import functools
import math

import jax
import jax.numpy as jnp
from jax import lax
from jax.experimental import pallas as pl
from jax.experimental.pallas import tpu as pltpu
from jax.sharding import PartitionSpec as P

bf16 = jnp.bfloat16
f32 = jnp.float32
MESH = pl.DeviceIdType.MESH

time_step = 0.1
FIELDS = 4
STENCIL = 10
PLANES = 6
ROWS = 64
LANES = 128
WIDE = 1024
HID = 128
SUMS = 384
SUBS = 2


def mm(former, latter):
    return lax.dot_general(former, latter, (((1,), (0,)), ((), ())), preferred_element_type=f32)


def mm_cells(former, latter):
    return lax.dot_general(former, latter, (((1,), (1,)), ((), ())), preferred_element_type=f32)


def lane_index(rows):
    return lax.broadcasted_iota(jnp.int32, (rows, LANES), 1)


def pack_lane(plane, lane, base, onto):
    index = lane_index(8)
    for part in range(8):
        moved = pltpu.roll(plane[8 * part : 8 * part + 8], (base + part - lane) % LANES, 1)
        onto = jnp.where(index == base + part, moved, onto)
    return onto


def unpack_lane(packed, base, lane):
    return jnp.concatenate(
        [pltpu.roll(packed, (lane - base - part) % LANES, 1) for part in range(8)], axis=0
    )


def rows_up(plane, first):
    return jnp.concatenate([first, plane[: ROWS - 4]], axis=0)


def rows_down(plane, last):
    return jnp.concatenate([plane[4:], last], axis=0)


def wide_of(plane):
    return jnp.concatenate([plane[8 * part : 8 * part + 8] for part in range(8)], axis=1)


def plane_of(wide):
    return jnp.concatenate(
        [wide[:, LANES * part : LANES * (part + 1)] for part in range(8)], axis=0
    )


def side_by_side(stacked):
    return jnp.concatenate([stacked[:HID], stacked[HID:]], axis=1)


def stacked_of(beside):
    half = beside.shape[1] // 2
    return jnp.concatenate([beside[:, :half], beside[:, half:]], axis=0)


def silu_parts(half):
    turned = jnp.tanh(half)
    raised = 1.0 + turned
    value = half * raised
    slope = raised * (1.0 - half * turned) + value
    return value.astype(bf16), slope.astype(bf16)


def kernel(
    sizes,
    scale,
    state_in,
    cot_in,
    diff_in,
    w_in,
    w_second,
    w_third,
    w_out,
    biases,
    bias_out,
    final_out,
    adjoint_out,
    g_in_out,
    g_second_out,
    g_third_out,
    g_readout_out,
    g_biases_out,
    g_bias_out_out,
    st,
    p_first,
    p_last,
    x_lo,
    x_hi,
    xy_hi,
    y_lo,
    y_hi,
    spread4,
    cot,
    adj_mid,
    staged,
    feats,
    acts,
    slopes,
    q,
    pa_last,
    pa_first,
    y_tiles,
    z_up,
    xa,
    xb,
    xya,
    ya,
    yb,
    l_one,
    l_two,
    l_three,
    l_out,
    v_out,
    v_three,
    v_two,
    v_one,
    square,
    g_one,
    g_two,
    g_three,
    g_four,
    sums,
    landed_a,
    landed_b,
    total,
    f_send,
    f_recv,
    f_send_z,
    f_recv_z,
    b_send,
    b_recv,
    b_send_z,
    b_recv_z,
    a_send,
    a_recv,
):
    nx, ny, nz = sizes
    gx, gy, gz = lax.axis_index("gx"), lax.axis_index("gy"), lax.axis_index("gz")
    right, left = lax.rem(gx + 1, nx), lax.rem(gx + nx - 1, nx)
    above, below = lax.rem(gy + 1, ny), lax.rem(gy + ny - 1, ny)
    other = 1 - gz
    group = nx * nz
    mine = gx * nz + gz
    share = SUMS // group

    def member(place):
        return (lax.div(place, nz), gy, lax.rem(place, nz))

    barrier = pltpu.get_barrier_semaphore()

    def greet(device):
        pl.semaphore_signal(barrier, inc=1, device_id=device, device_id_type=MESH)

    for device in ((right, above, gz), (left, below, gz), (gx, above, other), (gx, below, other)):
        greet(device)

    def greet_group(step, carry):
        greet(member(lax.rem(mine + step, group)))
        return carry

    lax.fori_loop(1, group, greet_group, 0)

    def greet_column(step, carry):
        greet((gx, lax.rem(gy + step, ny), gz))
        return carry

    lax.fori_loop(1, ny, greet_column, 0)

    def copy(source, target, send, recv, device):
        return pltpu.make_async_remote_copy(
            src_ref=source,
            dst_ref=target,
            send_sem=send,
            recv_sem=recv,
            device_id=device,
            device_id_type=MESH,
        )

    def field_copies(e, z):
        send, recv = f_send, f_recv
        return (
            copy(p_last.at[e, z], x_lo.at[e, z], send.at[e, 0, z], recv.at[e, 0, z], (right, gy, gz)),
            copy(p_first.at[e, z], x_hi.at[e, z], send.at[e, 1, z], recv.at[e, 1, z], (left, gy, gz)),
            copy(p_first.at[e, z], xy_hi.at[e, z], send.at[e, 2, z], recv.at[e, 2, z], (left, below, gz)),
            copy(st.at[e, z + 1, pl.ds(56, 8)], y_lo.at[e, z], send.at[e, 3, z], recv.at[e, 3, z], (gx, above, gz)),
            copy(st.at[e, z + 1, pl.ds(0, 8)], y_hi.at[e, z], send.at[e, 4, z], recv.at[e, 4, z], (gx, below, gz)),
        )

    def field_copies_low(e):
        send, recv = f_send_z, f_recv_z
        return (
            copy(p_first.at[e, 0], x_hi.at[e, PLANES], send.at[e, 0], recv.at[e, 0], (left, gy, other)),
            copy(st.at[e, 1, pl.ds(0, 8)], y_hi.at[e, PLANES], send.at[e, 1], recv.at[e, 1], (gx, below, other)),
            copy(st.at[e, 1], st.at[e, PLANES + 1], send.at[e, 2], recv.at[e, 2], (gx, gy, other)),
        )

    def field_copies_high(e):
        return (
            copy(st.at[e, PLANES], st.at[e, 0], f_send_z.at[e, 3], f_recv_z.at[e, 3], (gx, gy, other)),
        )

    def adjoint_copies(e, z):
        send, recv = b_send, b_recv
        return (
            copy(pa_last.at[e, z], xa.at[e, z + 1], send.at[e, 0, z], recv.at[e, 0, z], (right, gy, gz)),
            copy(pa_first.at[e, z], xb.at[e, z], send.at[e, 1, z], recv.at[e, 1, z], (left, gy, gz)),
            copy(pa_last.at[e, z], xya.at[e, z], send.at[e, 2, z], recv.at[e, 2, z], (right, above, gz)),
            copy(y_tiles.at[e, z], ya.at[e, z + 1], send.at[e, 3, z], recv.at[e, 3, z], (gx, above, gz)),
            copy(q.at[e, z + 1, 4, pl.ds(0, 8)], yb.at[e, z], send.at[e, 4, z], recv.at[e, 4, z], (gx, below, gz)),
        )

    def adjoint_copies_high(e):
        send, recv = b_send_z, b_recv_z
        return (
            copy(pa_last.at[e, PLANES - 1], xa.at[e, 0], send.at[e, 0], recv.at[e, 0], (right, gy, other)),
            copy(y_tiles.at[e, PLANES - 1], ya.at[e, 0], send.at[e, 1], recv.at[e, 1], (gx, above, other)),
            copy(z_up.at[e], q.at[e, 0, 5], send.at[e, 2], recv.at[e, 2], (gx, gy, other)),
        )

    def adjoint_copies_low(e):
        return (
            copy(q.at[e, 1, 6], q.at[e, PLANES + 1, 6], b_send_z.at[e, 3], b_recv_z.at[e, 3], (gx, gy, other)),
        )

    def start(copies):
        for each in copies:
            each.start()

    def arrive(copies):
        for each in copies:
            each.wait_recv()

    def sent(copies):
        for each in copies:
            each.wait_send()

    def send_fields(e, z):
        plane = st[e, z + 1]
        empty = jnp.zeros((8, LANES), f32)
        p_first[e, z] = pack_lane(plane, 0, 0, empty)
        p_last[e, z] = pack_lane(plane, LANES - 1, 0, empty)
        start(field_copies(e, z))

        @pl.when(z == 0)
        def _():
            start(field_copies_low(e))

        @pl.when(z == PLANES - 1)
        def _():
            start(field_copies_high(e))

    def place(step):
        odd = lax.rem(step, 2)
        half = lax.div(step, 2)
        return half + odd * (PLANES - 1 - 2 * half)

    def lay_out(z, carry):
        for k in range(FIELDS):
            st[0, z + 1, pl.ds(k, 16, stride=FIELDS), :] = state_in[k, z]
        return carry

    lax.fori_loop(0, PLANES, lay_out, 0)
    pl.semaphore_wait(barrier, 4 + (group - 1) + (ny - 1))

    def first_sends(step, carry):
        send_fields(0, place(step))
        return carry

    lax.fori_loop(0, PLANES, first_sends, 0)

    def lay_out_rest(z, carry):
        for k in range(FIELDS):
            cot[z, pl.ds(k, 16, stride=FIELDS), :] = cot_in[k, z]
            spread4[z, pl.ds(k, 16, stride=FIELDS), :] = diff_in[z]
        return carry

    lax.fori_loop(0, PLANES, lay_out_rest, 0)
    for e in range(2):
        for j in (8, 9):
            q[e, 0, j] = jnp.zeros((ROWS, LANES), f32)

    zero4 = jnp.zeros((4, LANES), f32)
    first = w_in[...].astype(f32)
    parts = [first[4 * j : 4 * j + 4] for j in range(STENCIL)]
    even = jnp.concatenate([piece for part in parts for piece in (part, zero4)], axis=0)
    odd = jnp.concatenate([piece for part in parts for piece in (zero4, part)], axis=0)
    v_one[...] = jnp.concatenate([even, odd], axis=1).astype(bf16)
    bias_high = biases[...].astype(bf16).astype(f32)
    bias_low = biases[...] - bias_high

    def bias_rows(layer):
        return jnp.concatenate(
            [
                0.5 * bias_high[layer : layer + 1],
                0.5 * bias_low[layer : layer + 1],
                jnp.zeros((14, HID), f32),
            ],
            axis=0,
        )

    def turned_first(half):
        tall = jnp.concatenate([0.5 * half, bias_rows(0), jnp.zeros((32, HID), f32)], axis=0)
        return tall.T[:, :96]

    l_one[...] = jnp.concatenate([turned_first(even), turned_first(odd)], axis=0).astype(bf16)
    for layer, source, ahead, back in ((1, w_second, l_two, v_two), (2, w_third, l_three, v_three)):
        matrix = 0.5 * source[...].astype(f32)
        back[...] = matrix.astype(bf16)
        tall = jnp.concatenate([bias_rows(layer), jnp.zeros((112, HID), f32)], axis=0)
        ahead[...] = jnp.concatenate([matrix.T, tall.T[:, :16]], axis=1).astype(bf16)
    square[...] = jnp.zeros((HID, HID), f32)
    square[:, 0:FIELDS] = w_out[...].astype(f32)
    readout = square[...]
    turned_out = readout.T[0:4]
    zero8 = jnp.zeros((8, LANES), f32)
    l_out[...] = jnp.concatenate(
        [
            jnp.concatenate([turned_out, zero4, zero8], axis=0),
            jnp.concatenate([zero4, turned_out, zero8], axis=0),
        ],
        axis=1,
    ).astype(bf16)
    v_out[...] = jnp.concatenate(
        [0.5 * readout[:, :16], 0.5 * pltpu.roll(readout, FIELDS, 1)[:, :16]], axis=0
    ).astype(bf16)
    field_row = lax.rem(lax.broadcasted_iota(jnp.int32, (8, LANES), 0), FIELDS)
    bias_tile = jnp.zeros((8, LANES), f32)
    for k in range(FIELDS):
        bias_tile = jnp.where(field_row == k, bias_out[k], bias_tile)
    bias_plane = jnp.concatenate([bias_tile] * 8, axis=0)
    for each in (g_one, g_two, g_three, g_four):
        each[...] = jnp.zeros(each.shape, f32)

    lane = lane_index(ROWS)
    lane8 = lane_index(8)
    sub_width = WIDE // SUBS
    ones_rows = lax.broadcasted_iota(jnp.int32, (16, WIDE), 0)
    ones_wide = jnp.where(ones_rows < 2, 1.0, 0.0).astype(bf16)
    ones_cells = jnp.concatenate([ones_wide[:, :sub_width]] * 2, axis=1)

    def to_right(plane, e, z):
        return jnp.where(
            lane == LANES - 1, unpack_lane(x_hi[e, z], 0, LANES - 1), pltpu.roll(plane, LANES - 1, 1)
        )

    def stencil(e, z):
        here, ahead, behind = st[e, z + 1], st[e, z + 2], st[e, z]
        beyond = y_hi[e, z]
        at_right = to_right(here, e, z)
        at_left = jnp.where(lane == 0, unpack_lane(x_lo[e, z], 0, 0), pltpu.roll(here, 1, 1))
        corner = jnp.where(
            lane8 == LANES - 1,
            pltpu.roll(xy_hi[e, z], LANES - 1, 1),
            pltpu.roll(beyond, LANES - 1, 1),
        )
        return (
            here,
            at_right,
            at_left,
            rows_down(here, beyond[0:4]),
            rows_up(here, y_lo[e, z][4:8]),
            ahead,
            behind,
            rows_down(at_right, corner[0:4]),
            rows_down(ahead, y_hi[e, z + 1][0:4]),
            to_right(ahead, e, z + 1),
        )

    def arrange(points):
        rows = jnp.concatenate([wide_of(point) for point in points], axis=0)
        return jnp.concatenate([rows.astype(bf16), ones_wide], axis=0)

    def laplace(points):
        total_of = -6.0 * points[0]
        for point in points[1:7]:
            total_of = total_of + point
        return total_of

    def layers(features):
        value, slope = silu_parts(side_by_side(mm(l_one[...], features)))
        values, doubled = [value], [slope]
        for matrix in (l_two, l_three):
            cells = jnp.concatenate([value, ones_cells], axis=0)
            value, slope = silu_parts(mm(matrix[...], cells))
            values.append(value)
            doubled.append(slope)
        return values, doubled

    def readout_of(value):
        return mm(l_out[...], stacked_of(value))[0:8]

    def times(product, slope):
        return (product * slope.astype(f32)).astype(bf16)

    def grad_rows(adjoint):
        scaled = wide_of(time_step * adjoint)
        return jnp.concatenate([scaled, jnp.zeros((8, WIDE), f32)], axis=0).astype(bf16)

    def backward(features, values, doubled, grad_out):
        back_three = times(side_by_side(mm(v_out[...], grad_out)), doubled[2])
        back_two = times(mm(v_three[...], back_three), doubled[1])
        back_one = stacked_of(times(mm(v_two[...], back_two), doubled[0]))
        ones_here = ones_cells[:, :sub_width]
        g_four[:, 0:16] += mm_cells(
            jnp.concatenate([stacked_of(values[2]), ones_here], axis=0), grad_out
        )
        g_three[...] += mm_cells(jnp.concatenate([values[1], ones_cells], axis=0), back_three)
        g_two[...] += mm_cells(jnp.concatenate([values[0], ones_cells], axis=0), back_two)
        g_one[...] += mm_cells(features, back_one)
        return mm(v_one[...], back_one)

    def send_adjoint(e, z, wide, adjoint):
        spread = spread4[z] * adjoint
        for j in range(STENCIL):
            part = plane_of(wide[8 * j : 8 * j + 8])
            if j == 0:
                part = part - 6.0 * spread
            elif j < 7:
                part = part + spread
            q[e, z + 1, j] = part
        empty = jnp.zeros((8, LANES), f32)
        across = pack_lane(q[e, z + 1, 1], LANES - 1, 0, empty)
        across = pack_lane(q[e, z + 1, 9], LANES - 1, 8, across)
        pa_last[e, z] = pack_lane(q[e, z + 1, 7], LANES - 1, 16, across)
        pa_first[e, z] = pack_lane(q[e, z + 1, 2], 0, 0, empty)
        slanted = q[e, z + 1, 7, 56:64]
        slanted = jnp.where(lane8 == 0, 0.0, pltpu.roll(slanted, 1, 1))
        y_tiles[e, z, 0:8] = q[e, z + 1, 3, 56:64] + slanted
        y_tiles[e, z, 8:16] = q[e, z + 1, 8, 56:64]
        start(adjoint_copies(e, z))

        @pl.when(z == 0)
        def _():
            start(adjoint_copies_low(e))

        @pl.when(z == PLANES - 1)
        def _():
            moved = jnp.where(lane == 0, 0.0, pltpu.roll(q[e, PLANES, 9], 1, 1))
            z_up[e] = q[e, PLANES, 5] + moved + rows_up(q[e, PLANES, 8], zero4)
            start(adjoint_copies_high(e))

    def gather(e, z, adjoint):
        here = z + 1
        result = adjoint + q[e, here, 0] + q[e, z, 5] + q[e, z + 2, 6]
        from_left = q[e, here, 1] + q[e, z, 9] + rows_up(q[e, here, 7], zero4)
        packed = xa[e, here]
        direct = unpack_lane(packed + pltpu.roll(xa[e, z], LANES - 8, 1), 0, 0)
        corner = pltpu.roll(xya[e, z], LANES - 23, 1)[4:8]
        edge = direct + rows_up(unpack_lane(packed, 16, 0), corner)
        result = result + jnp.where(lane == 0, edge, pltpu.roll(from_left, 1, 1))
        result = result + jnp.where(
            lane == LANES - 1,
            unpack_lane(xb[e, z], 0, LANES - 1),
            pltpu.roll(q[e, here, 2], LANES - 1, 1),
        )
        rows_in = ya[e, here, 0:8] + ya[e, z, 8:16]
        result = result + rows_up(q[e, here, 3] + q[e, z, 8], rows_in[4:8])
        return result + rows_down(q[e, here, 4], yb[e, z][0:4])

    def await_fields(e, step):
        @pl.when(step == 0)
        def _():
            arrive(field_copies(e, 0))
            arrive(field_copies(e, 1))
            arrive(field_copies_high(e))

        @pl.when(step == 1)
        def _():
            arrive(field_copies(e, 5))
            arrive(field_copies_low(e))

        @pl.when(step == 2)
        def _():
            arrive(field_copies(e, 2))

        @pl.when(step == 3)
        def _():
            arrive(field_copies(e, 4))

        @pl.when(step == 4)
        def _():
            arrive(field_copies(e, 3))

    def await_adjoint(e, step):
        @pl.when(step == 0)
        def _():
            arrive(adjoint_copies(e, 0))
            arrive(adjoint_copies_high(e))

        @pl.when(step == 1)
        def _():
            arrive(adjoint_copies(e, 5))
            arrive(adjoint_copies(e, 4))
            arrive(adjoint_copies_low(e))

        @pl.when(step == 2)
        def _():
            arrive(adjoint_copies(e, 1))

        @pl.when(step == 3)
        def _():
            arrive(adjoint_copies(e, 3))

        @pl.when(step == 4)
        def _():
            arrive(adjoint_copies(e, 2))

    def piece(sub):
        return slice(sub * sub_width, (sub + 1) * sub_width)

    def beside(sub):
        return slice(2 * sub * sub_width, 2 * (sub + 1) * sub_width)

    def stepped(points, z, wide):
        closed = plane_of(wide) + bias_plane
        return points[0] + spread4[z] * laplace(points) + time_step * closed

    def put(target, z, plane):
        staged[...] = plane
        for k in range(FIELDS):
            target[k, z] = staged[pl.ds(k, 16, stride=FIELDS), :]

    def first_step(step, carry):
        z = place(step)
        await_fields(0, step)
        points = stencil(0, z)
        features = arrange(points)
        feats[z] = features
        outs = []
        for sub in range(SUBS):
            values, doubled = layers(features[:, piece(sub)])
            for layer in range(3):
                acts[layer, z, :, beside(sub)] = values[layer]
                slopes[layer, z, :, beside(sub)] = doubled[layer]
            outs.append(readout_of(values[2]))
        st[1, z + 1] = stepped(points, z, jnp.concatenate(outs, axis=1))
        send_fields(1, z)
        return carry

    lax.fori_loop(0, PLANES, first_step, 0)

    def second_step(step, carry):
        z = place(step)
        await_fields(1, step)
        points = stencil(1, z)
        features = arrange(points)
        adjoint = cot[z]
        grad_out = grad_rows(adjoint)
        outs, wides = [], []
        for sub in range(SUBS):
            values, doubled = layers(features[:, piece(sub)])
            outs.append(readout_of(values[2]))
            wides.append(
                backward(features[:, piece(sub)], values, doubled, grad_out[:, piece(sub)])
            )
        put(final_out, z, stepped(points, z, jnp.concatenate(outs, axis=1)))
        send_adjoint(0, z, jnp.concatenate(wides, axis=1), adjoint)
        return carry

    lax.fori_loop(0, PLANES, second_step, 0)

    def first_back(step, carry):
        z = place(step)
        await_adjoint(0, step)
        adjoint = gather(0, z, cot[z])
        adj_mid[z] = adjoint
        grad_out = grad_rows(adjoint)
        wides = []
        for sub in range(SUBS):
            values = [acts[layer, z, :, beside(sub)] for layer in range(3)]
            doubled = [slopes[layer, z, :, beside(sub)] for layer in range(3)]
            wides.append(
                backward(feats[z, :, piece(sub)], values, doubled, grad_out[:, piece(sub)])
            )
        send_adjoint(1, z, jnp.concatenate(wides, axis=1), adjoint)
        return carry

    lax.fori_loop(0, PLANES, first_back, 0)

    one = g_one[...]
    merged = one[:, :HID] + jnp.concatenate([one[4:, HID:], one[:4, HID:]], axis=0)
    first_rows = jnp.concatenate([merged[8 * j : 8 * j + 4] for j in range(STENCIL)], axis=0)
    four = g_four[...]
    shifted = four[:HID] + pltpu.roll(four[HID : 2 * HID], LANES - FIELDS, 1)
    last = four[2 * HID : 2 * HID + 8]
    last = last + pltpu.roll(last, LANES - FIELDS, 1)
    rest = jnp.concatenate(
        [
            one[80:81, :HID] + one[80:81, HID:],
            g_two[HID : HID + 1],
            g_three[HID : HID + 1],
            last[0:1],
            shifted.T[0:4],
        ],
        axis=0,
    )
    everything = jnp.concatenate(
        [
            g_two[0:HID],
            g_three[0:HID],
            first_rows,
            rest,
            jnp.zeros((SUMS - 304, LANES), f32),
        ],
        axis=0,
    )
    sums[...] = everything.reshape(group, share, LANES)

    def scatter(step):
        target = lax.rem(mine + step, group)
        return copy(sums.at[target], landed_a.at[step], a_send.at[0, step], a_recv.at[0, step], member(target))

    def across(step):
        target = lax.rem(gy + step, ny)
        return copy(landed_b.at[gy], landed_b.at[gy], a_send.at[1, step], a_recv.at[1, gy], (gx, target, gz))

    def across_in(step):
        source = lax.rem(gy + ny - step, ny)
        return copy(landed_b.at[source], landed_b.at[source], a_send.at[1, step], a_recv.at[1, source], (gx, source, gz))

    def spread_out(step):
        target = lax.rem(mine + step, group)
        return copy(total.at[mine], total.at[mine], a_send.at[2, step], a_recv.at[2, mine], member(target))

    def spread_in(step):
        source = lax.rem(mine + group - step, group)
        return copy(total.at[source], total.at[source], a_send.at[2, step], a_recv.at[2, source], member(source))

    def each(count, act):
        def body(step, carry):
            act(step)
            return carry

        lax.fori_loop(1, count, body, 0)

    each(group, lambda step: scatter(step).start())

    def last_gather(step, carry):
        z = place(step)
        await_adjoint(1, step)
        put(adjoint_out, z, gather(1, z, adj_mid[z]))
        return carry

    each(group, lambda step: scatter(step).wait_recv())
    held = sums[mine]
    for step in range(1, group):
        held = held + landed_a[step]
    landed_b[gy] = held
    each(ny, lambda step: across(step).start())

    lax.fori_loop(0, PLANES, last_gather, 0)

    each(ny, lambda step: across_in(step).wait_recv())
    held = landed_b[0]
    for step in range(1, ny):
        held = held + landed_b[step]
    total[mine] = held * scale
    each(group, lambda step: spread_out(step).start())

    def finish_sends(z, carry):
        for e in range(2):
            sent(field_copies(e, z))
            sent(adjoint_copies(e, z))
        return carry

    lax.fori_loop(0, PLANES, finish_sends, 0)
    for e in range(2):
        sent(field_copies_low(e))
        sent(field_copies_high(e))
        sent(adjoint_copies_low(e))
        sent(adjoint_copies_high(e))
    each(group, lambda step: scatter(step).wait_send())
    each(ny, lambda step: across(step).wait_send())
    each(group, lambda step: spread_in(step).wait_recv())

    whole = total[...].reshape(SUMS, LANES)
    g_second_out[...] = whole[0:HID]
    g_third_out[...] = whole[HID : 2 * HID]
    g_in_out[...] = whole[2 * HID : 2 * HID + 40]
    tail = whole[296:304]
    g_biases_out[...] = tail[0:3]
    tall = jnp.concatenate([tail[4:8], jnp.zeros((HID - 4, LANES), f32)], axis=0)
    g_readout_out[...] = tall.T[:, 0:FIELDS]
    g_bias_out_out[...] = tail[3:4, 0:FIELDS]
    each(group, lambda step: spread_out(step).wait_send())


def solution(mesh):
    sizes = (mesh.shape["gx"], mesh.shape["gy"], mesh.shape["gz"])
    nx, ny, nz = sizes
    group = nx * nz
    share = SUMS // group
    cells = PLANES * 16 * LANES * nx * ny * nz
    scale = 1.0 / (time_step * math.sqrt(float(cells)))
    vmem = pl.BlockSpec(memory_space=pltpu.VMEM)
    block = jax.ShapeDtypeStruct((FIELDS, PLANES, 16, LANES), f32)
    tile = (8, LANES)
    dma = pltpu.SemaphoreType.DMA

    def buffer(*shape):
        return pltpu.VMEM(shape, f32)

    def packed(*shape):
        return pltpu.VMEM(shape, bf16)

    scratch = [
        buffer(2, PLANES + 2, ROWS, LANES),
        buffer(2, PLANES, *tile),
        buffer(2, PLANES, *tile),
        buffer(2, PLANES, *tile),
        buffer(2, PLANES + 1, *tile),
        buffer(2, PLANES, *tile),
        buffer(2, PLANES, *tile),
        buffer(2, PLANES + 1, *tile),
        buffer(PLANES, ROWS, LANES),
        buffer(PLANES, ROWS, LANES),
        buffer(PLANES, ROWS, LANES),
        buffer(ROWS, LANES),
        packed(PLANES, 96, WIDE),
        packed(3, PLANES, HID, 2 * WIDE),
        packed(3, PLANES, HID, 2 * WIDE),
        buffer(2, PLANES + 2, STENCIL, ROWS, LANES),
        buffer(2, PLANES, *tile),
        buffer(2, PLANES, *tile),
        buffer(2, PLANES, 16, LANES),
        buffer(2, ROWS, LANES),
        buffer(2, PLANES + 1, *tile),
        buffer(2, PLANES, *tile),
        buffer(2, PLANES, *tile),
        buffer(2, PLANES + 1, 16, LANES),
        buffer(2, PLANES, *tile),
        packed(2 * HID, 96),
        packed(HID, 144),
        packed(HID, 144),
        packed(16, 2 * HID),
        packed(2 * HID, 16),
        packed(HID, HID),
        packed(HID, HID),
        packed(80, 2 * HID),
        buffer(HID, HID),
        buffer(96, 2 * HID),
        buffer(144, HID),
        buffer(144, HID),
        buffer(2 * HID + 16, LANES),
        buffer(group, share, LANES),
        buffer(group, share, LANES),
        buffer(ny, share, LANES),
        buffer(group, share, LANES),
        dma((2, 5, PLANES)),
        dma((2, 5, PLANES)),
        dma((2, 4)),
        dma((2, 4)),
        dma((2, 5, PLANES)),
        dma((2, 5, PLANES)),
        dma((2, 4)),
        dma((2, 4)),
        dma((3, max(group, ny))),
        dma((3, max(group, ny))),
    ]

    def on_device(*operands):
        outs = pl.pallas_call(
            functools.partial(kernel, sizes, scale),
            out_shape=(
                block,
                block,
                jax.ShapeDtypeStruct((40, HID), f32),
                jax.ShapeDtypeStruct((HID, HID), f32),
                jax.ShapeDtypeStruct((HID, HID), f32),
                jax.ShapeDtypeStruct((HID, FIELDS), f32),
                jax.ShapeDtypeStruct((3, HID), f32),
                jax.ShapeDtypeStruct((1, FIELDS), f32),
            ),
            in_specs=[vmem] * 8 + [pl.BlockSpec(memory_space=pltpu.SMEM)],
            out_specs=[vmem] * 8,
            scratch_shapes=scratch,
            compiler_params=pltpu.CompilerParams(
                collective_id=0, has_side_effects=True, vmem_limit_bytes=60 * 2**20
            ),
            name="two_steps_and_adjoint",
        )(*operands)
        return outs[:7] + (outs[7].reshape(FIELDS),)

    fields = P(None, "gz", "gy", "gx")
    placed = (fields, fields, P("gz", "gy", "gx")) + (P(),) * 6
    return jax.shard_map(
        on_device,
        mesh=mesh,
        in_specs=placed,
        out_specs=(fields, fields) + (P(),) * 6,
        check_vma=False,
    )
```

```python
import functools
import math

import jax
import jax.numpy as jnp
from jax import lax
from jax.experimental import pallas as pl
from jax.experimental.pallas import tpu as pltpu
from jax.sharding import PartitionSpec as P

bf16 = jnp.bfloat16
f32 = jnp.float32
MESH = pl.DeviceIdType.MESH

time_step = 0.1
FIELDS = 4
STENCIL = 10
PLANES = 6
ROWS = 64
LANES = 128
WIDE = 1024
HID = 128
SUMS = 384
SUBS = 2


def mm(former, latter):
    return lax.dot_general(former, latter, (((1,), (0,)), ((), ())), preferred_element_type=f32)


def mm_cells(former, latter):
    return lax.dot_general(former, latter, (((1,), (1,)), ((), ())), preferred_element_type=f32)


def lane_index(rows):
    return lax.broadcasted_iota(jnp.int32, (rows, LANES), 1)


def pack_lane(plane, lane, base, onto):
    index = lane_index(8)
    for part in range(8):
        moved = pltpu.roll(plane[8 * part : 8 * part + 8], (base + part - lane) % LANES, 1)
        onto = jnp.where(index == base + part, moved, onto)
    return onto


def unpack_lane(packed, base, lane):
    return jnp.concatenate(
        [pltpu.roll(packed, (lane - base - part) % LANES, 1) for part in range(8)], axis=0
    )


def rows_up(plane, first):
    return jnp.concatenate([first, plane[: ROWS - 4]], axis=0)


def rows_down(plane, last):
    return jnp.concatenate([plane[4:], last], axis=0)


def wide_of(plane):
    return jnp.concatenate([plane[8 * part : 8 * part + 8] for part in range(8)], axis=1)


def plane_of(wide):
    return jnp.concatenate(
        [wide[:, LANES * part : LANES * (part + 1)] for part in range(8)], axis=0
    )


def side_by_side(stacked):
    return jnp.concatenate([stacked[:HID], stacked[HID:]], axis=1)


def stacked_of(beside):
    half = beside.shape[1] // 2
    return jnp.concatenate([beside[:, :half], beside[:, half:]], axis=0)


def silu_parts(half):
    half = half.astype(bf16)
    turned = jnp.tanh(half)
    raised = 1 + turned
    value = half * raised
    slope = raised * (1 - half * turned) + value
    return value, slope


def kernel(
    sizes,
    scale,
    state_in,
    cot_in,
    diff_in,
    w_in,
    w_second,
    w_third,
    w_out,
    biases,
    bias_out,
    final_out,
    adjoint_out,
    g_in_out,
    g_second_out,
    g_third_out,
    g_readout_out,
    g_biases_out,
    g_bias_out_out,
    state_here,
    cot_here,
    diff_here,
    w_in_here,
    w_second_here,
    w_third_here,
    w_out_here,
    biases_here,
    final_here,
    adjoint_here,
    st,
    p_first,
    p_last,
    x_lo,
    x_hi,
    xy_hi,
    y_lo,
    y_hi,
    spread4,
    cot,
    adj_mid,
    staged,
    feats,
    acts,
    slopes,
    backs,
    q,
    pa_last,
    pa_first,
    y_tiles,
    z_up,
    xa,
    xb,
    xya,
    ya,
    yb,
    l_one,
    l_two,
    l_three,
    l_out,
    v_out,
    v_three,
    v_two,
    v_one,
    g_one,
    g_two,
    g_three,
    g_four,
    sums,
    landed_pair,
    landed_a,
    landed_b,
    total,
    f_send,
    f_recv,
    f_send_z,
    f_recv_z,
    b_send,
    b_recv,
    b_send_z,
    b_recv_z,
    a_send,
    a_recv,
    here_sem,
):
    nx, ny, nz = sizes
    gx, gy, gz = lax.axis_index("gx"), lax.axis_index("gy"), lax.axis_index("gz")
    right, left = lax.rem(gx + 1, nx), lax.rem(gx + nx - 1, nx)
    above, below = lax.rem(gy + 1, ny), lax.rem(gy + ny - 1, ny)
    other = 1 - gz
    share = SUMS // nz // nx

    barrier = pltpu.get_barrier_semaphore()

    def greet(device):
        pl.semaphore_signal(barrier, inc=1, device_id=device, device_id_type=MESH)

    for device in (
        (right, above, gz),
        (left, below, gz),
        (gx, above, other),
        (gx, below, other),
        (right, gy, other),
        (left, gy, other),
        (gx, gy, other),
    ):
        greet(device)

    def greet_row(step, carry):
        greet((lax.rem(gx + step, nx), gy, gz))
        return carry

    lax.fori_loop(1, nx, greet_row, 0)

    def greet_column(step, carry):
        greet((gx, lax.rem(gy + step, ny), gz))
        return carry

    lax.fori_loop(1, ny, greet_column, 0)

    fetches = [
        pltpu.make_async_copy(source, target, here_sem.at[number])
        for number, (source, target) in enumerate(
            (
                (state_in, state_here),
                (cot_in, cot_here),
                (diff_in, diff_here),
                (w_in, w_in_here),
                (w_second, w_second_here),
                (w_third, w_third_here),
                (w_out, w_out_here),
                (biases, biases_here),
            )
        )
    ]
    for fetch in fetches:
        fetch.start()

    def copy(source, target, send, recv, device):
        return pltpu.make_async_remote_copy(
            src_ref=source,
            dst_ref=target,
            send_sem=send,
            recv_sem=recv,
            device_id=device,
            device_id_type=MESH,
        )

    def field_copies(e, z):
        send, recv = f_send, f_recv
        return (
            copy(p_last.at[e, z], x_lo.at[e, z], send.at[e, 0, z], recv.at[e, 0, z], (right, gy, gz)),
            copy(p_first.at[e, z], x_hi.at[e, z], send.at[e, 1, z], recv.at[e, 1, z], (left, gy, gz)),
            copy(p_first.at[e, z], xy_hi.at[e, z], send.at[e, 2, z], recv.at[e, 2, z], (left, below, gz)),
            copy(st.at[e, z + 1, pl.ds(56, 8)], y_lo.at[e, z], send.at[e, 3, z], recv.at[e, 3, z], (gx, above, gz)),
            copy(st.at[e, z + 1, pl.ds(0, 8)], y_hi.at[e, z], send.at[e, 4, z], recv.at[e, 4, z], (gx, below, gz)),
        )

    def field_copies_low(e):
        send, recv = f_send_z, f_recv_z
        return (
            copy(p_first.at[e, 0], x_hi.at[e, PLANES], send.at[e, 0], recv.at[e, 0], (left, gy, other)),
            copy(st.at[e, 1, pl.ds(0, 8)], y_hi.at[e, PLANES], send.at[e, 1], recv.at[e, 1], (gx, below, other)),
            copy(st.at[e, 1], st.at[e, PLANES + 1], send.at[e, 2], recv.at[e, 2], (gx, gy, other)),
        )

    def field_copies_high(e):
        return (
            copy(st.at[e, PLANES], st.at[e, 0], f_send_z.at[e, 3], f_recv_z.at[e, 3], (gx, gy, other)),
        )

    def adjoint_copies(e, z):
        send, recv = b_send, b_recv
        return (
            copy(pa_last.at[e, z], xa.at[e, z + 1], send.at[e, 0, z], recv.at[e, 0, z], (right, gy, gz)),
            copy(pa_first.at[e, z], xb.at[e, z], send.at[e, 1, z], recv.at[e, 1, z], (left, gy, gz)),
            copy(pa_last.at[e, z], xya.at[e, z], send.at[e, 2, z], recv.at[e, 2, z], (right, above, gz)),
            copy(y_tiles.at[e, z], ya.at[e, z + 1], send.at[e, 3, z], recv.at[e, 3, z], (gx, above, gz)),
            copy(q.at[e, z + 1, 4, pl.ds(0, 8)], yb.at[e, z], send.at[e, 4, z], recv.at[e, 4, z], (gx, below, gz)),
        )

    def adjoint_copies_high(e):
        send, recv = b_send_z, b_recv_z
        return (
            copy(pa_last.at[e, PLANES - 1], xa.at[e, 0], send.at[e, 0], recv.at[e, 0], (right, gy, other)),
            copy(y_tiles.at[e, PLANES - 1], ya.at[e, 0], send.at[e, 1], recv.at[e, 1], (gx, above, other)),
            copy(z_up.at[e], q.at[e, 0, 5], send.at[e, 2], recv.at[e, 2], (gx, gy, other)),
        )

    def adjoint_copies_low(e):
        return (
            copy(q.at[e, 1, 6], q.at[e, PLANES + 1, 6], b_send_z.at[e, 3], b_recv_z.at[e, 3], (gx, gy, other)),
        )

    def start(copies):
        for each in copies:
            each.start()

    def arrive(copies):
        for each in copies:
            each.wait_recv()

    def sent(copies):
        for each in copies:
            each.wait_send()

    def send_fields(e, z):
        plane = st[e, z + 1]
        empty = jnp.zeros((8, LANES), f32)
        p_first[e, z] = pack_lane(plane, 0, 0, empty)
        p_last[e, z] = pack_lane(plane, LANES - 1, 0, empty)
        start(field_copies(e, z))

        @pl.when(z == 0)
        def _():
            start(field_copies_low(e))

        @pl.when(z == PLANES - 1)
        def _():
            start(field_copies_high(e))

    def place(step):
        odd = lax.rem(step, 2)
        half = lax.div(step, 2)
        return half + odd * (PLANES - 1 - 2 * half)

    def lay_out(z, carry):
        for k in range(FIELDS):
            st[0, z + 1, pl.ds(k, 16, stride=FIELDS), :] = state_here[k, z]
        return carry

    fetches[0].wait()
    lax.fori_loop(0, PLANES, lay_out, 0)
    pl.semaphore_wait(barrier, 7 + (nx - 1) + (ny - 1))

    def first_sends(step, carry):
        send_fields(0, place(step))
        return carry

    lax.fori_loop(0, PLANES, first_sends, 0)

    for fetch in fetches[1:]:
        fetch.wait()

    def lay_out_rest(z, carry):
        for k in range(FIELDS):
            cot[z, pl.ds(k, 16, stride=FIELDS), :] = cot_here[k, z]
            spread4[z, pl.ds(k, 16, stride=FIELDS), :] = diff_here[z]
        return carry

    lax.fori_loop(0, PLANES, lay_out_rest, 0)
    for e in range(2):
        for j in (8, 9):
            q[e, 0, j] = jnp.zeros((ROWS, LANES), f32)

    zero4 = jnp.zeros((4, LANES), f32)
    first = w_in_here[...].astype(f32)
    parts = [first[4 * j : 4 * j + 4] for j in range(STENCIL)]
    even = jnp.concatenate([piece for part in parts for piece in (part, zero4)], axis=0)
    odd = jnp.concatenate([piece for part in parts for piece in (zero4, part)], axis=0)
    v_one[...] = jnp.concatenate([even, odd], axis=1).astype(bf16)
    bias_high = biases_here[...].astype(bf16).astype(f32)
    bias_low = biases_here[...] - bias_high

    def bias_rows(layer):
        return jnp.concatenate(
            [
                0.5 * bias_high[layer : layer + 1],
                0.5 * bias_low[layer : layer + 1],
                jnp.zeros((14, HID), f32),
            ],
            axis=0,
        )

    def turned_first(half):
        tall = jnp.concatenate([0.5 * half, bias_rows(0), jnp.zeros((32, HID), f32)], axis=0)
        return tall.T[:, :96]

    l_one[...] = jnp.concatenate([turned_first(even), turned_first(odd)], axis=0).astype(bf16)
    for layer, source, ahead, back in (
        (1, w_second_here, l_two, v_two),
        (2, w_third_here, l_three, v_three),
    ):
        matrix = 0.5 * source[...].astype(f32)
        back[...] = matrix.astype(bf16)
        tall = jnp.concatenate([bias_rows(layer), jnp.zeros((112, HID), f32)], axis=0)
        ahead[...] = jnp.concatenate([matrix.T, tall.T[:, :16]], axis=1).astype(bf16)
    turned_out = w_out_here[...].astype(f32)
    readout = jnp.concatenate([turned_out, jnp.zeros((HID - FIELDS, HID), f32)], axis=0).T
    zero8 = jnp.zeros((8, LANES), f32)
    l_out[...] = jnp.concatenate(
        [
            jnp.concatenate([turned_out, zero4, zero8], axis=0),
            jnp.concatenate([zero4, turned_out, zero8], axis=0),
        ],
        axis=1,
    ).astype(bf16)
    v_out[...] = jnp.concatenate(
        [0.5 * readout[:, :16], 0.5 * pltpu.roll(readout, FIELDS, 1)[:, :16]], axis=0
    ).astype(bf16)
    field_row = lax.rem(lax.broadcasted_iota(jnp.int32, (8, LANES), 0), FIELDS)
    bias_tile = jnp.zeros((8, LANES), f32)
    for k in range(FIELDS):
        bias_tile = jnp.where(field_row == k, bias_out[k], bias_tile)
    bias_plane = jnp.concatenate([bias_tile] * 8, axis=0)
    for each in (g_one, g_two, g_three, g_four):
        each[...] = jnp.zeros(each.shape, f32)

    lane = lane_index(ROWS)
    lane8 = lane_index(8)
    sub_width = WIDE // SUBS
    ones_rows = lax.broadcasted_iota(jnp.int32, (16, WIDE), 0)
    ones_wide = jnp.where(ones_rows < 2, 1.0, 0.0).astype(bf16)
    ones_cells = jnp.concatenate([ones_wide[:, :sub_width]] * 2, axis=1)

    def to_right(plane, e, z):
        return jnp.where(
            lane == LANES - 1, unpack_lane(x_hi[e, z], 0, LANES - 1), pltpu.roll(plane, LANES - 1, 1)
        )

    def stencil(e, z):
        here, ahead, behind = st[e, z + 1], st[e, z + 2], st[e, z]
        beyond = y_hi[e, z]
        at_right = to_right(here, e, z)
        at_left = jnp.where(lane == 0, unpack_lane(x_lo[e, z], 0, 0), pltpu.roll(here, 1, 1))
        corner = jnp.where(
            lane8 == LANES - 1,
            pltpu.roll(xy_hi[e, z], LANES - 1, 1),
            pltpu.roll(beyond, LANES - 1, 1),
        )
        return (
            here,
            at_right,
            at_left,
            rows_down(here, beyond[0:4]),
            rows_up(here, y_lo[e, z][4:8]),
            ahead,
            behind,
            rows_down(at_right, corner[0:4]),
            rows_down(ahead, y_hi[e, z + 1][0:4]),
            to_right(ahead, e, z + 1),
        )

    def arrange(points):
        rows = jnp.concatenate([wide_of(point) for point in points], axis=0)
        return jnp.concatenate([rows.astype(bf16), ones_wide], axis=0)

    def laplace(points):
        total_of = -6.0 * points[0]
        for point in points[1:7]:
            total_of = total_of + point
        return total_of

    def layers(features, values, doubled):
        value, slope = silu_parts(side_by_side(mm(l_one[...], features)))
        values.append(value)
        doubled.append(slope)
        yield
        for matrix in (l_two, l_three):
            cells = jnp.concatenate([value, ones_cells], axis=0)
            value, slope = silu_parts(mm(matrix[...], cells))
            values.append(value)
            doubled.append(slope)
            yield

    def readout_of(value):
        return mm(l_out[...], stacked_of(value))[0:8]

    def times(product, slope):
        return product.astype(bf16) * slope

    def grad_rows(adjoint):
        scaled = wide_of(time_step * adjoint)
        return jnp.concatenate([scaled, jnp.zeros((8, WIDE), f32)], axis=0).astype(bf16)

    def backward(features, values, doubled, grad_out):
        ones_here = ones_cells[:, :sub_width]
        back_three = times(side_by_side(mm(v_out[...], grad_out)), doubled[2])
        yield
        back_two = times(mm(v_three[...], back_three), doubled[1])
        yield
        g_four[:, 0:16] += mm_cells(
            jnp.concatenate([stacked_of(values[2]), ones_here], axis=0), grad_out
        )
        back_one = stacked_of(times(mm(v_two[...], back_two), doubled[0]))
        yield
        g_three[...] += mm_cells(jnp.concatenate([values[1], ones_cells], axis=0), back_three)
        yield
        g_two[...] += mm_cells(jnp.concatenate([values[0], ones_cells], axis=0), back_two)
        yield
        g_one[...] += mm_cells(features, back_one)
        return back_one

    def in_turn(pieces):
        results = [None] * len(pieces)
        running = list(range(len(pieces)))
        while running:
            for number in list(running):
                try:
                    next(pieces[number])
                except StopIteration as end:
                    results[number] = end.value
                    running.remove(number)
        return results

    def send_adjoint(e, z, wide, adjoint):
        spread = spread4[z] * adjoint
        for j in range(STENCIL):
            part = plane_of(wide[8 * j : 8 * j + 8])
            if j == 0:
                part = part - 6.0 * spread
            elif j < 7:
                part = part + spread
            q[e, z + 1, j] = part
        empty = jnp.zeros((8, LANES), f32)
        across = pack_lane(q[e, z + 1, 1], LANES - 1, 0, empty)
        across = pack_lane(q[e, z + 1, 9], LANES - 1, 8, across)
        pa_last[e, z] = pack_lane(q[e, z + 1, 7], LANES - 1, 16, across)
        pa_first[e, z] = pack_lane(q[e, z + 1, 2], 0, 0, empty)
        slanted = q[e, z + 1, 7, 56:64]
        slanted = jnp.where(lane8 == 0, 0.0, pltpu.roll(slanted, 1, 1))
        y_tiles[e, z, 0:8] = q[e, z + 1, 3, 56:64] + slanted
        y_tiles[e, z, 8:16] = q[e, z + 1, 8, 56:64]
        start(adjoint_copies(e, z))

        @pl.when(z == 0)
        def _():
            start(adjoint_copies_low(e))

        @pl.when(z == PLANES - 1)
        def _():
            moved = jnp.where(lane == 0, 0.0, pltpu.roll(q[e, PLANES, 9], 1, 1))
            z_up[e] = q[e, PLANES, 5] + moved + rows_up(q[e, PLANES, 8], zero4)
            start(adjoint_copies_high(e))

    def gather(e, z, adjoint):
        here = z + 1
        result = adjoint + q[e, here, 0] + q[e, z, 5] + q[e, z + 2, 6]
        from_left = q[e, here, 1] + q[e, z, 9] + rows_up(q[e, here, 7], zero4)
        packed = xa[e, here]
        direct = unpack_lane(packed + pltpu.roll(xa[e, z], LANES - 8, 1), 0, 0)
        corner = pltpu.roll(xya[e, z], LANES - 23, 1)[4:8]
        edge = direct + rows_up(unpack_lane(packed, 16, 0), corner)
        result = result + jnp.where(lane == 0, edge, pltpu.roll(from_left, 1, 1))
        result = result + jnp.where(
            lane == LANES - 1,
            unpack_lane(xb[e, z], 0, LANES - 1),
            pltpu.roll(q[e, here, 2], LANES - 1, 1),
        )
        rows_in = ya[e, here, 0:8] + ya[e, z, 8:16]
        result = result + rows_up(q[e, here, 3] + q[e, z, 8], rows_in[4:8])
        return result + rows_down(q[e, here, 4], yb[e, z][0:4])

    def await_fields(e, step):
        @pl.when(step == 0)
        def _():
            arrive(field_copies(e, 0))
            arrive(field_copies(e, 1))
            arrive(field_copies_high(e))

        @pl.when(step == 1)
        def _():
            arrive(field_copies(e, 5))
            arrive(field_copies_low(e))

        @pl.when(step == 2)
        def _():
            arrive(field_copies(e, 2))

        @pl.when(step == 3)
        def _():
            arrive(field_copies(e, 4))

        @pl.when(step == 4)
        def _():
            arrive(field_copies(e, 3))

    def await_adjoint(e, step):
        @pl.when(step == 0)
        def _():
            arrive(adjoint_copies(e, 0))
            arrive(adjoint_copies_high(e))

        @pl.when(step == 1)
        def _():
            arrive(adjoint_copies(e, 5))
            arrive(adjoint_copies(e, 4))
            arrive(adjoint_copies_low(e))

        @pl.when(step == 2)
        def _():
            arrive(adjoint_copies(e, 1))

        @pl.when(step == 3)
        def _():
            arrive(adjoint_copies(e, 3))

        @pl.when(step == 4)
        def _():
            arrive(adjoint_copies(e, 2))

    def piece(sub):
        return slice(sub * sub_width, (sub + 1) * sub_width)

    def beside(sub):
        return slice(2 * sub * sub_width, 2 * (sub + 1) * sub_width)

    def stepped(points, z, wide):
        closed = plane_of(wide) + bias_plane
        return points[0] + spread4[z] * laplace(points) + time_step * closed

    def put(target, z, plane):
        staged[...] = plane
        for k in range(FIELDS):
            target[k, z] = staged[pl.ds(k, 16, stride=FIELDS), :]

    def first_step(step, carry):
        z = place(step)
        await_fields(0, step)
        points = stencil(0, z)
        features = arrange(points)
        feats[z] = features

        def forward(sub):
            values, doubled = [], []
            for layer, _ in enumerate(layers(features[:, piece(sub)], values, doubled)):
                acts[layer, z, :, beside(sub)] = values[layer]
                slopes[layer, z, :, beside(sub)] = doubled[layer]
                yield
            return readout_of(values[2])

        outs = in_turn([forward(sub) for sub in range(SUBS)])
        st[1, z + 1] = stepped(points, z, jnp.concatenate(outs, axis=1))
        send_fields(1, z)
        return carry

    lax.fori_loop(0, PLANES, first_step, 0)

    def second_step(step, carry):
        z = place(step)
        await_fields(1, step)
        points = stencil(1, z)
        features = arrange(points)
        adjoint = cot[z]
        grad_out = grad_rows(adjoint)

        def both_ways(sub):
            values, doubled = [], []
            yield from layers(features[:, piece(sub)], values, doubled)
            out = readout_of(values[2])
            back_one = yield from backward(
                features[:, piece(sub)], values, doubled, grad_out[:, piece(sub)]
            )
            return out, mm(v_one[...], back_one)

        outs, wides = zip(*in_turn([both_ways(sub) for sub in range(SUBS)]))
        put(final_here, z, stepped(points, z, jnp.concatenate(outs, axis=1)))
        send_adjoint(0, z, jnp.concatenate(wides, axis=1), adjoint)
        return carry

    lax.fori_loop(0, PLANES, second_step, 0)
    final_copy = pltpu.make_async_copy(final_here, final_out, here_sem.at[8])
    final_copy.start()

    def first_back(step, carry):
        z = place(step)
        await_adjoint(0, step)
        adjoint = gather(0, z, cot[z])
        adj_mid[z] = adjoint
        grad_out = grad_rows(adjoint)

        def back(sub):
            values = [acts[layer, z, :, beside(sub)] for layer in range(3)]
            doubled = [slopes[layer, z, :, beside(sub)] for layer in range(3)]
            return backward(feats[z, :, piece(sub)], values, doubled, grad_out[:, piece(sub)])

        for sub, back_one in enumerate(in_turn([back(sub) for sub in range(SUBS)])):
            backs[z, :, piece(sub)] = back_one
        return carry

    lax.fori_loop(0, PLANES, first_back, 0)

    one = g_one[...]
    merged = one[:, :HID] + jnp.concatenate([one[4:, HID:], one[:4, HID:]], axis=0)
    first_rows = jnp.concatenate([merged[8 * j : 8 * j + 4] for j in range(STENCIL)], axis=0)
    four = g_four[...]
    shifted = four[:HID] + pltpu.roll(four[HID : 2 * HID], LANES - FIELDS, 1)
    last = four[2 * HID : 2 * HID + 8]
    last = last + pltpu.roll(last, LANES - FIELDS, 1)
    rest = jnp.concatenate(
        [
            one[80:81, :HID] + one[80:81, HID:],
            g_two[HID : HID + 1],
            g_three[HID : HID + 1],
            last[0:1],
            shifted.T[0:4],
        ],
        axis=0,
    )
    everything = jnp.concatenate(
        [
            g_two[0:HID],
            g_three[0:HID],
            first_rows,
            rest,
            jnp.zeros((SUMS - 304, LANES), f32),
        ],
        axis=0,
    )
    sums[...] = everything.reshape(nz, nx, share, LANES)

    pair = copy(sums.at[other], landed_pair, a_send.at[0, 0], a_recv.at[0, 0], (gx, gy, other))

    def scatter(step):
        target = lax.rem(gx + step, nx)
        return copy(
            sums.at[gz, target], landed_a.at[step], a_send.at[1, step], a_recv.at[1, step], (target, gy, gz)
        )

    def across(step):
        target = lax.rem(gy + step, ny)
        return copy(landed_b.at[gy], landed_b.at[gy], a_send.at[2, step], a_recv.at[2, gy], (gx, target, gz))

    def across_in(step):
        source = lax.rem(gy + ny - step, ny)
        return copy(landed_b.at[source], landed_b.at[source], a_send.at[2, step], a_recv.at[2, source], (gx, source, gz))

    def spread_out(step):
        target = lax.rem(gx + step, nx)
        return copy(total.at[gz, gx], total.at[gz, gx], a_send.at[3, step], a_recv.at[3, gx], (target, gy, gz))

    def spread_in(step):
        source = lax.rem(gx + nx - step, nx)
        return copy(total.at[gz, source], total.at[gz, source], a_send.at[3, step], a_recv.at[3, source], (source, gy, gz))

    def hand_over(step):
        source = lax.rem(gx + nx - step, nx)
        return copy(total.at[gz, source], total.at[gz, source], a_send.at[4, step], a_recv.at[4, source], (gx, gy, other))

    def hand_over_in(step):
        source = lax.rem(gx + nx - step, nx)
        return copy(total.at[other, source], total.at[other, source], a_send.at[4, step], a_recv.at[4, source], (gx, gy, other))

    def each(first, count, act):
        def body(step, carry):
            act(step)
            return carry

        lax.fori_loop(first, count, body, 0)

    def last_contributions(step, carry):
        z = place(step)
        send_adjoint(1, z, mm(v_one[...], backs[z]), adj_mid[z])
        return carry

    def last_gather(step, carry):
        z = place(step)
        await_adjoint(1, step)
        put(adjoint_here, z, gather(1, z, adj_mid[z]))
        return carry

    pair.start()
    lax.fori_loop(0, 2, last_contributions, 0)
    pair.wait_recv()
    sums[gz] = sums[gz] + landed_pair[...]
    each(1, nx, lambda step: scatter(step).start())
    lax.fori_loop(2, PLANES, last_contributions, 0)
    each(1, nx, lambda step: scatter(step).wait_recv())
    held = sums[gz, gx]
    for step in range(1, nx):
        held = held + landed_a[step]
    landed_b[gy] = held
    each(1, ny, lambda step: across(step).start())

    lax.fori_loop(0, PLANES, last_gather, 0)
    adjoint_copy = pltpu.make_async_copy(adjoint_here, adjoint_out, here_sem.at[9])
    adjoint_copy.start()

    each(1, ny, lambda step: across_in(step).wait_recv())
    held = landed_b[0]
    for step in range(1, ny):
        held = held + landed_b[step]
    total[gz, gx] = held * scale
    each(1, nx, lambda step: spread_out(step).start())
    hand_over(0).start()

    def finish_sends(z, carry):
        for e in range(2):
            sent(field_copies(e, z))
            sent(adjoint_copies(e, z))
        return carry

    lax.fori_loop(0, PLANES, finish_sends, 0)
    for e in range(2):
        sent(field_copies_low(e))
        sent(field_copies_high(e))
        sent(adjoint_copies_low(e))
        sent(adjoint_copies_high(e))
    pair.wait_send()
    each(1, nx, lambda step: scatter(step).wait_send())
    each(1, ny, lambda step: across(step).wait_send())
    final_copy.wait()
    adjoint_copy.wait()

    def pass_on(step):
        spread_in(step).wait_recv()
        hand_over(step).start()

    each(1, nx, pass_on)
    each(0, nx, lambda step: hand_over_in(step).wait_recv())

    whole = total[...].reshape(SUMS, LANES)
    g_second_out[...] = whole[0:HID]
    g_third_out[...] = whole[HID : 2 * HID]
    g_in_out[...] = whole[2 * HID : 2 * HID + 40]
    tail = whole[296:304]
    g_biases_out[...] = tail[0:3]
    g_readout_out[...] = tail[4:8]
    g_bias_out_out[...] = tail[3:4, 0:FIELDS]
    each(1, nx, lambda step: spread_out(step).wait_send())
    each(0, nx, lambda step: hand_over(step).wait_send())


def deliver(*refs):
    count = (len(refs) - 1) // 2
    copies = [
        pltpu.make_async_copy(refs[number], refs[count + number], refs[-1].at[number])
        for number in range(count)
    ]
    for each in copies:
        each.start()
    for each in copies:
        each.wait()


def solution(mesh):
    sizes = (mesh.shape["gx"], mesh.shape["gy"], mesh.shape["gz"])
    nx, ny, nz = sizes
    share = SUMS // nz // nx
    cells = PLANES * 16 * LANES * nx * ny * nz
    scale = 1.0 / (time_step * math.sqrt(float(cells)))
    vmem = pl.BlockSpec(memory_space=pltpu.VMEM)
    block = jax.ShapeDtypeStruct((FIELDS, PLANES, 16, LANES), f32)
    tile = (8, LANES)
    dma = pltpu.SemaphoreType.DMA

    def buffer(*shape):
        return pltpu.VMEM(shape, f32)

    def packed(*shape):
        return pltpu.VMEM(shape, bf16)

    scratch = [
        buffer(FIELDS, PLANES, 16, LANES),
        buffer(FIELDS, PLANES, 16, LANES),
        buffer(PLANES, 16, LANES),
        packed(40, HID),
        packed(HID, HID),
        packed(HID, HID),
        packed(FIELDS, HID),
        buffer(3, HID),
        buffer(FIELDS, PLANES, 16, LANES),
        buffer(FIELDS, PLANES, 16, LANES),
        buffer(2, PLANES + 2, ROWS, LANES),
        buffer(2, PLANES, *tile),
        buffer(2, PLANES, *tile),
        buffer(2, PLANES, *tile),
        buffer(2, PLANES + 1, *tile),
        buffer(2, PLANES, *tile),
        buffer(2, PLANES, *tile),
        buffer(2, PLANES + 1, *tile),
        buffer(PLANES, ROWS, LANES),
        buffer(PLANES, ROWS, LANES),
        buffer(PLANES, ROWS, LANES),
        buffer(ROWS, LANES),
        packed(PLANES, 96, WIDE),
        packed(3, PLANES, HID, 2 * WIDE),
        packed(3, PLANES, HID, 2 * WIDE),
        packed(PLANES, 2 * HID, WIDE),
        buffer(2, PLANES + 2, STENCIL, ROWS, LANES),
        buffer(2, PLANES, *tile),
        buffer(2, PLANES, *tile),
        buffer(2, PLANES, 16, LANES),
        buffer(2, ROWS, LANES),
        buffer(2, PLANES + 1, *tile),
        buffer(2, PLANES, *tile),
        buffer(2, PLANES, *tile),
        buffer(2, PLANES + 1, 16, LANES),
        buffer(2, PLANES, *tile),
        packed(2 * HID, 96),
        packed(HID, 144),
        packed(HID, 144),
        packed(16, 2 * HID),
        packed(2 * HID, 16),
        packed(HID, HID),
        packed(HID, HID),
        packed(80, 2 * HID),
        buffer(96, 2 * HID),
        buffer(144, HID),
        buffer(144, HID),
        buffer(2 * HID + 16, LANES),
        buffer(nz, nx, share, LANES),
        buffer(nx, share, LANES),
        buffer(nx, share, LANES),
        buffer(ny, share, LANES),
        buffer(nz, nx, share, LANES),
        dma((2, 5, PLANES)),
        dma((2, 5, PLANES)),
        dma((2, 4)),
        dma((2, 4)),
        dma((2, 5, PLANES)),
        dma((2, 5, PLANES)),
        dma((2, 4)),
        dma((2, 4)),
        dma((5, max(nx, ny))),
        dma((5, max(nx, ny))),
        dma((10,)),
    ]

    shapes = (
        block,
        block,
        jax.ShapeDtypeStruct((40, HID), f32),
        jax.ShapeDtypeStruct((HID, HID), f32),
        jax.ShapeDtypeStruct((HID, HID), f32),
        jax.ShapeDtypeStruct((FIELDS, HID), f32),
        jax.ShapeDtypeStruct((3, HID), f32),
        jax.ShapeDtypeStruct((1, FIELDS), f32),
    )
    anywhere = pl.BlockSpec(memory_space=pl.ANY)

    def on_device(state, cotangent, diffusion, w_in, w_second, w_third, w_out, biases, bias_out):
        outs = pl.pallas_call(
            functools.partial(kernel, sizes, scale),
            out_shape=shapes,
            in_specs=[anywhere] * 8 + [pl.BlockSpec(memory_space=pltpu.SMEM)],
            out_specs=[anywhere] * 2 + [vmem] * 6,
            scratch_shapes=scratch,
            compiler_params=pltpu.CompilerParams(
                collective_id=0, has_side_effects=True, vmem_limit_bytes=60 * 2**20
            ),
            name="two_steps_and_adjoint",
        )(state, cotangent, diffusion, w_in, w_second, w_third, w_out.T, biases, bias_out)
        outs = pl.pallas_call(
            deliver,
            out_shape=shapes,
            in_specs=[anywhere] * 8,
            out_specs=[anywhere] * 8,
            scratch_shapes=[dma((8,))],
            compiler_params=pltpu.CompilerParams(vmem_limit_bytes=60 * 2**20),
            name="deliver",
        )(*outs)
        return outs[:5] + (outs[5].T, outs[6], outs[7].reshape(FIELDS))

    fields = P(None, "gz", "gy", "gx")
    placed = (fields, fields, P("gz", "gy", "gx")) + (P(),) * 6
    return jax.shard_map(
        on_device,
        mesh=mesh,
        in_specs=placed,
        out_specs=(fields, fields) + (P(),) * 6,
        check_vma=False,
    )
```

```python
import functools
import math

import jax
import jax.numpy as jnp
from jax import lax
from jax.experimental import pallas as pl
from jax.experimental.pallas import tpu as pltpu
from jax.sharding import PartitionSpec as P

bf16 = jnp.bfloat16
f32 = jnp.float32
MESH = pl.DeviceIdType.MESH

time_step = 0.1
FIELDS = 4
STENCIL = 10
PLANES = 6
ROWS = 64
LANES = 128
WIDE = 1024
HID = 128
SUMS = 384
SUBS = 2


def mm(former, latter):
    return lax.dot_general(former, latter, (((1,), (0,)), ((), ())), preferred_element_type=f32)


def mm_cells(former, latter):
    return lax.dot_general(former, latter, (((1,), (1,)), ((), ())), preferred_element_type=f32)


def lane_index(rows):
    return lax.broadcasted_iota(jnp.int32, (rows, LANES), 1)


def pack_lane(plane, lane, base, onto):
    index = lane_index(8)
    for part in range(8):
        moved = pltpu.roll(plane[8 * part : 8 * part + 8], (base + part - lane) % LANES, 1)
        onto = jnp.where(index == base + part, moved, onto)
    return onto


def unpack_lane(packed, base, lane):
    return jnp.concatenate(
        [pltpu.roll(packed, (lane - base - part) % LANES, 1) for part in range(8)], axis=0
    )


def rows_up(plane, first):
    return jnp.concatenate([first, plane[: ROWS - 4]], axis=0)


def rows_down(plane, last):
    return jnp.concatenate([plane[4:], last], axis=0)


def wide_of(plane):
    return jnp.concatenate([plane[8 * part : 8 * part + 8] for part in range(8)], axis=1)


def plane_of(wide):
    return jnp.concatenate(
        [wide[:, LANES * part : LANES * (part + 1)] for part in range(8)], axis=0
    )


def side_by_side(stacked):
    return jnp.concatenate([stacked[:HID], stacked[HID:]], axis=1)


def stacked_of(beside):
    half = beside.shape[1] // 2
    return jnp.concatenate([beside[:, :half], beside[:, half:]], axis=0)


def silu_parts(half):
    half = half.astype(bf16)
    turned = jnp.tanh(half)
    raised = 1 + turned
    value = half * raised
    slope = raised * (1 - half * turned) + value
    return value, slope


def kernel(
    sizes,
    scale,
    state_in,
    cot_in,
    diff_in,
    w_in,
    w_second,
    w_third,
    w_out,
    biases,
    bias_out,
    final_out,
    adjoint_out,
    sums_out,
    state_here,
    cot_here,
    diff_here,
    w_in_here,
    w_second_here,
    w_third_here,
    w_out_here,
    biases_here,
    final_here,
    adjoint_here,
    st,
    p_first,
    p_last,
    x_lo,
    x_hi,
    xy_hi,
    y_lo,
    y_hi,
    spread4,
    cot,
    adj_mid,
    staged,
    feats,
    acts,
    slopes,
    backs,
    q,
    pa_last,
    pa_first,
    y_tiles,
    z_up,
    xa,
    xb,
    xya,
    ya,
    yb,
    l_one,
    l_two,
    l_three,
    l_out,
    v_out,
    v_three,
    v_two,
    v_one,
    g_one,
    g_two,
    g_three,
    g_four,
    g_last,
    sums,
    landed_pair,
    landed_a,
    landed_b,
    total,
    f_send,
    f_recv,
    f_send_z,
    f_recv_z,
    b_send,
    b_recv,
    b_send_z,
    b_recv_z,
    a_send,
    a_recv,
    here_sem,
):
    nx, ny, nz = sizes
    gx, gy, gz = lax.axis_index("gx"), lax.axis_index("gy"), lax.axis_index("gz")
    right, left = lax.rem(gx + 1, nx), lax.rem(gx + nx - 1, nx)
    above, below = lax.rem(gy + 1, ny), lax.rem(gy + ny - 1, ny)
    other = 1 - gz
    share = SUMS // nz // nx

    barrier = pltpu.get_barrier_semaphore()

    def greet(device):
        pl.semaphore_signal(barrier, inc=1, device_id=device, device_id_type=MESH)

    for device in (
        (right, above, gz),
        (left, below, gz),
        (gx, above, other),
        (gx, below, other),
        (right, gy, other),
        (left, gy, other),
        (gx, gy, other),
    ):
        greet(device)

    def greet_row(step, carry):
        greet((lax.rem(gx + step, nx), gy, gz))
        return carry

    lax.fori_loop(1, nx, greet_row, 0)

    def greet_column(step, carry):
        greet((gx, lax.rem(gy + step, ny), gz))
        return carry

    lax.fori_loop(1, ny, greet_column, 0)

    fetches = [
        pltpu.make_async_copy(source, target, here_sem.at[number])
        for number, (source, target) in enumerate(
            (
                (state_in, state_here),
                (cot_in, cot_here),
                (diff_in, diff_here),
                (w_in, w_in_here),
                (w_second, w_second_here),
                (w_third, w_third_here),
                (w_out, w_out_here),
                (biases, biases_here),
            )
        )
    ]
    for fetch in fetches:
        fetch.start()

    def copy(source, target, send, recv, device):
        return pltpu.make_async_remote_copy(
            src_ref=source,
            dst_ref=target,
            send_sem=send,
            recv_sem=recv,
            device_id=device,
            device_id_type=MESH,
        )

    def field_copies(e, z):
        send, recv = f_send, f_recv
        return (
            copy(p_last.at[e, z], x_lo.at[e, z], send.at[e, 0, z], recv.at[e, 0, z], (right, gy, gz)),
            copy(p_first.at[e, z], x_hi.at[e, z], send.at[e, 1, z], recv.at[e, 1, z], (left, gy, gz)),
            copy(p_first.at[e, z], xy_hi.at[e, z], send.at[e, 2, z], recv.at[e, 2, z], (left, below, gz)),
            copy(st.at[e, z + 1, pl.ds(56, 8)], y_lo.at[e, z], send.at[e, 3, z], recv.at[e, 3, z], (gx, above, gz)),
            copy(st.at[e, z + 1, pl.ds(0, 8)], y_hi.at[e, z], send.at[e, 4, z], recv.at[e, 4, z], (gx, below, gz)),
        )

    def field_copies_low(e):
        send, recv = f_send_z, f_recv_z
        return (
            copy(p_first.at[e, 0], x_hi.at[e, PLANES], send.at[e, 0], recv.at[e, 0], (left, gy, other)),
            copy(st.at[e, 1, pl.ds(0, 8)], y_hi.at[e, PLANES], send.at[e, 1], recv.at[e, 1], (gx, below, other)),
            copy(st.at[e, 1], st.at[e, PLANES + 1], send.at[e, 2], recv.at[e, 2], (gx, gy, other)),
        )

    def field_copies_high(e):
        return (
            copy(st.at[e, PLANES], st.at[e, 0], f_send_z.at[e, 3], f_recv_z.at[e, 3], (gx, gy, other)),
        )

    def adjoint_copies(e, z):
        send, recv = b_send, b_recv
        return (
            copy(pa_last.at[e, z], xa.at[e, z + 1], send.at[e, 0, z], recv.at[e, 0, z], (right, gy, gz)),
            copy(pa_first.at[e, z], xb.at[e, z], send.at[e, 1, z], recv.at[e, 1, z], (left, gy, gz)),
            copy(pa_last.at[e, z], xya.at[e, z], send.at[e, 2, z], recv.at[e, 2, z], (right, above, gz)),
            copy(y_tiles.at[e, z], ya.at[e, z + 1], send.at[e, 3, z], recv.at[e, 3, z], (gx, above, gz)),
            copy(q.at[e, z + 1, 4, pl.ds(0, 8)], yb.at[e, z], send.at[e, 4, z], recv.at[e, 4, z], (gx, below, gz)),
        )

    def adjoint_copies_high(e):
        send, recv = b_send_z, b_recv_z
        return (
            copy(pa_last.at[e, PLANES - 1], xa.at[e, 0], send.at[e, 0], recv.at[e, 0], (right, gy, other)),
            copy(y_tiles.at[e, PLANES - 1], ya.at[e, 0], send.at[e, 1], recv.at[e, 1], (gx, above, other)),
            copy(z_up.at[e], q.at[e, 0, 5], send.at[e, 2], recv.at[e, 2], (gx, gy, other)),
        )

    def adjoint_copies_low(e):
        return (
            copy(q.at[e, 1, 6], q.at[e, PLANES + 1, 6], b_send_z.at[e, 3], b_recv_z.at[e, 3], (gx, gy, other)),
        )

    def start(copies):
        for each in copies:
            each.start()

    def arrive(copies):
        for each in copies:
            each.wait_recv()

    def sent(copies):
        for each in copies:
            each.wait_send()

    def pack_fields(e, z):
        plane = st[e, z + 1]
        empty = jnp.zeros((8, LANES), f32)
        p_first[e, z] = pack_lane(plane, 0, 0, empty)
        p_last[e, z] = pack_lane(plane, LANES - 1, 0, empty)

    def send_fields(e, z):
        start(field_copies(e, z))

        @pl.when(z == 0)
        def _():
            start(field_copies_low(e))

        @pl.when(z == PLANES - 1)
        def _():
            start(field_copies_high(e))

    def place(step):
        odd = lax.rem(step, 2)
        half = lax.div(step, 2)
        return half + odd * (PLANES - 1 - 2 * half)

    def lay_out(z, carry):
        for k in range(FIELDS):
            st[0, z + 1, pl.ds(k, 16, stride=FIELDS), :] = state_here[k, z]
        pack_fields(0, z)
        return carry

    fetches[0].wait()
    lax.fori_loop(0, PLANES, lay_out, 0)
    pl.semaphore_wait(barrier, 7 + (nx - 1) + (ny - 1))

    def first_sends(step, carry):
        send_fields(0, place(step))
        return carry

    lax.fori_loop(0, PLANES, first_sends, 0)

    for fetch in fetches[1:]:
        fetch.wait()

    def lay_out_rest(z, carry):
        for k in range(FIELDS):
            cot[z, pl.ds(k, 16, stride=FIELDS), :] = cot_here[k, z]
            spread4[z, pl.ds(k, 16, stride=FIELDS), :] = diff_here[z]
        return carry

    lax.fori_loop(0, PLANES, lay_out_rest, 0)
    for e in range(2):
        for j in (8, 9):
            q[e, 0, j] = jnp.zeros((ROWS, LANES), f32)

    zero4 = jnp.zeros((4, LANES), f32)
    first = w_in_here[...].astype(f32)
    parts = [first[4 * j : 4 * j + 4] for j in range(STENCIL)]
    even = jnp.concatenate([piece for part in parts for piece in (part, zero4)], axis=0)
    odd = jnp.concatenate([piece for part in parts for piece in (zero4, part)], axis=0)
    v_one[...] = jnp.concatenate([even, odd], axis=1).astype(bf16)
    bias_high = biases_here[...].astype(bf16).astype(f32)
    bias_low = biases_here[...] - bias_high

    def bias_rows(layer):
        return jnp.concatenate(
            [
                0.5 * bias_high[layer : layer + 1],
                0.5 * bias_low[layer : layer + 1],
                jnp.zeros((14, HID), f32),
            ],
            axis=0,
        )

    def turned_first(half):
        tall = jnp.concatenate([0.5 * half, bias_rows(0), jnp.zeros((32, HID), f32)], axis=0)
        return tall.T[:, :96]

    l_one[...] = jnp.concatenate([turned_first(even), turned_first(odd)], axis=0).astype(bf16)
    for layer, source, ahead, back in (
        (1, w_second_here, l_two, v_two),
        (2, w_third_here, l_three, v_three),
    ):
        matrix = 0.5 * source[...].astype(f32)
        back[...] = matrix.astype(bf16)
        tall = jnp.concatenate([bias_rows(layer), jnp.zeros((112, HID), f32)], axis=0)
        ahead[...] = jnp.concatenate([matrix.T, tall.T[:, :16]], axis=1).astype(bf16)
    turned_out = w_out_here[...].astype(f32)
    readout = jnp.concatenate([turned_out, jnp.zeros((HID - FIELDS, HID), f32)], axis=0).T
    zero8 = jnp.zeros((8, LANES), f32)
    l_out[...] = jnp.concatenate(
        [
            jnp.concatenate([turned_out, zero4, zero8], axis=0),
            jnp.concatenate([zero4, turned_out, zero8], axis=0),
        ],
        axis=1,
    ).astype(bf16)
    v_out[...] = jnp.concatenate(
        [0.5 * readout[:, :16], 0.5 * pltpu.roll(readout, FIELDS, 1)[:, :16]], axis=0
    ).astype(bf16)
    field_row = lax.rem(lax.broadcasted_iota(jnp.int32, (8, LANES), 0), FIELDS)
    bias_tile = jnp.zeros((8, LANES), f32)
    for k in range(FIELDS):
        bias_tile = jnp.where(field_row == k, bias_out[k], bias_tile)
    bias_plane = jnp.concatenate([bias_tile] * 8, axis=0)
    for each in (g_one, g_two, g_three, g_four, g_last):
        each[...] = jnp.zeros(each.shape, f32)

    lane = lane_index(ROWS)
    lane8 = lane_index(8)
    sub_width = WIDE // SUBS
    ones_rows = lax.broadcasted_iota(jnp.int32, (16, WIDE), 0)
    ones_wide = jnp.where(ones_rows < 2, 1.0, 0.0).astype(bf16)
    ones_cells = jnp.concatenate([ones_wide[:, :sub_width]] * 2, axis=1)

    def to_right(plane, e, z):
        return jnp.where(
            lane == LANES - 1, unpack_lane(x_hi[e, z], 0, LANES - 1), pltpu.roll(plane, LANES - 1, 1)
        )

    def stencil(e, z):
        here, ahead, behind = st[e, z + 1], st[e, z + 2], st[e, z]
        beyond = y_hi[e, z]
        at_right = to_right(here, e, z)
        at_left = jnp.where(lane == 0, unpack_lane(x_lo[e, z], 0, 0), pltpu.roll(here, 1, 1))
        corner = jnp.where(
            lane8 == LANES - 1,
            pltpu.roll(xy_hi[e, z], LANES - 1, 1),
            pltpu.roll(beyond, LANES - 1, 1),
        )
        return (
            here,
            at_right,
            at_left,
            rows_down(here, beyond[0:4]),
            rows_up(here, y_lo[e, z][4:8]),
            ahead,
            behind,
            rows_down(at_right, corner[0:4]),
            rows_down(ahead, y_hi[e, z + 1][0:4]),
            to_right(ahead, e, z + 1),
        )

    def arrange(points):
        rows = jnp.concatenate([wide_of(point) for point in points], axis=0)
        return jnp.concatenate([rows.astype(bf16), ones_wide], axis=0)

    def laplace(points):
        total_of = -6.0 * points[0]
        for point in points[1:7]:
            total_of = total_of + point
        return total_of

    def layers(features, values, doubled):
        value, slope = silu_parts(side_by_side(mm(l_one[...], features)))
        values.append(value)
        doubled.append(slope)
        yield
        for matrix in (l_two, l_three):
            cells = jnp.concatenate([value, ones_cells], axis=0)
            value, slope = silu_parts(mm(matrix[...], cells))
            values.append(value)
            doubled.append(slope)
            yield

    def readout_of(value):
        return mm(l_out[...], stacked_of(value))[0:8]

    def times(product, slope):
        return product.astype(bf16) * slope

    def grad_rows(adjoint):
        scaled = wide_of(time_step * adjoint)
        rounded = jnp.concatenate([scaled, jnp.zeros((8, WIDE), f32)], axis=0).astype(bf16)
        added = rounded.astype(f32)[0:8]
        for part in range(8):
            g_last[...] += added[:, LANES * part : LANES * (part + 1)]
        return rounded

    def backward(features, values, doubled, grad_out):
        back_three = times(side_by_side(mm(v_out[...], grad_out)), doubled[2])
        yield
        back_two = times(mm(v_three[...], back_three), doubled[1])
        yield
        g_four[...] += mm_cells(grad_out, stacked_of(values[2]))
        back_one = stacked_of(times(mm(v_two[...], back_two), doubled[0]))
        yield
        g_three[...] += mm_cells(jnp.concatenate([values[1], ones_cells], axis=0), back_three)
        yield
        g_two[...] += mm_cells(jnp.concatenate([values[0], ones_cells], axis=0), back_two)
        yield
        g_one[...] += mm_cells(features, back_one)
        return back_one

    def in_turn(pieces):
        results = [None] * len(pieces)
        running = list(range(len(pieces)))
        while running:
            for number in list(running):
                try:
                    next(pieces[number])
                except StopIteration as end:
                    results[number] = end.value
                    running.remove(number)
        return results

    def send_adjoint(e, z, wide, adjoint):
        spread = spread4[z] * adjoint
        for j in range(STENCIL):
            part = plane_of(wide[8 * j : 8 * j + 8])
            if j == 0:
                part = part - 6.0 * spread
            elif j < 7:
                part = part + spread
            q[e, z + 1, j] = part
        empty = jnp.zeros((8, LANES), f32)
        across = pack_lane(q[e, z + 1, 1], LANES - 1, 0, empty)
        across = pack_lane(q[e, z + 1, 9], LANES - 1, 8, across)
        pa_last[e, z] = pack_lane(q[e, z + 1, 7], LANES - 1, 16, across)
        pa_first[e, z] = pack_lane(q[e, z + 1, 2], 0, 0, empty)
        slanted = q[e, z + 1, 7, 56:64]
        slanted = jnp.where(lane8 == 0, 0.0, pltpu.roll(slanted, 1, 1))
        y_tiles[e, z, 0:8] = q[e, z + 1, 3, 56:64] + slanted
        y_tiles[e, z, 8:16] = q[e, z + 1, 8, 56:64]
        start(adjoint_copies(e, z))

        @pl.when(z == 0)
        def _():
            start(adjoint_copies_low(e))

        @pl.when(z == PLANES - 1)
        def _():
            moved = jnp.where(lane == 0, 0.0, pltpu.roll(q[e, PLANES, 9], 1, 1))
            z_up[e] = q[e, PLANES, 5] + moved + rows_up(q[e, PLANES, 8], zero4)
            start(adjoint_copies_high(e))

    def gather(e, z, adjoint):
        here = z + 1
        result = adjoint + q[e, here, 0] + q[e, z, 5] + q[e, z + 2, 6]
        from_left = q[e, here, 1] + q[e, z, 9] + rows_up(q[e, here, 7], zero4)
        packed = xa[e, here]
        direct = unpack_lane(packed + pltpu.roll(xa[e, z], LANES - 8, 1), 0, 0)
        corner = pltpu.roll(xya[e, z], LANES - 23, 1)[4:8]
        edge = direct + rows_up(unpack_lane(packed, 16, 0), corner)
        result = result + jnp.where(lane == 0, edge, pltpu.roll(from_left, 1, 1))
        result = result + jnp.where(
            lane == LANES - 1,
            unpack_lane(xb[e, z], 0, LANES - 1),
            pltpu.roll(q[e, here, 2], LANES - 1, 1),
        )
        rows_in = ya[e, here, 0:8] + ya[e, z, 8:16]
        result = result + rows_up(q[e, here, 3] + q[e, z, 8], rows_in[4:8])
        return result + rows_down(q[e, here, 4], yb[e, z][0:4])

    def await_fields(e, step):
        @pl.when(step == 0)
        def _():
            arrive(field_copies(e, 0))
            arrive(field_copies(e, 1))
            arrive(field_copies_high(e))

        @pl.when(step == 1)
        def _():
            arrive(field_copies(e, 5))
            arrive(field_copies_low(e))

        @pl.when(step == 2)
        def _():
            arrive(field_copies(e, 2))

        @pl.when(step == 3)
        def _():
            arrive(field_copies(e, 4))

        @pl.when(step == 4)
        def _():
            arrive(field_copies(e, 3))

    def await_adjoint(e, step):
        @pl.when(step == 0)
        def _():
            arrive(adjoint_copies(e, 0))
            arrive(adjoint_copies_high(e))

        @pl.when(step == 1)
        def _():
            arrive(adjoint_copies(e, 5))
            arrive(adjoint_copies(e, 4))
            arrive(adjoint_copies_low(e))

        @pl.when(step == 2)
        def _():
            arrive(adjoint_copies(e, 1))

        @pl.when(step == 3)
        def _():
            arrive(adjoint_copies(e, 3))

        @pl.when(step == 4)
        def _():
            arrive(adjoint_copies(e, 2))

    def piece(sub):
        return slice(sub * sub_width, (sub + 1) * sub_width)

    def beside(sub):
        return slice(2 * sub * sub_width, 2 * (sub + 1) * sub_width)

    def stepped(points, z, wide):
        closed = plane_of(wide) + bias_plane
        return points[0] + spread4[z] * laplace(points) + time_step * closed

    def put(target, z, plane):
        staged[...] = plane
        for k in range(FIELDS):
            target[k, z] = staged[pl.ds(k, 16, stride=FIELDS), :]

    def first_step(step, carry):
        z = place(step)
        await_fields(0, step)
        points = stencil(0, z)
        features = arrange(points)
        feats[z] = features

        def forward(sub):
            values, doubled = [], []
            for layer, _ in enumerate(layers(features[:, piece(sub)], values, doubled)):
                acts[layer, z, :, beside(sub)] = values[layer]
                slopes[layer, z, :, beside(sub)] = doubled[layer]
                yield
            return readout_of(values[2])

        outs = in_turn([forward(sub) for sub in range(SUBS)])
        st[1, z + 1] = stepped(points, z, jnp.concatenate(outs, axis=1))
        pack_fields(1, z)
        send_fields(1, z)
        return carry

    lax.fori_loop(0, PLANES, first_step, 0)

    def second_step(step, carry):
        z = place(step)
        await_fields(1, step)
        points = stencil(1, z)
        features = arrange(points)
        adjoint = cot[z]
        grad_out = grad_rows(adjoint)

        def both_ways(sub):
            values, doubled = [], []
            yield from layers(features[:, piece(sub)], values, doubled)
            out = readout_of(values[2])
            back_one = yield from backward(
                features[:, piece(sub)], values, doubled, grad_out[:, piece(sub)]
            )
            return out, mm(v_one[...], back_one)

        outs, wides = zip(*in_turn([both_ways(sub) for sub in range(SUBS)]))
        put(final_here, z, stepped(points, z, jnp.concatenate(outs, axis=1)))
        send_adjoint(0, z, jnp.concatenate(wides, axis=1), adjoint)
        return carry

    lax.fori_loop(0, PLANES, second_step, 0)
    final_copy = pltpu.make_async_copy(final_here, final_out, here_sem.at[8])
    final_copy.start()

    def first_back(step, carry):
        z = place(step)
        await_adjoint(0, step)
        adjoint = gather(0, z, cot[z])
        adj_mid[z] = adjoint
        grad_out = grad_rows(adjoint)

        def back(sub):
            values = [acts[layer, z, :, beside(sub)] for layer in range(3)]
            doubled = [slopes[layer, z, :, beside(sub)] for layer in range(3)]
            return backward(feats[z, :, piece(sub)], values, doubled, grad_out[:, piece(sub)])

        for sub, back_one in enumerate(in_turn([back(sub) for sub in range(SUBS)])):
            backs[z, :, piece(sub)] = back_one
        return carry

    lax.fori_loop(0, PLANES, first_back, 0)

    one = g_one[...]
    merged = one[:, :HID] + jnp.concatenate([one[4:, HID:], one[:4, HID:]], axis=0)
    first_rows = jnp.concatenate([merged[8 * j : 8 * j + 4] for j in range(STENCIL)], axis=0)
    readout_rows = g_four[0:4, :HID] + g_four[4:8, HID:]
    last = jnp.sum(g_last[...], axis=1, keepdims=True)
    last = last[0:4] + last[4:8]
    row = lax.broadcasted_iota(jnp.int32, (FIELDS, LANES), 0)
    column = lax.broadcasted_iota(jnp.int32, (FIELDS, LANES), 1)
    last = jnp.sum(jnp.where(row == column, last, 0.0), axis=0, keepdims=True)
    rest = jnp.concatenate(
        [
            one[80:81, :HID] + one[80:81, HID:],
            g_two[HID : HID + 1],
            g_three[HID : HID + 1],
            last,
            readout_rows,
        ],
        axis=0,
    )
    everything = jnp.concatenate(
        [
            g_two[0:HID],
            g_three[0:HID],
            first_rows,
            rest,
            jnp.zeros((SUMS - 304, LANES), f32),
        ],
        axis=0,
    )
    sums[...] = everything.reshape(nz, nx, share, LANES)

    pair = copy(sums.at[other], landed_pair, a_send.at[0, 0], a_recv.at[0, 0], (gx, gy, other))

    def scatter(step):
        target = lax.rem(gx + step, nx)
        return copy(
            sums.at[gz, target], landed_a.at[step], a_send.at[1, step], a_recv.at[1, step], (target, gy, gz)
        )

    def across(step):
        target = lax.rem(gy + step, ny)
        return copy(landed_b.at[gy], landed_b.at[gy], a_send.at[2, step], a_recv.at[2, gy], (gx, target, gz))

    def across_in(step):
        source = lax.rem(gy + ny - step, ny)
        return copy(landed_b.at[source], landed_b.at[source], a_send.at[2, step], a_recv.at[2, source], (gx, source, gz))

    def spread_out(step):
        target = lax.rem(gx + step, nx)
        return copy(total.at[gz, gx], total.at[gz, gx], a_send.at[3, step], a_recv.at[3, gx], (target, gy, gz))

    def spread_in(step):
        source = lax.rem(gx + nx - step, nx)
        return copy(total.at[gz, source], total.at[gz, source], a_send.at[3, step], a_recv.at[3, source], (source, gy, gz))

    def hand_over(step):
        source = lax.rem(gx + nx - step, nx)
        return copy(total.at[gz, source], total.at[gz, source], a_send.at[4, step], a_recv.at[4, source], (gx, gy, other))

    def hand_over_in(step):
        source = lax.rem(gx + nx - step, nx)
        return copy(total.at[other, source], total.at[other, source], a_send.at[4, step], a_recv.at[4, source], (gx, gy, other))

    def each(first, count, act):
        def body(step, carry):
            act(step)
            return carry

        lax.fori_loop(first, count, body, 0)

    def last_contributions(step, carry):
        z = place(step)
        send_adjoint(1, z, mm(v_one[...], backs[z]), adj_mid[z])
        return carry

    def last_gather(step, carry):
        z = place(step)
        await_adjoint(1, step)
        put(adjoint_here, z, gather(1, z, adj_mid[z]))
        return carry

    pair.start()
    lax.fori_loop(0, 2, last_contributions, 0)
    pair.wait_recv()
    sums[gz] = sums[gz] + landed_pair[...]
    each(1, nx, lambda step: scatter(step).start())
    lax.fori_loop(2, PLANES, last_contributions, 0)
    each(1, nx, lambda step: scatter(step).wait_recv())
    held = sums[gz, gx]
    for step in range(1, nx):
        held = held + landed_a[step]
    landed_b[gy] = held
    each(1, ny, lambda step: across(step).start())

    lax.fori_loop(0, PLANES, last_gather, 0)
    adjoint_copy = pltpu.make_async_copy(adjoint_here, adjoint_out, here_sem.at[9])
    adjoint_copy.start()

    each(1, ny, lambda step: across_in(step).wait_recv())
    held = landed_b[0]
    for step in range(1, ny):
        held = held + landed_b[step]
    total[gz, gx] = held * scale
    each(1, nx, lambda step: spread_out(step).start())
    hand_over(0).start()

    def finish_sends(z, carry):
        for e in range(2):
            sent(field_copies(e, z))
            sent(adjoint_copies(e, z))
        return carry

    lax.fori_loop(0, PLANES, finish_sends, 0)
    for e in range(2):
        sent(field_copies_low(e))
        sent(field_copies_high(e))
        sent(adjoint_copies_low(e))
        sent(adjoint_copies_high(e))
    pair.wait_send()
    each(1, nx, lambda step: scatter(step).wait_send())
    each(1, ny, lambda step: across(step).wait_send())
    final_copy.wait()
    adjoint_copy.wait()

    def pass_on(step):
        spread_in(step).wait_recv()
        hand_over(step).start()

    each(1, nx, pass_on)
    each(0, nx, lambda step: hand_over_in(step).wait_recv())

    sums_copy = pltpu.make_async_copy(total, sums_out, here_sem.at[10])
    sums_copy.start()
    each(1, nx, lambda step: spread_out(step).wait_send())
    each(0, nx, lambda step: hand_over(step).wait_send())
    sums_copy.wait()


def deliver(
    final_in,
    adjoint_in,
    sums_in,
    final_out,
    adjoint_out,
    g_in_out,
    g_second_out,
    g_third_out,
    g_readout_out,
    g_biases_out,
    g_bias_out_out,
    final_here,
    adjoint_here,
    sums_here,
    load_sem,
    store_sem,
):
    loads = [
        pltpu.make_async_copy(source, target, load_sem.at[number])
        for number, (source, target) in enumerate(
            ((sums_in, sums_here), (final_in, final_here), (adjoint_in, adjoint_here))
        )
    ]
    stores = [
        pltpu.make_async_copy(source, target, store_sem.at[number])
        for number, (source, target) in enumerate(
            (
                (final_here, final_out),
                (adjoint_here, adjoint_out),
                (sums_here.at[pl.ds(0, HID)], g_second_out),
                (sums_here.at[pl.ds(HID, HID)], g_third_out),
                (sums_here.at[pl.ds(2 * HID, 40)], g_in_out),
            )
        )
    ]
    for load in loads:
        load.start()
    loads[1].wait()
    stores[0].start()
    loads[2].wait()
    stores[1].start()
    loads[0].wait()
    for store in stores[2:]:
        store.start()
    tail = sums_here[296:304]
    g_biases_out[...] = tail[0:3]
    g_readout_out[...] = tail[4:8]
    g_bias_out_out[...] = tail[3:4, 0:FIELDS]
    for store in stores:
        store.wait()


def solution(mesh):
    sizes = (mesh.shape["gx"], mesh.shape["gy"], mesh.shape["gz"])
    nx, ny, nz = sizes
    share = SUMS // nz // nx
    cells = PLANES * 16 * LANES * nx * ny * nz
    scale = 1.0 / (time_step * math.sqrt(float(cells)))
    vmem = pl.BlockSpec(memory_space=pltpu.VMEM)
    block = jax.ShapeDtypeStruct((FIELDS, PLANES, 16, LANES), f32)
    tile = (8, LANES)
    dma = pltpu.SemaphoreType.DMA

    def buffer(*shape):
        return pltpu.VMEM(shape, f32)

    def packed(*shape):
        return pltpu.VMEM(shape, bf16)

    scratch = [
        buffer(FIELDS, PLANES, 16, LANES),
        buffer(FIELDS, PLANES, 16, LANES),
        buffer(PLANES, 16, LANES),
        packed(40, HID),
        packed(HID, HID),
        packed(HID, HID),
        packed(FIELDS, HID),
        buffer(3, HID),
        buffer(FIELDS, PLANES, 16, LANES),
        buffer(FIELDS, PLANES, 16, LANES),
        buffer(2, PLANES + 2, ROWS, LANES),
        buffer(2, PLANES, *tile),
        buffer(2, PLANES, *tile),
        buffer(2, PLANES, *tile),
        buffer(2, PLANES + 1, *tile),
        buffer(2, PLANES, *tile),
        buffer(2, PLANES, *tile),
        buffer(2, PLANES + 1, *tile),
        buffer(PLANES, ROWS, LANES),
        buffer(PLANES, ROWS, LANES),
        buffer(PLANES, ROWS, LANES),
        buffer(ROWS, LANES),
        packed(PLANES, 96, WIDE),
        packed(3, PLANES, HID, 2 * WIDE),
        packed(3, PLANES, HID, 2 * WIDE),
        packed(PLANES, 2 * HID, WIDE),
        buffer(2, PLANES + 2, STENCIL, ROWS, LANES),
        buffer(2, PLANES, *tile),
        buffer(2, PLANES, *tile),
        buffer(2, PLANES, 16, LANES),
        buffer(2, ROWS, LANES),
        buffer(2, PLANES + 1, *tile),
        buffer(2, PLANES, *tile),
        buffer(2, PLANES, *tile),
        buffer(2, PLANES + 1, 16, LANES),
        buffer(2, PLANES, *tile),
        packed(2 * HID, 96),
        packed(HID, 144),
        packed(HID, 144),
        packed(16, 2 * HID),
        packed(2 * HID, 16),
        packed(HID, HID),
        packed(HID, HID),
        packed(80, 2 * HID),
        buffer(96, 2 * HID),
        buffer(144, HID),
        buffer(144, HID),
        buffer(16, 2 * HID),
        buffer(8, LANES),
        buffer(nz, nx, share, LANES),
        buffer(nx, share, LANES),
        buffer(nx, share, LANES),
        buffer(ny, share, LANES),
        buffer(nz, nx, share, LANES),
        dma((2, 5, PLANES)),
        dma((2, 5, PLANES)),
        dma((2, 4)),
        dma((2, 4)),
        dma((2, 5, PLANES)),
        dma((2, 5, PLANES)),
        dma((2, 4)),
        dma((2, 4)),
        dma((5, max(nx, ny))),
        dma((5, max(nx, ny))),
        dma((11,)),
    ]

    shapes = (
        block,
        block,
        jax.ShapeDtypeStruct((40, HID), f32),
        jax.ShapeDtypeStruct((HID, HID), f32),
        jax.ShapeDtypeStruct((HID, HID), f32),
        jax.ShapeDtypeStruct((FIELDS, HID), f32),
        jax.ShapeDtypeStruct((3, HID), f32),
        jax.ShapeDtypeStruct((1, FIELDS), f32),
    )
    anywhere = pl.BlockSpec(memory_space=pl.ANY)

    def on_device(state, cotangent, diffusion, w_in, w_second, w_third, w_out, biases, bias_out):
        outs = pl.pallas_call(
            functools.partial(kernel, sizes, scale),
            out_shape=(block, block, jax.ShapeDtypeStruct((nz, nx, share, LANES), f32)),
            in_specs=[anywhere] * 8 + [pl.BlockSpec(memory_space=pltpu.SMEM)],
            out_specs=[anywhere] * 3,
            scratch_shapes=scratch,
            compiler_params=pltpu.CompilerParams(
                collective_id=0, has_side_effects=True, vmem_limit_bytes=60 * 2**20
            ),
            name="two_steps_and_adjoint",
        )(state, cotangent, diffusion, w_in, w_second, w_third, w_out.T, biases, bias_out)
        outs = pl.pallas_call(
            deliver,
            out_shape=shapes,
            in_specs=[anywhere] * 3,
            out_specs=[anywhere] * 5 + [vmem] * 3,
            scratch_shapes=[
                buffer(FIELDS, PLANES, 16, LANES),
                buffer(FIELDS, PLANES, 16, LANES),
                buffer(SUMS, LANES),
                dma((3,)),
                dma((5,)),
            ],
            compiler_params=pltpu.CompilerParams(vmem_limit_bytes=60 * 2**20),
            name="deliver",
        )(outs[0], outs[1], outs[2].reshape(SUMS, LANES))
        return outs[:5] + (outs[5].T, outs[6], outs[7].reshape(FIELDS))

    fields = P(None, "gz", "gy", "gx")
    placed = (fields, fields, P("gz", "gy", "gx")) + (P(),) * 6
    return jax.shard_map(
        on_device,
        mesh=mesh,
        in_specs=placed,
        out_specs=(fields, fields) + (P(),) * 6,
        check_vma=False,
    )
```

```python
import functools
import math

import jax
import jax.numpy as jnp
from jax import lax
from jax.experimental import pallas as pl
from jax.experimental.pallas import tpu as pltpu
from jax.sharding import PartitionSpec as P

bf16 = jnp.bfloat16
f32 = jnp.float32
MESH = pl.DeviceIdType.MESH

time_step = 0.1
FIELDS = 4
STENCIL = 10
PLANES = 6
ROWS = 64
LANES = 128
WIDE = 1024
HID = 128
SUMS = 384
SUBS = 2


def mm(former, latter):
    return lax.dot_general(former, latter, (((1,), (0,)), ((), ())), preferred_element_type=f32)


def mm_cells(former, latter):
    return lax.dot_general(former, latter, (((1,), (1,)), ((), ())), preferred_element_type=f32)


def lane_index(rows):
    return lax.broadcasted_iota(jnp.int32, (rows, LANES), 1)


def pack_lane(plane, lane, base, onto):
    index = lane_index(8)
    for part in range(8):
        moved = pltpu.roll(plane[8 * part : 8 * part + 8], (base + part - lane) % LANES, 1)
        onto = jnp.where(index == base + part, moved, onto)
    return onto


def unpack_lane(packed, base, lane):
    return jnp.concatenate(
        [pltpu.roll(packed, (lane - base - part) % LANES, 1) for part in range(8)], axis=0
    )


def rows_up(plane, first):
    return jnp.concatenate([first, plane[: ROWS - 4]], axis=0)


def rows_down(plane, last):
    return jnp.concatenate([plane[4:], last], axis=0)


def wide_of(plane):
    return jnp.concatenate([plane[8 * part : 8 * part + 8] for part in range(8)], axis=1)


def plane_of(wide):
    return jnp.concatenate(
        [wide[:, LANES * part : LANES * (part + 1)] for part in range(8)], axis=0
    )


def side_by_side(stacked):
    return jnp.concatenate([stacked[:HID], stacked[HID:]], axis=1)


def stacked_of(beside):
    half = beside.shape[1] // 2
    return jnp.concatenate([beside[:, :half], beside[:, half:]], axis=0)


def silu_parts(half):
    half = half.astype(bf16)
    turned = jnp.tanh(half)
    raised = 1 + turned
    value = half * raised
    slope = raised * (1 - half * turned) + value
    return value, slope


def kernel(
    sizes,
    scale,
    state_in,
    cot_in,
    diff_in,
    w_in,
    w_second,
    w_third,
    w_out,
    biases,
    bias_out,
    final_out,
    adjoint_out,
    sums_out,
    state_here,
    cot_here,
    diff_here,
    w_in_here,
    w_second_here,
    w_third_here,
    w_out_here,
    biases_here,
    st,
    p_first,
    p_last,
    x_lo,
    x_hi,
    xy_hi,
    y_lo,
    y_hi,
    spread4,
    cot,
    adj_mid,
    staged,
    feats,
    acts,
    slopes,
    backs,
    q,
    pa_last,
    pa_first,
    y_tiles,
    z_up,
    xa,
    xb,
    xya,
    ya,
    yb,
    l_one,
    l_two,
    l_three,
    l_out,
    v_out,
    v_three,
    v_two,
    v_one,
    g_one,
    g_two,
    g_three,
    g_four,
    g_last,
    sums,
    landed_pair,
    landed_a,
    landed_b,
    total,
    f_send,
    f_recv,
    f_send_z,
    f_recv_z,
    b_send,
    b_recv,
    b_send_z,
    b_recv_z,
    a_send,
    a_recv,
    here_sem,
):
    nx, ny, nz = sizes
    gx, gy, gz = lax.axis_index("gx"), lax.axis_index("gy"), lax.axis_index("gz")
    right, left = lax.rem(gx + 1, nx), lax.rem(gx + nx - 1, nx)
    above, below = lax.rem(gy + 1, ny), lax.rem(gy + ny - 1, ny)
    other = 1 - gz
    share = SUMS // nz // nx

    barrier = pltpu.get_barrier_semaphore()

    def greet(device):
        pl.semaphore_signal(barrier, inc=1, device_id=device, device_id_type=MESH)

    for device in (
        (right, above, gz),
        (left, below, gz),
        (gx, above, other),
        (gx, below, other),
        (right, gy, other),
        (left, gy, other),
        (gx, gy, other),
    ):
        greet(device)

    def greet_row(step, carry):
        greet((lax.rem(gx + step, nx), gy, gz))
        return carry

    lax.fori_loop(1, nx, greet_row, 0)

    def greet_column(step, carry):
        greet((gx, lax.rem(gy + step, ny), gz))
        return carry

    lax.fori_loop(1, ny, greet_column, 0)

    fetches = [
        pltpu.make_async_copy(source, target, here_sem.at[number])
        for number, (source, target) in enumerate(
            (
                (state_in, state_here),
                (cot_in, cot_here),
                (diff_in, diff_here),
                (w_in, w_in_here),
                (w_second, w_second_here),
                (w_third, w_third_here),
                (w_out, w_out_here),
                (biases, biases_here),
            )
        )
    ]
    for fetch in fetches:
        fetch.start()

    def copy(source, target, send, recv, device):
        return pltpu.make_async_remote_copy(
            src_ref=source,
            dst_ref=target,
            send_sem=send,
            recv_sem=recv,
            device_id=device,
            device_id_type=MESH,
        )

    def field_copies(e, z):
        send, recv = f_send, f_recv
        return (
            copy(p_last.at[e, z], x_lo.at[e, z], send.at[e, 0, z], recv.at[e, 0, z], (right, gy, gz)),
            copy(p_first.at[e, z], x_hi.at[e, z], send.at[e, 1, z], recv.at[e, 1, z], (left, gy, gz)),
            copy(p_first.at[e, z], xy_hi.at[e, z], send.at[e, 2, z], recv.at[e, 2, z], (left, below, gz)),
            copy(st.at[e, z + 1, pl.ds(56, 8)], y_lo.at[e, z], send.at[e, 3, z], recv.at[e, 3, z], (gx, above, gz)),
            copy(st.at[e, z + 1, pl.ds(0, 8)], y_hi.at[e, z], send.at[e, 4, z], recv.at[e, 4, z], (gx, below, gz)),
        )

    def field_copies_low(e):
        send, recv = f_send_z, f_recv_z
        return (
            copy(p_first.at[e, 0], x_hi.at[e, PLANES], send.at[e, 0], recv.at[e, 0], (left, gy, other)),
            copy(st.at[e, 1, pl.ds(0, 8)], y_hi.at[e, PLANES], send.at[e, 1], recv.at[e, 1], (gx, below, other)),
            copy(st.at[e, 1], st.at[e, PLANES + 1], send.at[e, 2], recv.at[e, 2], (gx, gy, other)),
        )

    def field_copies_high(e):
        return (
            copy(st.at[e, PLANES], st.at[e, 0], f_send_z.at[e, 3], f_recv_z.at[e, 3], (gx, gy, other)),
        )

    def adjoint_copies(e, z):
        send, recv = b_send, b_recv
        return (
            copy(pa_last.at[e, z], xa.at[e, z + 1], send.at[e, 0, z], recv.at[e, 0, z], (right, gy, gz)),
            copy(pa_first.at[e, z], xb.at[e, z], send.at[e, 1, z], recv.at[e, 1, z], (left, gy, gz)),
            copy(pa_last.at[e, z], xya.at[e, z], send.at[e, 2, z], recv.at[e, 2, z], (right, above, gz)),
            copy(y_tiles.at[e, z], ya.at[e, z + 1], send.at[e, 3, z], recv.at[e, 3, z], (gx, above, gz)),
            copy(q.at[e, z + 1, 4, pl.ds(0, 8)], yb.at[e, z], send.at[e, 4, z], recv.at[e, 4, z], (gx, below, gz)),
        )

    def adjoint_copies_high(e):
        send, recv = b_send_z, b_recv_z
        return (
            copy(pa_last.at[e, PLANES - 1], xa.at[e, 0], send.at[e, 0], recv.at[e, 0], (right, gy, other)),
            copy(y_tiles.at[e, PLANES - 1], ya.at[e, 0], send.at[e, 1], recv.at[e, 1], (gx, above, other)),
            copy(z_up.at[e], q.at[e, 0, 5], send.at[e, 2], recv.at[e, 2], (gx, gy, other)),
        )

    def adjoint_copies_low(e):
        return (
            copy(q.at[e, 1, 6], q.at[e, PLANES + 1, 6], b_send_z.at[e, 3], b_recv_z.at[e, 3], (gx, gy, other)),
        )

    def start(copies):
        for each in copies:
            each.start()

    def arrive(copies):
        for each in copies:
            each.wait_recv()

    def sent(copies):
        for each in copies:
            each.wait_send()

    def pack_fields(e, z):
        plane = st[e, z + 1]
        empty = jnp.zeros((8, LANES), f32)
        p_first[e, z] = pack_lane(plane, 0, 0, empty)
        p_last[e, z] = pack_lane(plane, LANES - 1, 0, empty)

    def send_fields(e, z):
        start(field_copies(e, z))

        @pl.when(z == 0)
        def _():
            start(field_copies_low(e))

        @pl.when(z == PLANES - 1)
        def _():
            start(field_copies_high(e))

    def place(step):
        odd = lax.rem(step, 2)
        half = lax.div(step, 2)
        return half + odd * (PLANES - 1 - 2 * half)

    def first_place(step):
        after = lax.max(step - 1, 0)
        odd = lax.rem(after, 2)
        half = lax.div(after, 2)
        return lax.min(step, 1) * (1 + half + odd * (PLANES - 2 - 2 * half))

    def lay_out(z, carry):
        for k in range(FIELDS):
            st[0, z + 1, pl.ds(k, 16, stride=FIELDS), :] = state_here[k, z]
        pack_fields(0, z)
        return carry

    fetches[0].wait()
    lax.fori_loop(0, PLANES, lay_out, 0)
    pl.semaphore_wait(barrier, 7 + (nx - 1) + (ny - 1))

    def first_sends(step, carry):
        send_fields(0, first_place(step))
        return carry

    lax.fori_loop(0, PLANES, first_sends, 0)

    for fetch in fetches[1:]:
        fetch.wait()

    def lay_out_rest(z, carry):
        for k in range(FIELDS):
            cot[z, pl.ds(k, 16, stride=FIELDS), :] = cot_here[k, z]
            spread4[z, pl.ds(k, 16, stride=FIELDS), :] = diff_here[z]
        return carry

    lax.fori_loop(0, PLANES, lay_out_rest, 0)
    for e in range(2):
        for j in (8, 9):
            q[e, 0, j] = jnp.zeros((ROWS, LANES), f32)

    zero4 = jnp.zeros((4, LANES), f32)
    first = w_in_here[...].astype(f32)
    parts = [first[4 * j : 4 * j + 4] for j in range(STENCIL)]
    even = jnp.concatenate([piece for part in parts for piece in (part, zero4)], axis=0)
    odd = jnp.concatenate([piece for part in parts for piece in (zero4, part)], axis=0)
    v_one[...] = jnp.concatenate([even, odd], axis=1).astype(bf16)
    bias_high = biases_here[...].astype(bf16).astype(f32)
    bias_low = biases_here[...] - bias_high

    def bias_rows(layer):
        return jnp.concatenate(
            [
                0.5 * bias_high[layer : layer + 1],
                0.5 * bias_low[layer : layer + 1],
                jnp.zeros((14, HID), f32),
            ],
            axis=0,
        )

    def turned_first(half):
        tall = jnp.concatenate([0.5 * half, bias_rows(0), jnp.zeros((32, HID), f32)], axis=0)
        return tall.T[:, :96]

    l_one[...] = jnp.concatenate([turned_first(even), turned_first(odd)], axis=0).astype(bf16)
    for layer, source, ahead, back in (
        (1, w_second_here, l_two, v_two),
        (2, w_third_here, l_three, v_three),
    ):
        matrix = 0.5 * source[...].astype(f32)
        back[...] = matrix.astype(bf16)
        tall = jnp.concatenate([bias_rows(layer), jnp.zeros((112, HID), f32)], axis=0)
        ahead[...] = jnp.concatenate([matrix.T, tall.T[:, :16]], axis=1).astype(bf16)
    turned_out = w_out_here[...].astype(f32)
    readout = jnp.concatenate([turned_out, jnp.zeros((HID - FIELDS, HID), f32)], axis=0).T
    zero8 = jnp.zeros((8, LANES), f32)
    l_out[...] = jnp.concatenate(
        [
            jnp.concatenate([turned_out, zero4, zero8], axis=0),
            jnp.concatenate([zero4, turned_out, zero8], axis=0),
        ],
        axis=1,
    ).astype(bf16)
    v_out[...] = jnp.concatenate(
        [0.5 * readout[:, :16], 0.5 * pltpu.roll(readout, FIELDS, 1)[:, :16]], axis=0
    ).astype(bf16)
    field_row = lax.rem(lax.broadcasted_iota(jnp.int32, (8, LANES), 0), FIELDS)
    bias_tile = jnp.zeros((8, LANES), f32)
    for k in range(FIELDS):
        bias_tile = jnp.where(field_row == k, bias_out[k], bias_tile)
    bias_plane = jnp.concatenate([bias_tile] * 8, axis=0)
    for each in (g_one, g_two, g_three, g_four, g_last):
        each[...] = jnp.zeros(each.shape, f32)

    lane = lane_index(ROWS)
    lane8 = lane_index(8)
    sub_width = WIDE // SUBS
    ones_rows = lax.broadcasted_iota(jnp.int32, (16, WIDE), 0)
    ones_wide = jnp.where(ones_rows < 2, 1.0, 0.0).astype(bf16)
    ones_cells = jnp.concatenate([ones_wide[:, :sub_width]] * 2, axis=1)

    def to_right(plane, e, z):
        return jnp.where(
            lane == LANES - 1, unpack_lane(x_hi[e, z], 0, LANES - 1), pltpu.roll(plane, LANES - 1, 1)
        )

    def stencil(e, z):
        here, ahead, behind = st[e, z + 1], st[e, z + 2], st[e, z]
        beyond = y_hi[e, z]
        at_right = to_right(here, e, z)
        at_left = jnp.where(lane == 0, unpack_lane(x_lo[e, z], 0, 0), pltpu.roll(here, 1, 1))
        corner = jnp.where(
            lane8 == LANES - 1,
            pltpu.roll(xy_hi[e, z], LANES - 1, 1),
            pltpu.roll(beyond, LANES - 1, 1),
        )
        return (
            here,
            at_right,
            at_left,
            rows_down(here, beyond[0:4]),
            rows_up(here, y_lo[e, z][4:8]),
            ahead,
            behind,
            rows_down(at_right, corner[0:4]),
            rows_down(ahead, y_hi[e, z + 1][0:4]),
            to_right(ahead, e, z + 1),
        )

    def arrange(points):
        rows = jnp.concatenate([wide_of(point) for point in points], axis=0)
        return jnp.concatenate([rows.astype(bf16), ones_wide], axis=0)

    def laplace(points):
        total_of = -6.0 * points[0]
        for point in points[1:7]:
            total_of = total_of + point
        return total_of

    def layers(features, values, doubled):
        value, slope = silu_parts(side_by_side(mm(l_one[...], features)))
        values.append(value)
        doubled.append(slope)
        yield
        for matrix in (l_two, l_three):
            cells = jnp.concatenate([value, ones_cells], axis=0)
            value, slope = silu_parts(mm(matrix[...], cells))
            values.append(value)
            doubled.append(slope)
            yield

    def readout_of(value):
        return mm(l_out[...], stacked_of(value))[0:8]

    def times(product, slope):
        return product.astype(bf16) * slope

    def grad_rows(adjoint):
        scaled = wide_of(time_step * adjoint)
        rounded = jnp.concatenate([scaled, jnp.zeros((8, WIDE), f32)], axis=0).astype(bf16)
        added = rounded.astype(f32)[0:8]
        for part in range(8):
            g_last[...] += added[:, LANES * part : LANES * (part + 1)]
        return rounded

    def chain(values, doubled, grad_out):
        back_three = times(side_by_side(mm(v_out[...], grad_out)), doubled[2])
        yield
        back_two = times(mm(v_three[...], back_three), doubled[1])
        yield
        back_one = stacked_of(times(mm(v_two[...], back_two), doubled[0]))
        yield
        return back_three, back_two, back_one

    def add_terms(features, values, grad_out, backs_of, order):
        for layer in order:
            if layer == 4:
                g_four[...] += mm_cells(grad_out, stacked_of(values[2]))
            elif layer == 1:
                g_one[...] += mm_cells(features, backs_of[2])
            else:
                total_of = g_three if layer == 3 else g_two
                cells = jnp.concatenate([values[layer - 2], ones_cells], axis=0)
                total_of[...] += mm_cells(cells, backs_of[3 - layer])

    def in_turn(pieces):
        results = [None] * len(pieces)
        running = list(range(len(pieces)))
        while running:
            for number in list(running):
                try:
                    next(pieces[number])
                except StopIteration as end:
                    results[number] = end.value
                    running.remove(number)
        return results

    def send_adjoint(e, z, wide, adjoint):
        spread = spread4[z] * adjoint
        for j in range(STENCIL):
            part = plane_of(wide[8 * j : 8 * j + 8])
            if j == 0:
                part = part - 6.0 * spread
            elif j < 7:
                part = part + spread
            q[e, z + 1, j] = part
        empty = jnp.zeros((8, LANES), f32)
        across = pack_lane(q[e, z + 1, 1], LANES - 1, 0, empty)
        across = pack_lane(q[e, z + 1, 9], LANES - 1, 8, across)
        pa_last[e, z] = pack_lane(q[e, z + 1, 7], LANES - 1, 16, across)
        pa_first[e, z] = pack_lane(q[e, z + 1, 2], 0, 0, empty)
        slanted = q[e, z + 1, 7, 56:64]
        slanted = jnp.where(lane8 == 0, 0.0, pltpu.roll(slanted, 1, 1))
        y_tiles[e, z, 0:8] = q[e, z + 1, 3, 56:64] + slanted
        y_tiles[e, z, 8:16] = q[e, z + 1, 8, 56:64]
        start(adjoint_copies(e, z))

        @pl.when(z == 0)
        def _():
            start(adjoint_copies_low(e))

        @pl.when(z == PLANES - 1)
        def _():
            moved = jnp.where(lane == 0, 0.0, pltpu.roll(q[e, PLANES, 9], 1, 1))
            z_up[e] = q[e, PLANES, 5] + moved + rows_up(q[e, PLANES, 8], zero4)
            start(adjoint_copies_high(e))

    def gather(e, z, adjoint):
        here = z + 1
        result = adjoint + q[e, here, 0] + q[e, z, 5] + q[e, z + 2, 6]
        from_left = q[e, here, 1] + q[e, z, 9] + rows_up(q[e, here, 7], zero4)
        packed = xa[e, here]
        direct = unpack_lane(packed + pltpu.roll(xa[e, z], LANES - 8, 1), 0, 0)
        corner = pltpu.roll(xya[e, z], LANES - 23, 1)[4:8]
        edge = direct + rows_up(unpack_lane(packed, 16, 0), corner)
        result = result + jnp.where(lane == 0, edge, pltpu.roll(from_left, 1, 1))
        result = result + jnp.where(
            lane == LANES - 1,
            unpack_lane(xb[e, z], 0, LANES - 1),
            pltpu.roll(q[e, here, 2], LANES - 1, 1),
        )
        rows_in = ya[e, here, 0:8] + ya[e, z, 8:16]
        result = result + rows_up(q[e, here, 3] + q[e, z, 8], rows_in[4:8])
        return result + rows_down(q[e, here, 4], yb[e, z][0:4])

    def await_first(step):
        @pl.when(step == 0)
        def _():
            arrive(field_copies(0, 0))
            arrive(field_copies(0, 1))
            arrive(field_copies_high(0))

        @pl.when(step == 1)
        def _():
            arrive(field_copies(0, 2))

        @pl.when(step == 2)
        def _():
            arrive(field_copies(0, 5))
            arrive(field_copies_low(0))

        @pl.when(step == 3)
        def _():
            arrive(field_copies(0, 3))

        @pl.when(step == 4)
        def _():
            arrive(field_copies(0, 4))

    def await_fields(e, step):
        @pl.when(step == 0)
        def _():
            arrive(field_copies(e, 0))
            arrive(field_copies(e, 1))
            arrive(field_copies_high(e))

        @pl.when(step == 1)
        def _():
            arrive(field_copies(e, 5))
            arrive(field_copies_low(e))

        @pl.when(step == 2)
        def _():
            arrive(field_copies(e, 2))

        @pl.when(step == 3)
        def _():
            arrive(field_copies(e, 4))

        @pl.when(step == 4)
        def _():
            arrive(field_copies(e, 3))

    def await_adjoint(e, step):
        @pl.when(step == 0)
        def _():
            arrive(adjoint_copies(e, 0))
            arrive(adjoint_copies_high(e))

        @pl.when(step == 1)
        def _():
            arrive(adjoint_copies(e, 5))
            arrive(adjoint_copies(e, 4))
            arrive(adjoint_copies_low(e))

        @pl.when(step == 2)
        def _():
            arrive(adjoint_copies(e, 1))

        @pl.when(step == 3)
        def _():
            arrive(adjoint_copies(e, 3))

        @pl.when(step == 4)
        def _():
            arrive(adjoint_copies(e, 2))

    def piece(sub):
        return slice(sub * sub_width, (sub + 1) * sub_width)

    def beside(sub):
        return slice(2 * sub * sub_width, 2 * (sub + 1) * sub_width)

    def stepped(points, z, wide):
        closed = plane_of(wide) + bias_plane
        return points[0] + spread4[z] * laplace(points) + time_step * closed

    def put(target, z, plane):
        staged[...] = plane
        for k in range(FIELDS):
            target[k, z] = staged[pl.ds(k, 16, stride=FIELDS), :]

    def first_step(step, carry):
        z = first_place(step)
        await_first(step)
        points = stencil(0, z)
        features = arrange(points)
        feats[z] = features

        def forward(sub):
            values, doubled = [], []
            for layer, _ in enumerate(layers(features[:, piece(sub)], values, doubled)):
                acts[layer, z, :, beside(sub)] = values[layer]
                slopes[layer, z, :, beside(sub)] = doubled[layer]
                yield
            return readout_of(values[2])

        outs = in_turn([forward(sub) for sub in range(SUBS)])
        st[1, z + 1] = stepped(points, z, jnp.concatenate(outs, axis=1))
        pack_fields(1, z)
        send_fields(1, z)
        return carry

    lax.fori_loop(0, PLANES, first_step, 0)

    def second_step(step, carry):
        z = place(step)
        await_fields(1, step)
        points = stencil(1, z)
        features = arrange(points)
        adjoint = cot[z]
        grad_out = grad_rows(adjoint)

        def forward(sub):
            values, doubled = [], []
            yield from layers(features[:, piece(sub)], values, doubled)
            return values, doubled, readout_of(values[2])

        passed = in_turn([forward(sub) for sub in range(SUBS)])
        put(final_out, z, stepped(points, z, jnp.concatenate([one[2] for one in passed], axis=1)))
        chains = in_turn([chain(*passed[sub][0:2], grad_out[:, piece(sub)]) for sub in range(SUBS)])
        wides = [mm(v_one[...], backs_of[2]) for backs_of in chains]
        send_adjoint(0, z, jnp.concatenate(wides, axis=1), adjoint)
        for sub in range(SUBS):
            add_terms(
                features[:, piece(sub)],
                passed[sub][0],
                grad_out[:, piece(sub)],
                chains[sub],
                (4, 3, 2, 1),
            )
        return carry

    lax.fori_loop(0, PLANES, second_step, 0)

    def first_back(step, carry):
        z = place(step)
        await_adjoint(0, step)
        adjoint = gather(0, z, cot[z])
        adj_mid[z] = adjoint
        grad_out = grad_rows(adjoint)

        values, doubled = [
            [[kept[layer, z, :, beside(sub)] for layer in range(3)] for sub in range(SUBS)]
            for kept in (acts, slopes)
        ]
        chains = in_turn(
            [chain(values[sub], doubled[sub], grad_out[:, piece(sub)]) for sub in range(SUBS)]
        )
        for sub in range(SUBS):
            backs[z, :, piece(sub)] = chains[sub][2]
            add_terms(
                feats[z, :, piece(sub)],
                values[sub],
                grad_out[:, piece(sub)],
                chains[sub],
                (1, 2, 3, 4),
            )
        return carry

    lax.fori_loop(0, PLANES, first_back, 0)

    one = g_one[...]
    merged = one[:, :HID] + jnp.concatenate([one[4:, HID:], one[:4, HID:]], axis=0)
    first_rows = jnp.concatenate([merged[8 * j : 8 * j + 4] for j in range(STENCIL)], axis=0)
    readout_rows = g_four[0:4, :HID] + g_four[4:8, HID:]
    last = jnp.sum(g_last[...], axis=1, keepdims=True)
    last = last[0:4] + last[4:8]
    row = lax.broadcasted_iota(jnp.int32, (FIELDS, LANES), 0)
    column = lax.broadcasted_iota(jnp.int32, (FIELDS, LANES), 1)
    last = jnp.sum(jnp.where(row == column, last, 0.0), axis=0, keepdims=True)
    rest = jnp.concatenate(
        [
            one[80:81, :HID] + one[80:81, HID:],
            g_two[HID : HID + 1],
            g_three[HID : HID + 1],
            last,
            readout_rows,
        ],
        axis=0,
    )
    everything = jnp.concatenate(
        [
            g_two[0:HID],
            g_three[0:HID],
            first_rows,
            rest,
            jnp.zeros((SUMS - 304, LANES), f32),
        ],
        axis=0,
    )
    sums[...] = everything.reshape(nz, nx, share, LANES)

    pair = copy(sums.at[other], landed_pair, a_send.at[0, 0], a_recv.at[0, 0], (gx, gy, other))

    def scatter(step):
        target = lax.rem(gx + step, nx)
        return copy(
            sums.at[gz, target], landed_a.at[step], a_send.at[1, step], a_recv.at[1, step], (target, gy, gz)
        )

    def across(step):
        target = lax.rem(gy + step, ny)
        return copy(landed_b.at[gy], landed_b.at[gy], a_send.at[2, step], a_recv.at[2, gy], (gx, target, gz))

    def across_in(step):
        source = lax.rem(gy + ny - step, ny)
        return copy(landed_b.at[source], landed_b.at[source], a_send.at[2, step], a_recv.at[2, source], (gx, source, gz))

    def spread_out(step):
        target = lax.rem(gx + step, nx)
        return copy(total.at[gz, gx], total.at[gz, gx], a_send.at[3, step], a_recv.at[3, gx], (target, gy, gz))

    def spread_in(step):
        source = lax.rem(gx + nx - step, nx)
        return copy(total.at[gz, source], total.at[gz, source], a_send.at[3, step], a_recv.at[3, source], (source, gy, gz))

    def hand_over(step):
        source = lax.rem(gx + nx - step, nx)
        return copy(total.at[gz, source], total.at[gz, source], a_send.at[4, step], a_recv.at[4, source], (gx, gy, other))

    def hand_over_in(step):
        source = lax.rem(gx + nx - step, nx)
        return copy(total.at[other, source], total.at[other, source], a_send.at[4, step], a_recv.at[4, source], (gx, gy, other))

    def each(first, count, act):
        def body(step, carry):
            act(step)
            return carry

        lax.fori_loop(first, count, body, 0)

    def last_contributions(step, carry):
        z = place(step)
        send_adjoint(1, z, mm(v_one[...], backs[z]), adj_mid[z])
        return carry

    def last_gather(step, carry):
        z = place(step)
        await_adjoint(1, step)
        put(adjoint_out, z, gather(1, z, adj_mid[z]))
        return carry

    pair.start()
    lax.fori_loop(0, 2, last_contributions, 0)
    pair.wait_recv()
    sums[gz] = sums[gz] + landed_pair[...]
    each(1, nx, lambda step: scatter(step).start())
    lax.fori_loop(2, PLANES, last_contributions, 0)
    each(1, nx, lambda step: scatter(step).wait_recv())
    held = sums[gz, gx]
    for step in range(1, nx):
        held = held + landed_a[step]
    landed_b[gy] = held
    each(1, ny, lambda step: across(step).start())

    lax.fori_loop(0, PLANES, last_gather, 0)

    each(1, ny, lambda step: across_in(step).wait_recv())
    held = landed_b[0]
    for step in range(1, ny):
        held = held + landed_b[step]
    total[gz, gx] = held * scale
    each(1, nx, lambda step: spread_out(step).start())
    hand_over(0).start()

    def finish_sends(z, carry):
        for e in range(2):
            sent(field_copies(e, z))
            sent(adjoint_copies(e, z))
        return carry

    lax.fori_loop(0, PLANES, finish_sends, 0)
    for e in range(2):
        sent(field_copies_low(e))
        sent(field_copies_high(e))
        sent(adjoint_copies_low(e))
        sent(adjoint_copies_high(e))
    pair.wait_send()
    each(1, nx, lambda step: scatter(step).wait_send())
    each(1, ny, lambda step: across(step).wait_send())

    def pass_on(step):
        spread_in(step).wait_recv()
        hand_over(step).start()

    each(1, nx, pass_on)
    each(0, nx, lambda step: hand_over_in(step).wait_recv())

    sums_out[...] = total[...].reshape(SUMS, LANES)
    each(1, nx, lambda step: spread_out(step).wait_send())
    each(0, nx, lambda step: hand_over(step).wait_send())


def deliver(
    final_in,
    adjoint_in,
    sums_in,
    final_out,
    adjoint_out,
    g_in_out,
    g_second_out,
    g_third_out,
    g_readout_out,
    g_biases_out,
    g_bias_out_out,
    store_sem,
):
    stores = [
        pltpu.make_async_copy(source, target, store_sem.at[number])
        for number, (source, target) in enumerate(
            (
                (final_in, final_out),
                (adjoint_in, adjoint_out),
                (sums_in.at[pl.ds(0, HID)], g_second_out),
                (sums_in.at[pl.ds(HID, HID)], g_third_out),
                (sums_in.at[pl.ds(2 * HID, 40)], g_in_out),
            )
        )
    ]
    for store in stores:
        store.start()
    tail = sums_in[296:304]
    g_biases_out[...] = tail[0:3]
    g_readout_out[...] = tail[4:8]
    g_bias_out_out[...] = tail[3:4, 0:FIELDS]
    for store in stores:
        store.wait()


def solution(mesh):
    sizes = (mesh.shape["gx"], mesh.shape["gy"], mesh.shape["gz"])
    nx, ny, nz = sizes
    share = SUMS // nz // nx
    cells = PLANES * 16 * LANES * nx * ny * nz
    scale = 1.0 / (time_step * math.sqrt(float(cells)))
    vmem = pl.BlockSpec(memory_space=pltpu.VMEM)
    block = jax.ShapeDtypeStruct((FIELDS, PLANES, 16, LANES), f32)
    tile = (8, LANES)
    dma = pltpu.SemaphoreType.DMA

    def buffer(*shape):
        return pltpu.VMEM(shape, f32)

    def packed(*shape):
        return pltpu.VMEM(shape, bf16)

    scratch = [
        buffer(FIELDS, PLANES, 16, LANES),
        buffer(FIELDS, PLANES, 16, LANES),
        buffer(PLANES, 16, LANES),
        packed(40, HID),
        packed(HID, HID),
        packed(HID, HID),
        packed(FIELDS, HID),
        buffer(3, HID),
        buffer(2, PLANES + 2, ROWS, LANES),
        buffer(2, PLANES, *tile),
        buffer(2, PLANES, *tile),
        buffer(2, PLANES, *tile),
        buffer(2, PLANES + 1, *tile),
        buffer(2, PLANES, *tile),
        buffer(2, PLANES, *tile),
        buffer(2, PLANES + 1, *tile),
        buffer(PLANES, ROWS, LANES),
        buffer(PLANES, ROWS, LANES),
        buffer(PLANES, ROWS, LANES),
        buffer(ROWS, LANES),
        packed(PLANES, 96, WIDE),
        packed(3, PLANES, HID, 2 * WIDE),
        packed(3, PLANES, HID, 2 * WIDE),
        packed(PLANES, 2 * HID, WIDE),
        buffer(2, PLANES + 2, STENCIL, ROWS, LANES),
        buffer(2, PLANES, *tile),
        buffer(2, PLANES, *tile),
        buffer(2, PLANES, 16, LANES),
        buffer(2, ROWS, LANES),
        buffer(2, PLANES + 1, *tile),
        buffer(2, PLANES, *tile),
        buffer(2, PLANES, *tile),
        buffer(2, PLANES + 1, 16, LANES),
        buffer(2, PLANES, *tile),
        packed(2 * HID, 96),
        packed(HID, 144),
        packed(HID, 144),
        packed(16, 2 * HID),
        packed(2 * HID, 16),
        packed(HID, HID),
        packed(HID, HID),
        packed(80, 2 * HID),
        buffer(96, 2 * HID),
        buffer(144, HID),
        buffer(144, HID),
        buffer(16, 2 * HID),
        buffer(8, LANES),
        buffer(nz, nx, share, LANES),
        buffer(nx, share, LANES),
        buffer(nx, share, LANES),
        buffer(ny, share, LANES),
        buffer(nz, nx, share, LANES),
        dma((2, 5, PLANES)),
        dma((2, 5, PLANES)),
        dma((2, 4)),
        dma((2, 4)),
        dma((2, 5, PLANES)),
        dma((2, 5, PLANES)),
        dma((2, 4)),
        dma((2, 4)),
        dma((5, max(nx, ny))),
        dma((5, max(nx, ny))),
        dma((11,)),
    ]

    shapes = (
        block,
        block,
        jax.ShapeDtypeStruct((40, HID), f32),
        jax.ShapeDtypeStruct((HID, HID), f32),
        jax.ShapeDtypeStruct((HID, HID), f32),
        jax.ShapeDtypeStruct((FIELDS, HID), f32),
        jax.ShapeDtypeStruct((3, HID), f32),
        jax.ShapeDtypeStruct((1, FIELDS), f32),
    )
    anywhere = pl.BlockSpec(memory_space=pl.ANY)

    def on_device(state, cotangent, diffusion, w_in, w_second, w_third, w_out, biases, bias_out):
        outs = pl.pallas_call(
            functools.partial(kernel, sizes, scale),
            out_shape=(
                buffer(FIELDS, PLANES, 16, LANES),
                buffer(FIELDS, PLANES, 16, LANES),
                buffer(SUMS, LANES),
            ),
            in_specs=[pl.BlockSpec(memory_space=pl.ANY)] * 8 + [pl.BlockSpec(memory_space=pltpu.SMEM)],
            out_specs=[vmem] * 3,
            scratch_shapes=scratch,
            compiler_params=pltpu.CompilerParams(
                collective_id=0, has_side_effects=True, vmem_limit_bytes=58 * 2**20
            ),
            name="two_steps_and_adjoint",
        )(state, cotangent, diffusion, w_in, w_second, w_third, w_out.T, biases, bias_out)
        outs = pl.pallas_call(
            deliver,
            out_shape=shapes,
            in_specs=[vmem] * 3,
            out_specs=[anywhere] * 5 + [vmem] * 3,
            scratch_shapes=[dma((5,))],
            compiler_params=pltpu.CompilerParams(vmem_limit_bytes=16 * 2**20),
            name="deliver",
        )(*outs)
        return outs[:5] + (outs[5].T, outs[6], outs[7].reshape(FIELDS))

    fields = P(None, "gz", "gy", "gx")
    placed = (fields, fields, P("gz", "gy", "gx")) + (P(),) * 6
    return jax.shard_map(
        on_device,
        mesh=mesh,
        in_specs=placed,
        out_specs=(fields, fields) + (P(),) * 6,
        check_vma=False,
    )
```

```python
import functools
import math

import jax
import jax.numpy as jnp
from jax import lax
from jax.experimental import pallas as pl
from jax.experimental.pallas import tpu as pltpu
from jax.sharding import PartitionSpec as P

bf16 = jnp.bfloat16
f32 = jnp.float32
MESH = pl.DeviceIdType.MESH

time_step = 0.1
FIELDS = 4
STENCIL = 10
PLANES = 6
ROWS = 64
LANES = 128
WIDE = 1024
HID = 128
SUMS = 384
SUBS = 4


def mm(former, latter):
    return lax.dot_general(former, latter, (((1,), (0,)), ((), ())), preferred_element_type=f32)


def mm_cells(former, latter):
    return lax.dot_general(former, latter, (((1,), (1,)), ((), ())), preferred_element_type=f32)


def lane_index(rows):
    return lax.broadcasted_iota(jnp.int32, (rows, LANES), 1)


def pack_lane(plane, lane, base, onto):
    index = lane_index(8)
    for part in range(8):
        moved = pltpu.roll(plane[8 * part : 8 * part + 8], (base + part - lane) % LANES, 1)
        onto = jnp.where(index == base + part, moved, onto)
    return onto


def unpack_lane(packed, base, lane):
    return jnp.concatenate(
        [pltpu.roll(packed, (lane - base - part) % LANES, 1) for part in range(8)], axis=0
    )


def rows_up(plane, first):
    return jnp.concatenate([first, plane[: ROWS - 4]], axis=0)


def rows_down(plane, last):
    return jnp.concatenate([plane[4:], last], axis=0)


def wide_of(plane):
    return jnp.concatenate([plane[8 * part : 8 * part + 8] for part in range(8)], axis=1)


def plane_of(wide):
    return jnp.concatenate(
        [wide[:, LANES * part : LANES * (part + 1)] for part in range(8)], axis=0
    )


def side_by_side(stacked):
    return jnp.concatenate([stacked[:HID], stacked[HID:]], axis=1)


def stacked_of(beside):
    half = beside.shape[1] // 2
    return jnp.concatenate([beside[:, :half], beside[:, half:]], axis=0)


def silu_parts(half):
    half = half.astype(bf16)
    turned = jnp.tanh(half)
    raised = 1 + turned
    value = half * raised
    slope = raised * (1 - half * turned) + value
    return value, slope


def kernel(
    sizes,
    scale,
    state_in,
    cot_in,
    diff_in,
    w_in,
    w_second,
    w_third,
    w_out,
    biases,
    bias_out,
    final_out,
    adjoint_out,
    sums_out,
    state_here,
    cot_here,
    diff_here,
    w_in_here,
    w_second_here,
    w_third_here,
    w_out_here,
    biases_here,
    st,
    p_first,
    p_last,
    x_lo,
    x_hi,
    xy_hi,
    y_lo,
    y_hi,
    spread4,
    cot,
    adj_mid,
    staged,
    feats,
    acts,
    slopes,
    backs,
    q,
    pa_last,
    pa_first,
    y_tiles,
    z_up,
    xa,
    xb,
    xya,
    ya,
    yb,
    l_one,
    l_two,
    l_three,
    l_out,
    v_out,
    v_three,
    v_two,
    v_one,
    g_one,
    g_two,
    g_three,
    g_four,
    g_last,
    sums,
    landed_pair,
    landed_a,
    landed_b,
    total,
    f_send,
    f_recv,
    f_send_z,
    f_recv_z,
    b_send,
    b_recv,
    b_send_z,
    b_recv_z,
    a_send,
    a_recv,
    here_sem,
):
    nx, ny, nz = sizes
    gx, gy, gz = lax.axis_index("gx"), lax.axis_index("gy"), lax.axis_index("gz")
    right, left = lax.rem(gx + 1, nx), lax.rem(gx + nx - 1, nx)
    above, below = lax.rem(gy + 1, ny), lax.rem(gy + ny - 1, ny)
    other = 1 - gz
    share = SUMS // nz // nx

    barrier = pltpu.get_barrier_semaphore()

    def greet(device):
        pl.semaphore_signal(barrier, inc=1, device_id=device, device_id_type=MESH)

    for device in (
        (right, above, gz),
        (left, below, gz),
        (gx, above, other),
        (gx, below, other),
        (right, gy, other),
        (left, gy, other),
        (gx, gy, other),
    ):
        greet(device)

    def greet_row(step, carry):
        greet((lax.rem(gx + step, nx), gy, gz))
        return carry

    lax.fori_loop(1, nx, greet_row, 0)

    def greet_column(step, carry):
        greet((gx, lax.rem(gy + step, ny), gz))
        return carry

    lax.fori_loop(1, ny, greet_column, 0)

    fetches = [
        pltpu.make_async_copy(source, target, here_sem.at[number])
        for number, (source, target) in enumerate(
            (
                (state_in, state_here),
                (cot_in, cot_here),
                (diff_in, diff_here),
                (w_in, w_in_here),
                (w_second, w_second_here),
                (w_third, w_third_here),
                (w_out, w_out_here),
                (biases, biases_here),
            )
        )
    ]
    for fetch in fetches:
        fetch.start()

    def copy(source, target, send, recv, device):
        return pltpu.make_async_remote_copy(
            src_ref=source,
            dst_ref=target,
            send_sem=send,
            recv_sem=recv,
            device_id=device,
            device_id_type=MESH,
        )

    def field_copies(e, z):
        send, recv = f_send, f_recv
        return (
            copy(p_last.at[e, z], x_lo.at[e, z], send.at[e, 0, z], recv.at[e, 0, z], (right, gy, gz)),
            copy(p_first.at[e, z], x_hi.at[e, z], send.at[e, 1, z], recv.at[e, 1, z], (left, gy, gz)),
            copy(p_first.at[e, z], xy_hi.at[e, z], send.at[e, 2, z], recv.at[e, 2, z], (left, below, gz)),
            copy(st.at[e, z + 1, pl.ds(56, 8)], y_lo.at[e, z], send.at[e, 3, z], recv.at[e, 3, z], (gx, above, gz)),
            copy(st.at[e, z + 1, pl.ds(0, 8)], y_hi.at[e, z], send.at[e, 4, z], recv.at[e, 4, z], (gx, below, gz)),
        )

    def field_copies_low(e):
        send, recv = f_send_z, f_recv_z
        return (
            copy(p_first.at[e, 0], x_hi.at[e, PLANES], send.at[e, 0], recv.at[e, 0], (left, gy, other)),
            copy(st.at[e, 1, pl.ds(0, 8)], y_hi.at[e, PLANES], send.at[e, 1], recv.at[e, 1], (gx, below, other)),
            copy(st.at[e, 1], st.at[e, PLANES + 1], send.at[e, 2], recv.at[e, 2], (gx, gy, other)),
        )

    def field_copies_high(e):
        return (
            copy(st.at[e, PLANES], st.at[e, 0], f_send_z.at[e, 3], f_recv_z.at[e, 3], (gx, gy, other)),
        )

    def adjoint_copies(e, z):
        send, recv = b_send, b_recv
        return (
            copy(pa_last.at[e, z], xa.at[e, z + 1], send.at[e, 0, z], recv.at[e, 0, z], (right, gy, gz)),
            copy(pa_first.at[e, z], xb.at[e, z], send.at[e, 1, z], recv.at[e, 1, z], (left, gy, gz)),
            copy(pa_last.at[e, z], xya.at[e, z], send.at[e, 2, z], recv.at[e, 2, z], (right, above, gz)),
            copy(y_tiles.at[e, z], ya.at[e, z + 1], send.at[e, 3, z], recv.at[e, 3, z], (gx, above, gz)),
            copy(q.at[e, z + 1, 4, pl.ds(0, 8)], yb.at[e, z], send.at[e, 4, z], recv.at[e, 4, z], (gx, below, gz)),
        )

    def adjoint_copies_high(e):
        send, recv = b_send_z, b_recv_z
        return (
            copy(pa_last.at[e, PLANES - 1], xa.at[e, 0], send.at[e, 0], recv.at[e, 0], (right, gy, other)),
            copy(y_tiles.at[e, PLANES - 1], ya.at[e, 0], send.at[e, 1], recv.at[e, 1], (gx, above, other)),
            copy(z_up.at[e], q.at[e, 0, 5], send.at[e, 2], recv.at[e, 2], (gx, gy, other)),
        )

    def adjoint_copies_low(e):
        return (
            copy(q.at[e, 1, 6], q.at[e, PLANES + 1, 6], b_send_z.at[e, 3], b_recv_z.at[e, 3], (gx, gy, other)),
        )

    def start(copies):
        for each in copies:
            each.start()

    def arrive(copies):
        for each in copies:
            each.wait_recv()

    def sent(copies):
        for each in copies:
            each.wait_send()

    def pack_fields(e, z):
        plane = st[e, z + 1]
        empty = jnp.zeros((8, LANES), f32)
        p_first[e, z] = pack_lane(plane, 0, 0, empty)
        p_last[e, z] = pack_lane(plane, LANES - 1, 0, empty)

    def send_fields(e, z):
        start(field_copies(e, z))

        @pl.when(z == 0)
        def _():
            start(field_copies_low(e))

        @pl.when(z == PLANES - 1)
        def _():
            start(field_copies_high(e))

    def place(step):
        odd = lax.rem(step, 2)
        half = lax.div(step, 2)
        return half + odd * (PLANES - 1 - 2 * half)

    def first_place(step):
        after = lax.max(step - 1, 0)
        odd = lax.rem(after, 2)
        half = lax.div(after, 2)
        return lax.min(step, 1) * (1 + half + odd * (PLANES - 2 - 2 * half))

    def lay_out(z, carry):
        for k in range(FIELDS):
            st[0, z + 1, pl.ds(k, 16, stride=FIELDS), :] = state_here[k, z]
        pack_fields(0, z)
        return carry

    fetches[0].wait()
    lax.fori_loop(0, PLANES, lay_out, 0)
    pl.semaphore_wait(barrier, 7 + (nx - 1) + (ny - 1))

    def first_sends(step, carry):
        send_fields(0, first_place(step))
        return carry

    lax.fori_loop(0, PLANES, first_sends, 0)

    for fetch in fetches[1:]:
        fetch.wait()

    def lay_out_rest(z, carry):
        for k in range(FIELDS):
            cot[z, pl.ds(k, 16, stride=FIELDS), :] = cot_here[k, z]
            spread4[z, pl.ds(k, 16, stride=FIELDS), :] = diff_here[z]
        return carry

    lax.fori_loop(0, PLANES, lay_out_rest, 0)
    for e in range(2):
        for j in (8, 9):
            q[e, 0, j] = jnp.zeros((ROWS, LANES), f32)

    zero4 = jnp.zeros((4, LANES), f32)
    first = w_in_here[...].astype(f32)
    parts = [first[4 * j : 4 * j + 4] for j in range(STENCIL)]
    even = jnp.concatenate([piece for part in parts for piece in (part, zero4)], axis=0)
    odd = jnp.concatenate([piece for part in parts for piece in (zero4, part)], axis=0)
    v_one[...] = jnp.concatenate([even, odd], axis=1).astype(bf16)
    bias_high = biases_here[...].astype(bf16).astype(f32)
    bias_low = biases_here[...] - bias_high

    def bias_rows(layer):
        return jnp.concatenate(
            [
                0.5 * bias_high[layer : layer + 1],
                0.5 * bias_low[layer : layer + 1],
                jnp.zeros((14, HID), f32),
            ],
            axis=0,
        )

    def turned_first(half):
        tall = jnp.concatenate([0.5 * half, bias_rows(0), jnp.zeros((32, HID), f32)], axis=0)
        return tall.T[:, :96]

    l_one[...] = jnp.concatenate([turned_first(even), turned_first(odd)], axis=0).astype(bf16)
    for layer, source, ahead, back in (
        (1, w_second_here, l_two, v_two),
        (2, w_third_here, l_three, v_three),
    ):
        matrix = 0.5 * source[...].astype(f32)
        back[...] = matrix.astype(bf16)
        tall = jnp.concatenate([bias_rows(layer), jnp.zeros((112, HID), f32)], axis=0)
        ahead[...] = jnp.concatenate([matrix.T, tall.T[:, :16]], axis=1).astype(bf16)
    turned_out = w_out_here[...].astype(f32)
    readout = jnp.concatenate([turned_out, jnp.zeros((HID - FIELDS, HID), f32)], axis=0).T
    zero8 = jnp.zeros((8, LANES), f32)
    l_out[...] = jnp.concatenate(
        [
            jnp.concatenate([turned_out, zero4, zero8], axis=0),
            jnp.concatenate([zero4, turned_out, zero8], axis=0),
        ],
        axis=1,
    ).astype(bf16)
    v_out[...] = jnp.concatenate(
        [0.5 * readout[:, :16], 0.5 * pltpu.roll(readout, FIELDS, 1)[:, :16]], axis=0
    ).astype(bf16)
    field_row = lax.rem(lax.broadcasted_iota(jnp.int32, (8, LANES), 0), FIELDS)
    bias_tile = jnp.zeros((8, LANES), f32)
    for k in range(FIELDS):
        bias_tile = jnp.where(field_row == k, bias_out[k], bias_tile)
    bias_plane = jnp.concatenate([bias_tile] * 8, axis=0)
    for each in (g_one, g_two, g_three, g_four, g_last):
        each[...] = jnp.zeros(each.shape, f32)

    lane = lane_index(ROWS)
    lane8 = lane_index(8)
    sub_width = WIDE // SUBS
    ones_rows = lax.broadcasted_iota(jnp.int32, (16, WIDE), 0)
    ones_wide = jnp.where(ones_rows < 2, 1.0, 0.0).astype(bf16)
    ones_cells = jnp.concatenate([ones_wide[:, :sub_width]] * 2, axis=1)

    def to_right(plane, e, z):
        return jnp.where(
            lane == LANES - 1, unpack_lane(x_hi[e, z], 0, LANES - 1), pltpu.roll(plane, LANES - 1, 1)
        )

    def stencil(e, z):
        here, ahead, behind = st[e, z + 1], st[e, z + 2], st[e, z]
        beyond = y_hi[e, z]
        at_right = to_right(here, e, z)
        at_left = jnp.where(lane == 0, unpack_lane(x_lo[e, z], 0, 0), pltpu.roll(here, 1, 1))
        corner = jnp.where(
            lane8 == LANES - 1,
            pltpu.roll(xy_hi[e, z], LANES - 1, 1),
            pltpu.roll(beyond, LANES - 1, 1),
        )
        return (
            here,
            at_right,
            at_left,
            rows_down(here, beyond[0:4]),
            rows_up(here, y_lo[e, z][4:8]),
            ahead,
            behind,
            rows_down(at_right, corner[0:4]),
            rows_down(ahead, y_hi[e, z + 1][0:4]),
            to_right(ahead, e, z + 1),
        )

    def arrange(points):
        rows = jnp.concatenate([wide_of(point) for point in points], axis=0)
        return jnp.concatenate([rows.astype(bf16), ones_wide], axis=0)

    def laplace(points):
        total_of = -6.0 * points[0]
        for point in points[1:7]:
            total_of = total_of + point
        return total_of

    def layers(features, values, doubled):
        value, slope = silu_parts(side_by_side(mm(l_one[...], features)))
        values.append(value)
        doubled.append(slope)
        yield
        for matrix in (l_two, l_three):
            cells = jnp.concatenate([value, ones_cells], axis=0)
            value, slope = silu_parts(mm(matrix[...], cells))
            values.append(value)
            doubled.append(slope)
            yield

    def readout_of(value):
        return mm(l_out[...], stacked_of(value))[0:8]

    def times(product, slope):
        return product.astype(bf16) * slope

    def grad_rows(adjoint):
        scaled = wide_of(time_step * adjoint)
        rounded = jnp.concatenate([scaled, jnp.zeros((8, WIDE), f32)], axis=0).astype(bf16)
        added = rounded.astype(f32)[0:8]
        for part in range(8):
            g_last[...] += added[:, LANES * part : LANES * (part + 1)]
        return rounded

    def backward(features, values, doubled, grad_out, to_features):
        back_three = times(side_by_side(mm(v_out[...], grad_out)), doubled[2])
        yield
        back_two = times(mm(v_three[...], back_three), doubled[1])
        yield
        g_four[...] += mm_cells(grad_out, stacked_of(values[2]))
        back_one = stacked_of(times(mm(v_two[...], back_two), doubled[0]))
        yield
        g_three[...] += mm_cells(jnp.concatenate([values[1], ones_cells], axis=0), back_three)
        result = mm(v_one[...], back_one) if to_features else back_one
        yield
        g_two[...] += mm_cells(jnp.concatenate([values[0], ones_cells], axis=0), back_two)
        yield
        g_one[...] += mm_cells(features, back_one)
        return result

    def in_turn(pieces):
        results = [None] * len(pieces)
        running = list(range(len(pieces)))
        while running:
            for number in list(running):
                try:
                    next(pieces[number])
                except StopIteration as end:
                    results[number] = end.value
                    running.remove(number)
        return results

    def send_adjoint(e, z, wide, adjoint):
        spread = spread4[z] * adjoint
        for j in range(STENCIL):
            part = plane_of(wide[8 * j : 8 * j + 8])
            if j == 0:
                part = part - 6.0 * spread
            elif j < 7:
                part = part + spread
            q[e, z + 1, j] = part
        empty = jnp.zeros((8, LANES), f32)
        across = pack_lane(q[e, z + 1, 1], LANES - 1, 0, empty)
        across = pack_lane(q[e, z + 1, 9], LANES - 1, 8, across)
        pa_last[e, z] = pack_lane(q[e, z + 1, 7], LANES - 1, 16, across)
        pa_first[e, z] = pack_lane(q[e, z + 1, 2], 0, 0, empty)
        slanted = q[e, z + 1, 7, 56:64]
        slanted = jnp.where(lane8 == 0, 0.0, pltpu.roll(slanted, 1, 1))
        y_tiles[e, z, 0:8] = q[e, z + 1, 3, 56:64] + slanted
        y_tiles[e, z, 8:16] = q[e, z + 1, 8, 56:64]
        start(adjoint_copies(e, z))

        @pl.when(z == 0)
        def _():
            start(adjoint_copies_low(e))

        @pl.when(z == PLANES - 1)
        def _():
            moved = jnp.where(lane == 0, 0.0, pltpu.roll(q[e, PLANES, 9], 1, 1))
            z_up[e] = q[e, PLANES, 5] + moved + rows_up(q[e, PLANES, 8], zero4)
            start(adjoint_copies_high(e))

    def gather(e, z, adjoint):
        here = z + 1
        result = adjoint + q[e, here, 0] + q[e, z, 5] + q[e, z + 2, 6]
        from_left = q[e, here, 1] + q[e, z, 9] + rows_up(q[e, here, 7], zero4)
        packed = xa[e, here]
        direct = unpack_lane(packed + pltpu.roll(xa[e, z], LANES - 8, 1), 0, 0)
        corner = pltpu.roll(xya[e, z], LANES - 23, 1)[4:8]
        edge = direct + rows_up(unpack_lane(packed, 16, 0), corner)
        result = result + jnp.where(lane == 0, edge, pltpu.roll(from_left, 1, 1))
        result = result + jnp.where(
            lane == LANES - 1,
            unpack_lane(xb[e, z], 0, LANES - 1),
            pltpu.roll(q[e, here, 2], LANES - 1, 1),
        )
        rows_in = ya[e, here, 0:8] + ya[e, z, 8:16]
        result = result + rows_up(q[e, here, 3] + q[e, z, 8], rows_in[4:8])
        return result + rows_down(q[e, here, 4], yb[e, z][0:4])

    def await_first(step):
        @pl.when(step == 0)
        def _():
            arrive(field_copies(0, 0))
            arrive(field_copies(0, 1))
            arrive(field_copies_high(0))

        @pl.when(step == 1)
        def _():
            arrive(field_copies(0, 2))

        @pl.when(step == 2)
        def _():
            arrive(field_copies(0, 5))
            arrive(field_copies_low(0))

        @pl.when(step == 3)
        def _():
            arrive(field_copies(0, 3))

        @pl.when(step == 4)
        def _():
            arrive(field_copies(0, 4))

    def await_fields(e, step):
        @pl.when(step == 0)
        def _():
            arrive(field_copies(e, 0))
            arrive(field_copies(e, 1))
            arrive(field_copies_high(e))

        @pl.when(step == 1)
        def _():
            arrive(field_copies(e, 5))
            arrive(field_copies_low(e))

        @pl.when(step == 2)
        def _():
            arrive(field_copies(e, 2))

        @pl.when(step == 3)
        def _():
            arrive(field_copies(e, 4))

        @pl.when(step == 4)
        def _():
            arrive(field_copies(e, 3))

    def await_adjoint(e, step):
        @pl.when(step == 0)
        def _():
            arrive(adjoint_copies(e, 0))
            arrive(adjoint_copies_high(e))

        @pl.when(step == 1)
        def _():
            arrive(adjoint_copies(e, 1))

        @pl.when(step == 2)
        def _():
            arrive(adjoint_copies(e, 5))
            arrive(adjoint_copies(e, 4))
            arrive(adjoint_copies_low(e))

        @pl.when(step == 3)
        def _():
            arrive(adjoint_copies(e, 2))

        @pl.when(step == 4)
        def _():
            arrive(adjoint_copies(e, 3))

    def piece(sub):
        return slice(sub * sub_width, (sub + 1) * sub_width)

    def beside(sub):
        return slice(2 * sub * sub_width, 2 * (sub + 1) * sub_width)

    def stepped(points, z, wide):
        closed = plane_of(wide) + bias_plane
        return points[0] + spread4[z] * laplace(points) + time_step * closed

    def put(target, z, plane):
        staged[...] = plane
        for k in range(FIELDS):
            target[k, z] = staged[pl.ds(k, 16, stride=FIELDS), :]

    def first_step(step, carry):
        z = first_place(step)
        await_first(step)
        points = stencil(0, z)
        features = arrange(points)
        feats[z] = features

        def forward(sub):
            values, doubled = [], []
            for layer, _ in enumerate(layers(features[:, piece(sub)], values, doubled)):
                acts[layer, z, :, beside(sub)] = values[layer]
                slopes[layer, z, :, beside(sub)] = doubled[layer]
                yield
            return readout_of(values[2])

        outs = in_turn([forward(sub) for sub in range(SUBS)])
        st[1, z + 1] = stepped(points, z, jnp.concatenate(outs, axis=1))
        pack_fields(1, z)
        send_fields(1, z)
        return carry

    lax.fori_loop(0, PLANES, first_step, 0)

    def second_step(step, carry):
        z = place(step)
        await_fields(1, step)
        points = stencil(1, z)
        features = arrange(points)
        adjoint = cot[z]
        grad_out = grad_rows(adjoint)

        def forward(sub):
            values, doubled = [], []
            yield from layers(features[:, piece(sub)], values, doubled)
            return values, doubled, readout_of(values[2])

        passed = in_turn([forward(sub) for sub in range(SUBS)])
        put(final_out, z, stepped(points, z, jnp.concatenate([one[2] for one in passed], axis=1)))
        wides = in_turn(
            [
                backward(features[:, piece(sub)], *passed[sub][0:2], grad_out[:, piece(sub)], True)
                for sub in range(SUBS)
            ]
        )
        send_adjoint(0, z, jnp.concatenate(wides, axis=1), adjoint)
        return carry

    lax.fori_loop(0, PLANES, second_step, 0)

    def first_back(step, carry):
        z = first_place(step)
        await_adjoint(0, step)
        adjoint = gather(0, z, cot[z])
        adj_mid[z] = adjoint
        grad_out = grad_rows(adjoint)

        def back(sub):
            values = [acts[layer, z, :, beside(sub)] for layer in range(3)]
            doubled = [slopes[layer, z, :, beside(sub)] for layer in range(3)]
            return backward(
                feats[z, :, piece(sub)], values, doubled, grad_out[:, piece(sub)], False
            )

        for sub, back_one in enumerate(in_turn([back(sub) for sub in range(SUBS)])):
            backs[z, :, piece(sub)] = back_one
        return carry

    lax.fori_loop(0, PLANES, first_back, 0)

    one = g_one[...]
    merged = one[:, :HID] + jnp.concatenate([one[4:, HID:], one[:4, HID:]], axis=0)
    first_rows = jnp.concatenate([merged[8 * j : 8 * j + 4] for j in range(STENCIL)], axis=0)
    readout_rows = g_four[0:4, :HID] + g_four[4:8, HID:]
    last = jnp.sum(g_last[...], axis=1, keepdims=True)
    last = last[0:4] + last[4:8]
    row = lax.broadcasted_iota(jnp.int32, (FIELDS, LANES), 0)
    column = lax.broadcasted_iota(jnp.int32, (FIELDS, LANES), 1)
    last = jnp.sum(jnp.where(row == column, last, 0.0), axis=0, keepdims=True)
    rest = jnp.concatenate(
        [
            one[80:81, :HID] + one[80:81, HID:],
            g_two[HID : HID + 1],
            g_three[HID : HID + 1],
            last,
            readout_rows,
        ],
        axis=0,
    )
    everything = jnp.concatenate(
        [
            g_two[0:HID],
            g_three[0:HID],
            first_rows,
            rest,
            jnp.zeros((SUMS - 304, LANES), f32),
        ],
        axis=0,
    )
    sums[...] = everything.reshape(nz, nx, share, LANES)

    pair = copy(sums.at[other], landed_pair, a_send.at[0, 0], a_recv.at[0, 0], (gx, gy, other))

    def scatter(step):
        target = lax.rem(gx + step, nx)
        return copy(
            sums.at[gz, target], landed_a.at[step], a_send.at[1, step], a_recv.at[1, step], (target, gy, gz)
        )

    def across(step):
        target = lax.rem(gy + step, ny)
        return copy(landed_b.at[gy], landed_b.at[gy], a_send.at[2, step], a_recv.at[2, gy], (gx, target, gz))

    def across_in(step):
        source = lax.rem(gy + ny - step, ny)
        return copy(landed_b.at[source], landed_b.at[source], a_send.at[2, step], a_recv.at[2, source], (gx, source, gz))

    def spread_out(step):
        target = lax.rem(gx + step, nx)
        return copy(total.at[gz, gx], total.at[gz, gx], a_send.at[3, step], a_recv.at[3, gx], (target, gy, gz))

    def spread_in(step):
        source = lax.rem(gx + nx - step, nx)
        return copy(total.at[gz, source], total.at[gz, source], a_send.at[3, step], a_recv.at[3, source], (source, gy, gz))

    def hand_over(step):
        source = lax.rem(gx + nx - step, nx)
        return copy(total.at[gz, source], total.at[gz, source], a_send.at[4, step], a_recv.at[4, source], (gx, gy, other))

    def hand_over_in(step):
        source = lax.rem(gx + nx - step, nx)
        return copy(total.at[other, source], total.at[other, source], a_send.at[4, step], a_recv.at[4, source], (gx, gy, other))

    def each(first, count, act):
        def body(step, carry):
            act(step)
            return carry

        lax.fori_loop(first, count, body, 0)

    def last_contributions(step, carry):
        z = place(step)
        send_adjoint(1, z, mm(v_one[...], backs[z]), adj_mid[z])
        return carry

    def last_gather(step, carry):
        z = first_place(step)
        await_adjoint(1, step)
        put(adjoint_out, z, gather(1, z, adj_mid[z]))
        return carry

    pair.start()
    lax.fori_loop(0, 2, last_contributions, 0)
    pair.wait_recv()
    sums[gz] = sums[gz] + landed_pair[...]
    each(1, nx, lambda step: scatter(step).start())
    lax.fori_loop(2, PLANES, last_contributions, 0)
    each(1, nx, lambda step: scatter(step).wait_recv())
    held = sums[gz, gx]
    for step in range(1, nx):
        held = held + landed_a[step]
    landed_b[gy] = held
    each(1, ny, lambda step: across(step).start())

    lax.fori_loop(0, PLANES, last_gather, 0)

    each(1, ny, lambda step: across_in(step).wait_recv())
    held = landed_b[0]
    for step in range(1, ny):
        held = held + landed_b[step]
    total[gz, gx] = held * scale
    each(1, nx, lambda step: spread_out(step).start())
    hand_over(0).start()

    def finish_sends(z, carry):
        for e in range(2):
            sent(field_copies(e, z))
            sent(adjoint_copies(e, z))
        return carry

    lax.fori_loop(0, PLANES, finish_sends, 0)
    for e in range(2):
        sent(field_copies_low(e))
        sent(field_copies_high(e))
        sent(adjoint_copies_low(e))
        sent(adjoint_copies_high(e))
    pair.wait_send()
    each(1, nx, lambda step: scatter(step).wait_send())
    each(1, ny, lambda step: across(step).wait_send())

    def pass_on(step):
        spread_in(step).wait_recv()
        hand_over(step).start()

    each(1, nx, pass_on)
    each(0, nx, lambda step: hand_over_in(step).wait_recv())

    sums_out[...] = total[...].reshape(SUMS, LANES)
    each(1, nx, lambda step: spread_out(step).wait_send())
    each(0, nx, lambda step: hand_over(step).wait_send())


def deliver(
    final_in,
    adjoint_in,
    sums_in,
    final_out,
    adjoint_out,
    g_in_out,
    g_second_out,
    g_third_out,
    g_readout_out,
    g_biases_out,
    g_bias_out_out,
    store_sem,
):
    stores = [
        pltpu.make_async_copy(source, target, store_sem.at[number])
        for number, (source, target) in enumerate(
            (
                (final_in, final_out),
                (adjoint_in, adjoint_out),
                (sums_in.at[pl.ds(0, HID)], g_second_out),
                (sums_in.at[pl.ds(HID, HID)], g_third_out),
                (sums_in.at[pl.ds(2 * HID, 40)], g_in_out),
            )
        )
    ]
    for store in stores:
        store.start()
    tail = sums_in[296:304]
    g_biases_out[...] = tail[0:3]
    g_readout_out[...] = tail[4:8]
    g_bias_out_out[...] = tail[3:4, 0:FIELDS]
    for store in stores:
        store.wait()


def solution(mesh):
    sizes = (mesh.shape["gx"], mesh.shape["gy"], mesh.shape["gz"])
    nx, ny, nz = sizes
    share = SUMS // nz // nx
    cells = PLANES * 16 * LANES * nx * ny * nz
    scale = 1.0 / (time_step * math.sqrt(float(cells)))
    vmem = pl.BlockSpec(memory_space=pltpu.VMEM)
    block = jax.ShapeDtypeStruct((FIELDS, PLANES, 16, LANES), f32)
    tile = (8, LANES)
    dma = pltpu.SemaphoreType.DMA

    def buffer(*shape):
        return pltpu.VMEM(shape, f32)

    def packed(*shape):
        return pltpu.VMEM(shape, bf16)

    scratch = [
        buffer(FIELDS, PLANES, 16, LANES),
        buffer(FIELDS, PLANES, 16, LANES),
        buffer(PLANES, 16, LANES),
        packed(40, HID),
        packed(HID, HID),
        packed(HID, HID),
        packed(FIELDS, HID),
        buffer(3, HID),
        buffer(2, PLANES + 2, ROWS, LANES),
        buffer(2, PLANES, *tile),
        buffer(2, PLANES, *tile),
        buffer(2, PLANES, *tile),
        buffer(2, PLANES + 1, *tile),
        buffer(2, PLANES, *tile),
        buffer(2, PLANES, *tile),
        buffer(2, PLANES + 1, *tile),
        buffer(PLANES, ROWS, LANES),
        buffer(PLANES, ROWS, LANES),
        buffer(PLANES, ROWS, LANES),
        buffer(ROWS, LANES),
        packed(PLANES, 96, WIDE),
        packed(3, PLANES, HID, 2 * WIDE),
        packed(3, PLANES, HID, 2 * WIDE),
        packed(PLANES, 2 * HID, WIDE),
        buffer(2, PLANES + 2, STENCIL, ROWS, LANES),
        buffer(2, PLANES, *tile),
        buffer(2, PLANES, *tile),
        buffer(2, PLANES, 16, LANES),
        buffer(2, ROWS, LANES),
        buffer(2, PLANES + 1, *tile),
        buffer(2, PLANES, *tile),
        buffer(2, PLANES, *tile),
        buffer(2, PLANES + 1, 16, LANES),
        buffer(2, PLANES, *tile),
        packed(2 * HID, 96),
        packed(HID, 144),
        packed(HID, 144),
        packed(16, 2 * HID),
        packed(2 * HID, 16),
        packed(HID, HID),
        packed(HID, HID),
        packed(80, 2 * HID),
        buffer(96, 2 * HID),
        buffer(144, HID),
        buffer(144, HID),
        buffer(16, 2 * HID),
        buffer(8, LANES),
        buffer(nz, nx, share, LANES),
        buffer(nx, share, LANES),
        buffer(nx, share, LANES),
        buffer(ny, share, LANES),
        buffer(nz, nx, share, LANES),
        dma((2, 5, PLANES)),
        dma((2, 5, PLANES)),
        dma((2, 4)),
        dma((2, 4)),
        dma((2, 5, PLANES)),
        dma((2, 5, PLANES)),
        dma((2, 4)),
        dma((2, 4)),
        dma((5, max(nx, ny))),
        dma((5, max(nx, ny))),
        dma((11,)),
    ]

    shapes = (
        block,
        block,
        jax.ShapeDtypeStruct((40, HID), f32),
        jax.ShapeDtypeStruct((HID, HID), f32),
        jax.ShapeDtypeStruct((HID, HID), f32),
        jax.ShapeDtypeStruct((FIELDS, HID), f32),
        jax.ShapeDtypeStruct((3, HID), f32),
        jax.ShapeDtypeStruct((1, FIELDS), f32),
    )
    anywhere = pl.BlockSpec(memory_space=pl.ANY)

    def on_device(state, cotangent, diffusion, w_in, w_second, w_third, w_out, biases, bias_out):
        outs = pl.pallas_call(
            functools.partial(kernel, sizes, scale),
            out_shape=(
                buffer(FIELDS, PLANES, 16, LANES),
                buffer(FIELDS, PLANES, 16, LANES),
                buffer(SUMS, LANES),
            ),
            in_specs=[pl.BlockSpec(memory_space=pl.ANY)] * 8 + [pl.BlockSpec(memory_space=pltpu.SMEM)],
            out_specs=[vmem] * 3,
            scratch_shapes=scratch,
            compiler_params=pltpu.CompilerParams(
                collective_id=0, has_side_effects=True, vmem_limit_bytes=58 * 2**20
            ),
            name="two_steps_and_adjoint",
        )(state, cotangent, diffusion, w_in, w_second, w_third, w_out.T, biases, bias_out)
        outs = pl.pallas_call(
            deliver,
            out_shape=shapes,
            in_specs=[vmem] * 3,
            out_specs=[anywhere] * 5 + [vmem] * 3,
            scratch_shapes=[dma((5,))],
            compiler_params=pltpu.CompilerParams(vmem_limit_bytes=16 * 2**20),
            name="deliver",
        )(*outs)
        return outs[:5] + (outs[5].T, outs[6], outs[7].reshape(FIELDS))

    fields = P(None, "gz", "gy", "gx")
    placed = (fields, fields, P("gz", "gy", "gx")) + (P(),) * 6
    return jax.shard_map(
        on_device,
        mesh=mesh,
        in_specs=placed,
        out_specs=(fields, fields) + (P(),) * 6,
        check_vma=False,
    )
```

```python
import functools
import math

import jax
import jax.numpy as jnp
from jax import lax
from jax.experimental import pallas as pl
from jax.experimental.pallas import tpu as pltpu
from jax.sharding import PartitionSpec as P

bf16 = jnp.bfloat16
f32 = jnp.float32
MESH = pl.DeviceIdType.MESH

time_step = 0.1
FIELDS = 4
STENCIL = 10
PLANES = 6
ROWS = 64
LANES = 128
WIDE = 1024
HID = 128
FIRST_SUMS = 192
SUMS = FIRST_SUMS + 128
SUBS = 4


def mm(former, latter):
    return lax.dot_general(former, latter, (((1,), (0,)), ((), ())), preferred_element_type=f32)


def mm_cells(former, latter):
    return lax.dot_general(former, latter, (((1,), (1,)), ((), ())), preferred_element_type=f32)


def lane_index(rows):
    return lax.broadcasted_iota(jnp.int32, (rows, LANES), 1)


def pack_lane(plane, lane, base, onto):
    index = lane_index(8)
    for part in range(8):
        moved = pltpu.roll(plane[8 * part : 8 * part + 8], (base + part - lane) % LANES, 1)
        onto = jnp.where(index == base + part, moved, onto)
    return onto


def unpack_lane(packed, base, lane):
    return jnp.concatenate(
        [pltpu.roll(packed, (lane - base - part) % LANES, 1) for part in range(8)], axis=0
    )


def rows_up(plane, first):
    return jnp.concatenate([first, plane[: ROWS - 4]], axis=0)


def rows_down(plane, last):
    return jnp.concatenate([plane[4:], last], axis=0)


def wide_of(plane):
    return jnp.concatenate([plane[8 * part : 8 * part + 8] for part in range(8)], axis=1)


def plane_of(wide):
    return jnp.concatenate(
        [wide[:, LANES * part : LANES * (part + 1)] for part in range(8)], axis=0
    )


def side_by_side(stacked):
    return jnp.concatenate([stacked[:HID], stacked[HID:]], axis=1)


def stacked_of(beside):
    half = beside.shape[1] // 2
    return jnp.concatenate([beside[:, :half], beside[:, half:]], axis=0)


def silu_parts(half):
    half = half.astype(bf16)
    turned = jnp.tanh(half)
    raised = 1 + turned
    value = half * raised
    slope = raised * (1 - half * turned) + value
    return value, slope


def kernel(
    sizes,
    scale,
    state_in,
    cot_in,
    diff_in,
    w_in,
    w_second,
    w_third,
    w_out,
    biases,
    bias_out,
    final_out,
    adjoint_out,
    sums_out,
    state_here,
    cot_here,
    diff_here,
    w_in_here,
    w_second_here,
    w_third_here,
    w_out_here,
    biases_here,
    st,
    p_first,
    p_last,
    x_lo,
    x_hi,
    xy_hi,
    y_lo,
    y_hi,
    spread4,
    cot,
    adj_mid,
    staged,
    feats,
    acts,
    slopes,
    backs,
    q,
    pa_last,
    pa_first,
    y_tiles,
    z_up,
    xa,
    xb,
    xya,
    ya,
    yb,
    l_one,
    l_two,
    l_three,
    l_out,
    v_out,
    v_three,
    v_two,
    v_one,
    g_one,
    g_two,
    g_three,
    g_four,
    g_last,
    sums,
    landed_pair,
    landed_a,
    landed_b,
    total,
    f_send,
    f_recv,
    f_send_z,
    f_recv_z,
    b_send,
    b_recv,
    b_send_z,
    b_recv_z,
    a_send,
    a_recv,
    here_sem,
):
    nx, ny, nz = sizes
    gx, gy, gz = lax.axis_index("gx"), lax.axis_index("gy"), lax.axis_index("gz")
    right, left = lax.rem(gx + 1, nx), lax.rem(gx + nx - 1, nx)
    above, below = lax.rem(gy + 1, ny), lax.rem(gy + ny - 1, ny)
    other = 1 - gz
    share = FIRST_SUMS // nx
    shares = (share, HID // nx)

    barrier = pltpu.get_barrier_semaphore()

    def greet(device):
        pl.semaphore_signal(barrier, inc=1, device_id=device, device_id_type=MESH)

    for device in (
        (gx, above, gz),
        (gx, below, gz),
        (right, above, gz),
        (left, below, gz),
        (right, gy, gz),
        (left, gy, gz),
        (gx, above, other),
        (gx, below, other),
        (right, gy, other),
        (left, gy, other),
        (gx, gy, other),
    ):
        greet(device)

    def greet_row(step, carry):
        greet((lax.rem(gx + step, nx), gy, gz))
        return carry

    lax.fori_loop(2, max(nx - 1, 2), greet_row, 0)

    def greet_column(step, carry):
        greet((gx, lax.rem(gy + step, ny), gz))
        return carry

    lax.fori_loop(2, max(ny - 1, 2), greet_column, 0)

    fetches = [
        pltpu.make_async_copy(source, target, here_sem.at[number])
        for number, (source, target) in enumerate(
            (
                (state_in, state_here),
                (cot_in, cot_here),
                (diff_in, diff_here),
                (w_in, w_in_here),
                (w_second, w_second_here),
                (w_third, w_third_here),
                (w_out, w_out_here),
                (biases, biases_here),
            )
        )
    ]
    for fetch in fetches:
        fetch.start()

    def copy(source, target, send, recv, device):
        return pltpu.make_async_remote_copy(
            src_ref=source,
            dst_ref=target,
            send_sem=send,
            recv_sem=recv,
            device_id=device,
            device_id_type=MESH,
        )

    def field_copies(e, z):
        send, recv = f_send, f_recv
        return (
            copy(p_last.at[e, z], x_lo.at[e, z], send.at[e, 0, z], recv.at[e, 0, z], (right, gy, gz)),
            copy(p_first.at[e, z], x_hi.at[e, z], send.at[e, 1, z], recv.at[e, 1, z], (left, gy, gz)),
            copy(p_first.at[e, z], xy_hi.at[e, z], send.at[e, 2, z], recv.at[e, 2, z], (left, below, gz)),
            copy(st.at[e, z + 1, pl.ds(56, 8)], y_lo.at[e, z], send.at[e, 3, z], recv.at[e, 3, z], (gx, above, gz)),
            copy(st.at[e, z + 1, pl.ds(0, 8)], y_hi.at[e, z], send.at[e, 4, z], recv.at[e, 4, z], (gx, below, gz)),
        )

    def field_copies_low(e):
        send, recv = f_send_z, f_recv_z
        return (
            copy(p_first.at[e, 0], x_hi.at[e, PLANES], send.at[e, 0], recv.at[e, 0], (left, gy, other)),
            copy(st.at[e, 1, pl.ds(0, 8)], y_hi.at[e, PLANES], send.at[e, 1], recv.at[e, 1], (gx, below, other)),
            copy(st.at[e, 1], st.at[e, PLANES + 1], send.at[e, 2], recv.at[e, 2], (gx, gy, other)),
        )

    def field_copies_high(e):
        return (
            copy(st.at[e, PLANES], st.at[e, 0], f_send_z.at[e, 3], f_recv_z.at[e, 3], (gx, gy, other)),
        )

    def adjoint_copies(e, z):
        send, recv = b_send, b_recv
        return (
            copy(pa_last.at[e, z], xa.at[e, z + 1], send.at[e, 0, z], recv.at[e, 0, z], (right, gy, gz)),
            copy(pa_first.at[e, z], xb.at[e, z], send.at[e, 1, z], recv.at[e, 1, z], (left, gy, gz)),
            copy(pa_last.at[e, z], xya.at[e, z], send.at[e, 2, z], recv.at[e, 2, z], (right, above, gz)),
            copy(y_tiles.at[e, z], ya.at[e, z + 1], send.at[e, 3, z], recv.at[e, 3, z], (gx, above, gz)),
            copy(q.at[e, z + 1, 4, pl.ds(0, 8)], yb.at[e, z], send.at[e, 4, z], recv.at[e, 4, z], (gx, below, gz)),
        )

    def adjoint_copies_high(e):
        send, recv = b_send_z, b_recv_z
        return (
            copy(pa_last.at[e, PLANES - 1], xa.at[e, 0], send.at[e, 0], recv.at[e, 0], (right, gy, other)),
            copy(y_tiles.at[e, PLANES - 1], ya.at[e, 0], send.at[e, 1], recv.at[e, 1], (gx, above, other)),
            copy(z_up.at[e], q.at[e, 0, 5], send.at[e, 2], recv.at[e, 2], (gx, gy, other)),
        )

    def adjoint_copies_low(e):
        return (
            copy(q.at[e, 1, 6], q.at[e, PLANES + 1, 6], b_send_z.at[e, 3], b_recv_z.at[e, 3], (gx, gy, other)),
        )

    def start(copies):
        for each in copies:
            each.start()

    def arrive(copies):
        for each in copies:
            each.wait_recv()

    def sent(copies):
        for each in copies:
            each.wait_send()

    def pack_fields(e, z):
        plane = st[e, z + 1]
        empty = jnp.zeros((8, LANES), f32)
        p_first[e, z] = pack_lane(plane, 0, 0, empty)
        p_last[e, z] = pack_lane(plane, LANES - 1, 0, empty)

    def send_fields(e, z):
        start(field_copies(e, z))

        @pl.when(z == 0)
        def _():
            start(field_copies_low(e))

        @pl.when(z == PLANES - 1)
        def _():
            start(field_copies_high(e))

    def place(step):
        odd = lax.rem(step, 2)
        half = lax.div(step, 2)
        return half + odd * (PLANES - 1 - 2 * half)

    def first_place(step):
        after = lax.max(step - 1, 0)
        odd = lax.rem(after, 2)
        half = lax.div(after, 2)
        return lax.min(step, 1) * (1 + half + odd * (PLANES - 2 - 2 * half))

    def lay_out(z, carry):
        for k in range(FIELDS):
            st[0, z + 1, pl.ds(k, 16, stride=FIELDS), :] = state_here[k, z]
        pack_fields(0, z)
        return carry

    fetches[0].wait()
    lax.fori_loop(0, PLANES, lay_out, 0)
    pl.semaphore_wait(barrier, 11 + max(nx - 3, 0) + max(ny - 3, 0))

    def first_sends(step, carry):
        send_fields(0, first_place(step))
        return carry

    lax.fori_loop(0, PLANES, first_sends, 0)

    for fetch in fetches[1:]:
        fetch.wait()

    def lay_out_rest(z, carry):
        for k in range(FIELDS):
            cot[z, pl.ds(k, 16, stride=FIELDS), :] = cot_here[k, z]
            spread4[z, pl.ds(k, 16, stride=FIELDS), :] = diff_here[z]
        return carry

    lax.fori_loop(0, PLANES, lay_out_rest, 0)
    for e in range(2):
        for j in (8, 9):
            q[e, 0, j] = jnp.zeros((ROWS, LANES), f32)

    zero4 = jnp.zeros((4, LANES), f32)
    first = w_in_here[...].astype(f32)
    parts = [first[4 * j : 4 * j + 4] for j in range(STENCIL)]
    even = jnp.concatenate([piece for part in parts for piece in (part, zero4)], axis=0)
    odd = jnp.concatenate([piece for part in parts for piece in (zero4, part)], axis=0)
    v_one[...] = jnp.concatenate([even, odd], axis=1).astype(bf16)
    bias_high = biases_here[...].astype(bf16).astype(f32)
    bias_low = biases_here[...] - bias_high

    def bias_rows(layer):
        return jnp.concatenate(
            [
                0.5 * bias_high[layer : layer + 1],
                0.5 * bias_low[layer : layer + 1],
                jnp.zeros((14, HID), f32),
            ],
            axis=0,
        )

    def turned_first(half):
        tall = jnp.concatenate([0.5 * half, bias_rows(0), jnp.zeros((32, HID), f32)], axis=0)
        return tall.T[:, :96]

    l_one[...] = jnp.concatenate([turned_first(even), turned_first(odd)], axis=0).astype(bf16)
    for layer, source, ahead, back in (
        (1, w_second_here, l_two, v_two),
        (2, w_third_here, l_three, v_three),
    ):
        matrix = 0.5 * source[...].astype(f32)
        back[...] = matrix.astype(bf16)
        tall = jnp.concatenate([bias_rows(layer), jnp.zeros((112, HID), f32)], axis=0)
        ahead[...] = jnp.concatenate([matrix.T, tall.T[:, :16]], axis=1).astype(bf16)
    turned_out = w_out_here[...].astype(f32)
    readout = jnp.concatenate([turned_out, jnp.zeros((HID - FIELDS, HID), f32)], axis=0).T
    zero8 = jnp.zeros((8, LANES), f32)
    l_out[...] = jnp.concatenate(
        [
            jnp.concatenate([turned_out, zero4, zero8], axis=0),
            jnp.concatenate([zero4, turned_out, zero8], axis=0),
        ],
        axis=1,
    ).astype(bf16)
    v_out[...] = jnp.concatenate(
        [0.5 * readout[:, :16], 0.5 * pltpu.roll(readout, FIELDS, 1)[:, :16]], axis=0
    ).astype(bf16)
    field_row = lax.rem(lax.broadcasted_iota(jnp.int32, (8, LANES), 0), FIELDS)
    bias_tile = jnp.zeros((8, LANES), f32)
    for k in range(FIELDS):
        bias_tile = jnp.where(field_row == k, bias_out[k], bias_tile)
    bias_plane = jnp.concatenate([bias_tile] * 8, axis=0)
    for each in (g_one, g_two, g_three, g_four, g_last):
        each[...] = jnp.zeros(each.shape, f32)

    lane = lane_index(ROWS)
    lane8 = lane_index(8)
    sub_width = WIDE // SUBS
    ones_rows = lax.broadcasted_iota(jnp.int32, (16, WIDE), 0)
    ones_wide = jnp.where(ones_rows < 2, 1.0, 0.0).astype(bf16)
    ones_cells = jnp.concatenate([ones_wide[:, :sub_width]] * 2, axis=1)

    def to_right(plane, e, z):
        return jnp.where(
            lane == LANES - 1, unpack_lane(x_hi[e, z], 0, LANES - 1), pltpu.roll(plane, LANES - 1, 1)
        )

    def stencil(e, z):
        here, ahead, behind = st[e, z + 1], st[e, z + 2], st[e, z]
        beyond = y_hi[e, z]
        at_right = to_right(here, e, z)
        at_left = jnp.where(lane == 0, unpack_lane(x_lo[e, z], 0, 0), pltpu.roll(here, 1, 1))
        corner = jnp.where(
            lane8 == LANES - 1,
            pltpu.roll(xy_hi[e, z], LANES - 1, 1),
            pltpu.roll(beyond, LANES - 1, 1),
        )
        return (
            here,
            at_right,
            at_left,
            rows_down(here, beyond[0:4]),
            rows_up(here, y_lo[e, z][4:8]),
            ahead,
            behind,
            rows_down(at_right, corner[0:4]),
            rows_down(ahead, y_hi[e, z + 1][0:4]),
            to_right(ahead, e, z + 1),
        )

    def arrange(points):
        rows = jnp.concatenate([wide_of(point) for point in points], axis=0)
        return jnp.concatenate([rows.astype(bf16), ones_wide], axis=0)

    def laplace(points):
        total_of = -6.0 * points[0]
        for point in points[1:7]:
            total_of = total_of + point
        return total_of

    def layers(features, values, doubled):
        value, slope = silu_parts(side_by_side(mm(l_one[...], features)))
        values.append(value)
        doubled.append(slope)
        yield
        for matrix in (l_two, l_three):
            cells = jnp.concatenate([value, ones_cells], axis=0)
            value, slope = silu_parts(mm(matrix[...], cells))
            values.append(value)
            doubled.append(slope)
            yield

    def readout_of(value):
        return mm(l_out[...], stacked_of(value))[0:8]

    def times(product, slope):
        return product.astype(bf16) * slope

    def grad_rows(adjoint):
        scaled = wide_of(time_step * adjoint)
        rounded = jnp.concatenate([scaled, jnp.zeros((8, WIDE), f32)], axis=0).astype(bf16)
        added = rounded.astype(f32)[0:8]
        for part in range(8):
            g_last[...] += added[:, LANES * part : LANES * (part + 1)]
        return rounded

    def backward(features, values, doubled, grad_out, to_features):
        back_three = times(side_by_side(mm(v_out[...], grad_out)), doubled[2])
        yield
        back_two = times(mm(v_three[...], back_three), doubled[1])
        yield
        g_four[...] += mm_cells(grad_out, stacked_of(values[2]))
        back_one = stacked_of(times(mm(v_two[...], back_two), doubled[0]))
        yield
        g_three[...] += mm_cells(jnp.concatenate([values[1], ones_cells], axis=0), back_three)
        result = mm(v_one[...], back_one) if to_features else back_one
        yield
        g_two[...] += mm_cells(jnp.concatenate([values[0], ones_cells], axis=0), back_two)
        yield
        g_one[...] += mm_cells(features, back_one)
        return result

    def in_turn(pieces):
        results = [None] * len(pieces)
        running = list(range(len(pieces)))
        while running:
            for number in list(running):
                try:
                    next(pieces[number])
                except StopIteration as end:
                    results[number] = end.value
                    running.remove(number)
        return results

    def send_adjoint(e, z, wide, adjoint):
        spread = spread4[z] * adjoint
        for j in range(STENCIL):
            part = plane_of(wide[8 * j : 8 * j + 8])
            if j == 0:
                part = part - 6.0 * spread
            elif j < 7:
                part = part + spread
            q[e, z + 1, j] = part
        empty = jnp.zeros((8, LANES), f32)
        across = pack_lane(q[e, z + 1, 1], LANES - 1, 0, empty)
        across = pack_lane(q[e, z + 1, 9], LANES - 1, 8, across)
        pa_last[e, z] = pack_lane(q[e, z + 1, 7], LANES - 1, 16, across)
        pa_first[e, z] = pack_lane(q[e, z + 1, 2], 0, 0, empty)
        slanted = q[e, z + 1, 7, 56:64]
        slanted = jnp.where(lane8 == 0, 0.0, pltpu.roll(slanted, 1, 1))
        y_tiles[e, z, 0:8] = q[e, z + 1, 3, 56:64] + slanted
        y_tiles[e, z, 8:16] = q[e, z + 1, 8, 56:64]
        start(adjoint_copies(e, z))

        @pl.when(z == 0)
        def _():
            start(adjoint_copies_low(e))

        @pl.when(z == PLANES - 1)
        def _():
            moved = jnp.where(lane == 0, 0.0, pltpu.roll(q[e, PLANES, 9], 1, 1))
            z_up[e] = q[e, PLANES, 5] + moved + rows_up(q[e, PLANES, 8], zero4)
            start(adjoint_copies_high(e))

    def gather(e, z, adjoint):
        here = z + 1
        result = adjoint + q[e, here, 0] + q[e, z, 5] + q[e, z + 2, 6]
        from_left = q[e, here, 1] + q[e, z, 9] + rows_up(q[e, here, 7], zero4)
        packed = xa[e, here]
        direct = unpack_lane(packed + pltpu.roll(xa[e, z], LANES - 8, 1), 0, 0)
        corner = pltpu.roll(xya[e, z], LANES - 23, 1)[4:8]
        edge = direct + rows_up(unpack_lane(packed, 16, 0), corner)
        result = result + jnp.where(lane == 0, edge, pltpu.roll(from_left, 1, 1))
        result = result + jnp.where(
            lane == LANES - 1,
            unpack_lane(xb[e, z], 0, LANES - 1),
            pltpu.roll(q[e, here, 2], LANES - 1, 1),
        )
        rows_in = ya[e, here, 0:8] + ya[e, z, 8:16]
        result = result + rows_up(q[e, here, 3] + q[e, z, 8], rows_in[4:8])
        return result + rows_down(q[e, here, 4], yb[e, z][0:4])

    def await_first(step):
        @pl.when(step == 0)
        def _():
            arrive(field_copies(0, 0))
            arrive(field_copies(0, 1))
            arrive(field_copies_high(0))

        @pl.when(step == 1)
        def _():
            arrive(field_copies(0, 2))

        @pl.when(step == 2)
        def _():
            arrive(field_copies(0, 5))
            arrive(field_copies_low(0))

        @pl.when(step == 3)
        def _():
            arrive(field_copies(0, 3))

        @pl.when(step == 4)
        def _():
            arrive(field_copies(0, 4))

    def await_fields(e, step):
        @pl.when(step == 0)
        def _():
            arrive(field_copies(e, 0))
            arrive(field_copies(e, 1))
            arrive(field_copies_high(e))

        @pl.when(step == 1)
        def _():
            arrive(field_copies(e, 5))
            arrive(field_copies_low(e))

        @pl.when(step == 2)
        def _():
            arrive(field_copies(e, 2))

        @pl.when(step == 3)
        def _():
            arrive(field_copies(e, 4))

        @pl.when(step == 4)
        def _():
            arrive(field_copies(e, 3))

    def await_adjoint(e, step):
        @pl.when(step == 0)
        def _():
            arrive(adjoint_copies(e, 0))
            arrive(adjoint_copies_high(e))

        @pl.when(step == 1)
        def _():
            arrive(adjoint_copies(e, 1))

        @pl.when(step == 2)
        def _():
            arrive(adjoint_copies(e, 5))
            arrive(adjoint_copies(e, 4))
            arrive(adjoint_copies_low(e))

        @pl.when(step == 3)
        def _():
            arrive(adjoint_copies(e, 2))

        @pl.when(step == 4)
        def _():
            arrive(adjoint_copies(e, 3))

    def piece(sub):
        return slice(sub * sub_width, (sub + 1) * sub_width)

    def beside(sub):
        return slice(2 * sub * sub_width, 2 * (sub + 1) * sub_width)

    def stepped(points, z, wide):
        closed = plane_of(wide) + bias_plane
        return points[0] + spread4[z] * laplace(points) + time_step * closed

    def put(target, z, plane):
        staged[...] = plane
        for k in range(FIELDS):
            target[k, z] = staged[pl.ds(k, 16, stride=FIELDS), :]

    def first_step(step, carry):
        z = first_place(step)
        await_first(step)
        points = stencil(0, z)
        features = arrange(points)
        feats[z] = features

        def forward(sub):
            values, doubled = [], []
            for layer, _ in enumerate(layers(features[:, piece(sub)], values, doubled)):
                acts[layer, z, :, beside(sub)] = values[layer]
                slopes[layer, z, :, beside(sub)] = doubled[layer]
                yield
            return readout_of(values[2])

        outs = in_turn([forward(sub) for sub in range(SUBS)])
        st[1, z + 1] = stepped(points, z, jnp.concatenate(outs, axis=1))
        pack_fields(1, z)
        send_fields(1, z)
        return carry

    lax.fori_loop(0, PLANES, first_step, 0)

    def second_step(step, carry):
        z = place(step)
        await_fields(1, step)
        points = stencil(1, z)
        features = arrange(points)
        adjoint = cot[z]
        grad_out = grad_rows(adjoint)

        def forward(sub):
            values, doubled = [], []
            yield from layers(features[:, piece(sub)], values, doubled)
            return values, doubled, readout_of(values[2])

        passed = in_turn([forward(sub) for sub in range(SUBS)])
        put(final_out, z, stepped(points, z, jnp.concatenate([one[2] for one in passed], axis=1)))
        wides = in_turn(
            [
                backward(features[:, piece(sub)], *passed[sub][0:2], grad_out[:, piece(sub)], True)
                for sub in range(SUBS)
            ]
        )
        send_adjoint(0, z, jnp.concatenate(wides, axis=1), adjoint)
        return carry

    lax.fori_loop(0, PLANES, second_step, 0)

    def first_back(step, carry):
        z = first_place(step)
        await_adjoint(0, step)
        adjoint = gather(0, z, cot[z])
        adj_mid[z] = adjoint
        grad_out = grad_rows(adjoint)

        def back(sub):
            values = [acts[layer, z, :, beside(sub)] for layer in range(3)]
            doubled = [slopes[layer, z, :, beside(sub)] for layer in range(3)]
            return backward(
                feats[z, :, piece(sub)], values, doubled, grad_out[:, piece(sub)], False
            )

        for sub, back_one in enumerate(in_turn([back(sub) for sub in range(SUBS)])):
            backs[z, :, piece(sub)] = back_one
        return carry

    lax.fori_loop(0, PLANES, first_back, 0)

    one = g_one[...]
    merged = one[:, :HID] + jnp.concatenate([one[4:, HID:], one[:4, HID:]], axis=0)
    first_rows = jnp.concatenate([merged[8 * j : 8 * j + 4] for j in range(STENCIL)], axis=0)
    readout_rows = g_four[0:4, :HID] + g_four[4:8, HID:]
    last = jnp.sum(g_last[...], axis=1, keepdims=True)
    last = last[0:4] + last[4:8]
    row = lax.broadcasted_iota(jnp.int32, (FIELDS, LANES), 0)
    column = lax.broadcasted_iota(jnp.int32, (FIELDS, LANES), 1)
    last = jnp.sum(jnp.where(row == column, last, 0.0), axis=0, keepdims=True)
    rest = jnp.concatenate(
        [
            one[80:81, :HID] + one[80:81, HID:],
            g_two[HID : HID + 1],
            g_three[HID : HID + 1],
            last,
            readout_rows,
        ],
        axis=0,
    )
    everything = jnp.concatenate(
        [g_two[0:HID], first_rows, rest, jnp.zeros((FIRST_SUMS - 176, LANES), f32)], axis=0
    )
    sums[0] = everything.reshape(nx, share, LANES)
    sums[1, :, 0 : shares[1]] = g_three[0:HID].reshape(nx, shares[1], LANES)

    pair = copy(sums.at[other], landed_pair, a_send.at[0, 0], a_recv.at[0, 0], (gx, gy, other))

    def by_core(act):
        for core in range(2):
            pl.when(gz == core)(functools.partial(act, shares[core]))

    def scatter(rows, step):
        target = lax.rem(gx + step, nx)
        part = pl.ds(0, rows)
        return copy(
            sums.at[gz, target, part], landed_a.at[step, part], a_send.at[1, step], a_recv.at[1, step], (target, gy, gz)
        )

    def across(rows, step):
        target = lax.rem(gy + step, ny)
        part = pl.ds(0, rows)
        return copy(landed_b.at[gy, part], landed_b.at[gy, part], a_send.at[2, step], a_recv.at[2, gy], (gx, target, gz))

    def across_in(rows, step):
        source = lax.rem(gy + ny - step, ny)
        part = pl.ds(0, rows)
        return copy(landed_b.at[source, part], landed_b.at[source, part], a_send.at[2, step], a_recv.at[2, source], (gx, source, gz))

    def spread_out(rows, step):
        target = lax.rem(gx + step, nx)
        part = pl.ds(0, rows)
        return copy(total.at[gz, gx, part], total.at[gz, gx, part], a_send.at[3, step], a_recv.at[3, gx], (target, gy, gz))

    def spread_in(rows, step):
        source = lax.rem(gx + nx - step, nx)
        part = pl.ds(0, rows)
        return copy(total.at[gz, source, part], total.at[gz, source, part], a_send.at[3, step], a_recv.at[3, source], (source, gy, gz))

    def hand_over(step):
        source = lax.rem(gx + nx - step, nx)
        return copy(total.at[gz, source], total.at[gz, source], a_send.at[4, step], a_recv.at[4, source], (gx, gy, other))

    def hand_over_in(step):
        source = lax.rem(gx + nx - step, nx)
        return copy(total.at[other, source], total.at[other, source], a_send.at[4, step], a_recv.at[4, source], (gx, gy, other))

    def each(first, count, act):
        def body(step, carry):
            act(step)
            return carry

        lax.fori_loop(first, count, body, 0)

    def near(turn):
        half = lax.div(turn + 1, 2)
        return half + (1 - lax.rem(turn, 2)) * (nx - 2 * half)

    def last_contributions(step, carry):
        z = place(step)
        send_adjoint(1, z, mm(v_one[...], backs[z]), adj_mid[z])
        return carry

    def last_gather(step, carry):
        z = first_place(step)
        await_adjoint(1, step)
        put(adjoint_out, z, gather(1, z, adj_mid[z]))
        return carry

    pair.start()
    lax.fori_loop(0, 2, last_contributions, 0)
    pair.wait_recv()
    sums[gz] = sums[gz] + landed_pair[...]
    by_core(lambda rows: each(1, nx, lambda turn: scatter(rows, near(nx - turn)).start()))
    lax.fori_loop(2, PLANES, last_contributions, 0)
    by_core(lambda rows: each(1, nx, lambda step: scatter(rows, step).wait_recv()))
    held = sums[gz, gx]
    for step in range(1, nx):
        held = held + landed_a[step]
    landed_b[gy] = held
    by_core(lambda rows: each(1, ny, lambda step: across(rows, step).start()))

    lax.fori_loop(0, PLANES, last_gather, 0)

    by_core(lambda rows: each(1, ny, lambda step: across_in(rows, step).wait_recv()))
    held = landed_b[0]
    for step in range(1, ny):
        held = held + landed_b[step]
    total[gz, gx] = held * scale
    by_core(lambda rows: each(1, nx, lambda turn: spread_out(rows, near(nx - turn)).start()))
    hand_over(0).start()

    def finish_sends(z, carry):
        for e in range(2):
            sent(field_copies(e, z))
            sent(adjoint_copies(e, z))
        return carry

    lax.fori_loop(0, PLANES, finish_sends, 0)
    for e in range(2):
        sent(field_copies_low(e))
        sent(field_copies_high(e))
        sent(adjoint_copies_low(e))
        sent(adjoint_copies_high(e))
    pair.wait_send()
    by_core(lambda rows: each(1, nx, lambda step: scatter(rows, step).wait_send()))
    by_core(lambda rows: each(1, ny, lambda step: across(rows, step).wait_send()))

    def pass_on(rows, turn):
        step = near(turn)
        spread_in(rows, step).wait_recv()
        hand_over(step).start()

    by_core(lambda rows: each(1, nx, functools.partial(pass_on, rows)))
    each(0, nx, lambda step: hand_over_in(step).wait_recv())

    sums_out[0:FIRST_SUMS] = total[0].reshape(FIRST_SUMS, LANES)
    sums_out[FIRST_SUMS:SUMS] = total[1, :, 0 : shares[1]].reshape(HID, LANES)
    by_core(lambda rows: each(1, nx, lambda step: spread_out(rows, step).wait_send()))
    each(0, nx, lambda step: hand_over(step).wait_send())


def deliver(
    final_in,
    adjoint_in,
    sums_in,
    final_out,
    adjoint_out,
    g_in_out,
    g_second_out,
    g_third_out,
    g_readout_out,
    g_biases_out,
    g_bias_out_out,
    store_sem,
):
    stores = [
        pltpu.make_async_copy(source, target, store_sem.at[number])
        for number, (source, target) in enumerate(
            (
                (final_in, final_out),
                (adjoint_in, adjoint_out),
                (sums_in.at[pl.ds(0, HID)], g_second_out),
                (sums_in.at[pl.ds(FIRST_SUMS, HID)], g_third_out),
                (sums_in.at[pl.ds(HID, 40)], g_in_out),
            )
        )
    ]
    for store in stores:
        store.start()
    tail = sums_in[168:176]
    g_biases_out[...] = tail[0:3]
    g_readout_out[...] = tail[4:8]
    g_bias_out_out[...] = tail[3:4, 0:FIELDS]
    for store in stores:
        store.wait()


def solution(mesh):
    sizes = (mesh.shape["gx"], mesh.shape["gy"], mesh.shape["gz"])
    nx, ny, nz = sizes
    share = FIRST_SUMS // nx
    cells = PLANES * 16 * LANES * nx * ny * nz
    scale = 1.0 / (time_step * math.sqrt(float(cells)))
    vmem = pl.BlockSpec(memory_space=pltpu.VMEM)
    block = jax.ShapeDtypeStruct((FIELDS, PLANES, 16, LANES), f32)
    tile = (8, LANES)
    dma = pltpu.SemaphoreType.DMA

    def buffer(*shape):
        return pltpu.VMEM(shape, f32)

    def packed(*shape):
        return pltpu.VMEM(shape, bf16)

    scratch = [
        buffer(FIELDS, PLANES, 16, LANES),
        buffer(FIELDS, PLANES, 16, LANES),
        buffer(PLANES, 16, LANES),
        packed(40, HID),
        packed(HID, HID),
        packed(HID, HID),
        packed(FIELDS, HID),
        buffer(3, HID),
        buffer(2, PLANES + 2, ROWS, LANES),
        buffer(2, PLANES, *tile),
        buffer(2, PLANES, *tile),
        buffer(2, PLANES, *tile),
        buffer(2, PLANES + 1, *tile),
        buffer(2, PLANES, *tile),
        buffer(2, PLANES, *tile),
        buffer(2, PLANES + 1, *tile),
        buffer(PLANES, ROWS, LANES),
        buffer(PLANES, ROWS, LANES),
        buffer(PLANES, ROWS, LANES),
        buffer(ROWS, LANES),
        packed(PLANES, 96, WIDE),
        packed(3, PLANES, HID, 2 * WIDE),
        packed(3, PLANES, HID, 2 * WIDE),
        packed(PLANES, 2 * HID, WIDE),
        buffer(2, PLANES + 2, STENCIL, ROWS, LANES),
        buffer(2, PLANES, *tile),
        buffer(2, PLANES, *tile),
        buffer(2, PLANES, 16, LANES),
        buffer(2, ROWS, LANES),
        buffer(2, PLANES + 1, *tile),
        buffer(2, PLANES, *tile),
        buffer(2, PLANES, *tile),
        buffer(2, PLANES + 1, 16, LANES),
        buffer(2, PLANES, *tile),
        packed(2 * HID, 96),
        packed(HID, 144),
        packed(HID, 144),
        packed(16, 2 * HID),
        packed(2 * HID, 16),
        packed(HID, HID),
        packed(HID, HID),
        packed(80, 2 * HID),
        buffer(96, 2 * HID),
        buffer(144, HID),
        buffer(144, HID),
        buffer(16, 2 * HID),
        buffer(8, LANES),
        buffer(nz, nx, share, LANES),
        buffer(nx, share, LANES),
        buffer(nx, share, LANES),
        buffer(ny, share, LANES),
        buffer(nz, nx, share, LANES),
        dma((2, 5, PLANES)),
        dma((2, 5, PLANES)),
        dma((2, 4)),
        dma((2, 4)),
        dma((2, 5, PLANES)),
        dma((2, 5, PLANES)),
        dma((2, 4)),
        dma((2, 4)),
        dma((5, max(nx, ny))),
        dma((5, max(nx, ny))),
        dma((11,)),
    ]

    shapes = (
        block,
        block,
        jax.ShapeDtypeStruct((40, HID), f32),
        jax.ShapeDtypeStruct((HID, HID), f32),
        jax.ShapeDtypeStruct((HID, HID), f32),
        jax.ShapeDtypeStruct((FIELDS, HID), f32),
        jax.ShapeDtypeStruct((3, HID), f32),
        jax.ShapeDtypeStruct((1, FIELDS), f32),
    )
    anywhere = pl.BlockSpec(memory_space=pl.ANY)

    def on_device(state, cotangent, diffusion, w_in, w_second, w_third, w_out, biases, bias_out):
        outs = pl.pallas_call(
            functools.partial(kernel, sizes, scale),
            out_shape=(
                buffer(FIELDS, PLANES, 16, LANES),
                buffer(FIELDS, PLANES, 16, LANES),
                buffer(SUMS, LANES),
            ),
            in_specs=[pl.BlockSpec(memory_space=pl.ANY)] * 8 + [pl.BlockSpec(memory_space=pltpu.SMEM)],
            out_specs=[vmem] * 3,
            scratch_shapes=scratch,
            compiler_params=pltpu.CompilerParams(
                collective_id=0, has_side_effects=True, vmem_limit_bytes=58 * 2**20
            ),
            name="two_steps_and_adjoint",
        )(state, cotangent, diffusion, w_in, w_second, w_third, w_out.T, biases, bias_out)
        outs = pl.pallas_call(
            deliver,
            out_shape=shapes,
            in_specs=[vmem] * 3,
            out_specs=[anywhere] * 5 + [vmem] * 3,
            scratch_shapes=[dma((5,))],
            compiler_params=pltpu.CompilerParams(vmem_limit_bytes=16 * 2**20),
            name="deliver",
        )(*outs)
        return outs[:5] + (outs[5].T, outs[6], outs[7].reshape(FIELDS))

    fields = P(None, "gz", "gy", "gx")
    placed = (fields, fields, P("gz", "gy", "gx")) + (P(),) * 6
    return jax.shard_map(
        on_device,
        mesh=mesh,
        in_specs=placed,
        out_specs=(fields, fields) + (P(),) * 6,
        check_vma=False,
    )
```
